512 devices in a mesh: table: 64 (over y, z), replica: 8 (over x, core).
Axes of the slice: x: 4, y: 4, z: 16, core: 2. Of those that a mesh axis runs over, the one named last changes fastest.
Arguments:
- bottom: bfloat16 [131072, 128], P(('table', 'replica')), may hold values from -6 to 6
- hot_ids: int32 [131072, 20], P(('table', 'replica')), may hold values from 0 to 127
- hot_tables: bfloat16 [20, 128, 128], replicated, may hold values from -4 to 4
- cold_owner: int32 [131072, 12], P(('table', 'replica')), may hold values from 0 to 63, all different within a row; in each aligned block of 256 rows (0 to 255, 256 to 511, ...) at most 128 rows name the same one
- cold_row: int32 [131072, 12], P(('table', 'replica')), may hold values from 0 to 255
- cold_rows: float32 [98304, 128], P('table'), may hold values from -3 to 3
- cold_acc: float32 [98304], P('table'), may hold values from 0.001 to 0.1
- u_weight: bfloat16 [3456, 256], P('replica'), may hold values from -0.109375 to 0.109375
- v_weight: float32 [256, 3456], P('replica'), may hold values from -0.375 to 0.375
- v_acc: float32 [256], P('replica'), may hold values from 1 to 100
- cross_bias: float32 [3456], replicated, may hold values from -2 to 2
- head: float32 [3456], replicated, may hold values from -0.109375 to 0.109375
- labels: int32 [131072], P(('table', 'replica')), may hold values 0 or 1
Outputs:
- new_cold_rows: float32 [98304, 128], P('table')
- new_cold_acc: float32 [98304], P('table')
- new_v: float32 [256, 3456], P('replica')
The draws below stay inside these ranges and needn't reach their ends.
Inputs may be any that keep to these rules, and one draw needn't show every extreme that they name: `cold_owner`: the 12 lookups of one sample name distinct owners; among the samples of one device (aligned blocks of 256 samples) no owner is named more than 128 times, and in every draw some owner is named exactly 128 times in some block.
All inputs are finite; a program needn't handle non-finite values. No bound on the sum of `labels` on one device may be relied on, other than what follows from the above.
Results may differ from the reference program's by a relative error of at most 0.0015.
Values may be sent and summed in bfloat16 or wider, within the bound.
A program may use at most 64 MiB of HBM per device.

```python
import math
import jax
import jax.numpy as jnp
import numpy as np
from jax import lax

E = 128
NCOLD = 6
LOOK = 2
HOT_ROWS = 128
RANK = 256
B_DEV = 256
SHARD_ROWS = 256
NHOT = 20
CROSS = 3456
CAP = 128
BATCH = 131072
COLD_TOTAL = 98304
N_TABLE = 64


def touch_ends(drawn, key, smallest, high):
    index_at = [jax.random.randint(jax.random.fold_in(key, axis), (), 0, length) for axis, length in enumerate(drawn.shape)]
    widest = drawn.shape.index(max(drawn.shape))
    next_to = index_at[:widest] + [(index_at[widest] + 1) % drawn.shape[widest]] + index_at[widest + 1:]
    return drawn.at[tuple(index_at)].set(smallest).at[tuple(next_to)].set(high)


def levels(stream_key, shape, split, low, high):
    level = 1.0
    for dim, shards_of in split:
        steps = jax.random.uniform(jax.random.fold_in(jax.random.fold_in(stream_key, 6), dim), (shards_of,), jnp.float32, low / len(split), high / len(split))
        level = level * jnp.repeat(jnp.exp(steps), shape[dim] // shards_of).reshape((-1,) + (1,) * (len(shape) - 1 - dim))
    return level


def shared_out(rng, own, number, rows, count, top, reach, skew):
    order = jax.random.permutation(rng, count)
    crowded, ordinary = portions_of(count, rows * top, reach, skew, True), portions_of(count, rows * top, reach, skew, False)
    places = jnp.arange(count)

    def named(sizes, turn):
        used = int((sizes > 0).sum())
        fixed = max(1, used // 4)
        passed = fixed + (places - fixed + turn * (used - fixed)) % max(1, count - fixed)
        return jnp.zeros((count,), jnp.int32).at[order[jnp.where(places < fixed, places, passed)]].set(jnp.asarray(sizes, jnp.int32))

    sizes = jnp.where(number % 4 == 0, named(crowded, number // 4), named(ordinary, number - number // 4 - 1))
    mixed = jax.random.permutation(jax.random.fold_in(own, 3), count)
    source_of, taker = mixed[0:count // 2 * 2:2], mixed[1:count // 2 * 2:2]
    room = jnp.minimum(sizes[source_of] - 1, reach - sizes[taker]) // 2
    room = jnp.where((source_of == order[0]) | (taker == order[0]) | (sizes[taker] == 0), 0, jnp.maximum(room, 0))
    passed = jax.random.randint(jax.random.fold_in(own, 4), (count // 2,), 0, 1 << 20) % (room + 1)
    sizes = sizes.at[source_of].add(-passed).at[taker].add(passed)
    members = jnp.searchsorted(jnp.cumsum(sizes), jnp.arange(rows * top), side="right").astype(jnp.int32)
    grid = members.reshape(top, rows).T
    grid = grid[jax.random.permutation(jax.random.fold_in(own, 1), rows)]
    turn = jax.random.randint(jax.random.fold_in(own, 2), (rows, 1), 0, top)
    return jnp.take_along_axis(grid, (jnp.arange(top)[None, :] + turn) % top, axis=1)


def portions_of(count, total, bound, lean, full):
    portions = [(1 << 20) // math.isqrt(rank ** lean) + 1 for rank in range(1, count + 1)]
    largest = bound if full else min(bound, max(-(-total // count), total * portions[0] // sum(portions)))
    least = 1 if total - largest >= count - 1 else 0
    counts, spare = [largest] + [least] * (count - 1), total - largest - least * (count - 1)
    while spare > 0:
        movable = [i for i in range(1, count) if counts[i] < largest] or [i for i in range(1, count) if counts[i] < bound]
        mass, budget = sum([portions[i] for i in movable]), spare
        for i in movable:
            addition = min(bound - counts[i], max(1, budget * portions[i] // mass), spare)
            counts[i] = counts[i] + addition
            spare = spare - addition
    return np.array(counts)


def noise(stream_key, extent, width, bound, cuts=(), kind=jnp.bfloat16):
    entries = width * jax.random.normal(stream_key, extent, jnp.float32)
    if cuts:
        entries = entries * levels(stream_key, extent, cuts, -0.22, 0.18)
    return jnp.clip(entries, -bound, bound).astype(kind)


def setup_inputs(seed: int = 0) -> dict:
    splits = jax.random.split(jax.random.key(seed), 14)
    bottom = noise(splits[0], (BATCH, E), 1.0, 6.0, ((0, 512),))
    hot_ids = touch_ends(jax.random.randint(splits[1], (BATCH, NHOT), 0, HOT_ROWS), jax.random.fold_in(splits[1], 1), 0, HOT_ROWS - 1).astype(jnp.int32)
    hot_tables = noise(splits[2], (NHOT, HOT_ROWS, E), 0.7, 4.0)
    cold_owner_keys = jax.random.split(jax.random.fold_in(splits[3], 1), BATCH // B_DEV)
    cold_owner_turns = jax.random.permutation(jax.random.fold_in(splits[3], 3), BATCH // B_DEV)
    cold_owner = jax.vmap(lambda own, number: shared_out(jax.random.fold_in(splits[3], 2), own, number, B_DEV, N_TABLE, NCOLD * LOOK, CAP, 2))(cold_owner_keys, cold_owner_turns).reshape((BATCH, NCOLD * LOOK))
    cold_row = touch_ends(jax.random.randint(splits[4], (BATCH, NCOLD * LOOK), 0, SHARD_ROWS), jax.random.fold_in(splits[4], 1), 0, SHARD_ROWS - 1).astype(jnp.int32)
    cold_rows = noise(splits[5], (COLD_TOTAL, E), 0.5, 3.0, ((0, 64),), jnp.float32)
    cold_acc = jnp.clip(jnp.exp(math.log(0.1) - 4.6051702 * jax.random.uniform(splits[6], (COLD_TOTAL,), jnp.float32) ** levels(splits[6], (COLD_TOTAL,), ((0, 64),), -0.2, 0.2)), 0.001, 0.1)
    u_weight = noise(splits[7], (CROSS, RANK), CROSS ** -0.5, 0.109375, ((0, 8),))
    v_weight = noise(splits[8], (RANK, CROSS), RANK ** -0.5, 0.375, ((0, 8),), jnp.float32)
    v_acc = jnp.clip(jnp.exp(math.log(100.0) - 4.6051702 * jax.random.uniform(splits[9], (RANK,), jnp.float32) ** levels(splits[9], (RANK,), ((0, 8),), -0.2, 0.2)), 1.0, 100.0)
    cross_bias = noise(splits[10], (CROSS,), 0.3, 2.0, (), jnp.float32)
    head = noise(splits[11], (CROSS,), CROSS ** -0.5, 0.109375, (), jnp.float32)
    labels = touch_ends((jax.random.randint(splits[12], (BATCH,), 0, 4) < 1).astype(jnp.int32), jax.random.fold_in(splits[12], 1), 0, 1)
    return dict(bottom=bottom, hot_ids=hot_ids, hot_tables=hot_tables, cold_owner=cold_owner, cold_row=cold_row, cold_rows=cold_rows, cold_acc=cold_acc, u_weight=u_weight, v_weight=v_weight, v_acc=v_acc, cross_bias=cross_bias, head=head, labels=labels)


row_rate = 0.1
dense_rate = 0.05
eps_value = 1e-08

def reference(bottom, hot_ids, hot_tables, cold_owner, cold_row, cold_rows, cold_acc, u_weight, v_weight, v_acc, cross_bias, head, labels):
    per_owner = NCOLD * SHARD_ROWS
    table_of = (jnp.arange(NCOLD * LOOK, dtype=jnp.int32) // LOOK).astype(jnp.int32)
    served = lax.optimization_barrier(cold_rows.astype(jnp.bfloat16))
    v_half = v_weight.astype(jnp.bfloat16)
    u_cold = u_weight[E:E + NCOLD * E]
    block = math.gcd(BATCH, 2048)
    hot_index = jnp.arange(NHOT, dtype=jnp.int32)
    contract = (((1,), (1,)), ((), ()))

    def advance(carry, index):
        grad_v, grad_rows = carry
        start = (index * block).astype(jnp.int32)

        def cut(array):
            return lax.dynamic_slice_in_dim(array, start, block, 0)
        global_row = (cut(cold_owner) * per_owner + table_of[None, :] * SHARD_ROWS + cut(cold_row)).astype(jnp.int32)
        looked = served[global_row].astype(jnp.float32)
        pooled = lax.optimization_barrier(jnp.sum(looked.reshape(block, NCOLD, LOOK, E), axis=2)).astype(jnp.bfloat16)
        hot = hot_tables[hot_index[None, :], cut(hot_ids)]
        first = jnp.concatenate([cut(bottom), pooled.reshape(block, NCOLD * E), hot.reshape(block, NHOT * E)], axis=1)
        low = jnp.dot(first, u_weight, preferred_element_type=jnp.float32).astype(jnp.bfloat16)
        mixing = jnp.dot(low, v_half, preferred_element_type=jnp.float32) + cross_bias[None, :]
        wide = first.astype(jnp.float32)
        crossed = wide * mixing + wide
        logit = jnp.dot(crossed, head, precision=lax.Precision.HIGHEST)
        dlogit = jax.nn.sigmoid(logit) - cut(labels).astype(jnp.float32)
        dcross = dlogit[:, None] * head[None, :]
        dmix = (dcross * wide).astype(jnp.bfloat16)
        grad_v = grad_v + lax.dot_general(low, dmix, (((0,), (0,)), ((), ())), preferred_element_type=jnp.float32)
        dlow = lax.dot_general(dmix, v_half, contract, preferred_element_type=jnp.float32).astype(jnp.bfloat16)
        dpool = dcross[:, E:E + NCOLD * E] * (mixing[:, E:E + NCOLD * E] + 1.0)
        dpool = dpool + lax.dot_general(dlow, u_cold, contract, preferred_element_type=jnp.float32)
        dpool = lax.optimization_barrier(dpool.astype(jnp.bfloat16)).reshape(block, NCOLD, 1, E)
        each = jnp.broadcast_to(dpool, (block, NCOLD, LOOK, E)).reshape(block * NCOLD * LOOK, E).astype(jnp.float32)
        grad_rows = grad_rows.at[global_row.reshape(-1)].add(each)
        return ((grad_v, grad_rows), None)
    start_carry = (jnp.zeros((RANK, CROSS), jnp.float32), jnp.zeros((COLD_TOTAL, E), jnp.float32))
    (grad_v, grad_rows), _ = lax.scan(advance, start_carry, jnp.arange(BATCH // block, dtype=jnp.int32))
    new_cold_acc = cold_acc + lax.optimization_barrier(jnp.mean(grad_rows * grad_rows, axis=1))
    new_cold_rows = cold_rows - row_rate * grad_rows / (jnp.sqrt(new_cold_acc)[:, None] + eps_value)
    acc_dense = v_acc + lax.optimization_barrier(jnp.mean(grad_v * grad_v, axis=1))
    new_v = v_weight - dense_rate * grad_v / (jnp.sqrt(acc_dense)[:, None] + eps_value)
    return (new_cold_rows, new_cold_acc, new_v)
```

```python
import functools
import jax
import jax.numpy as jnp
from jax import lax
from jax.experimental import pallas as pl
from jax.experimental.pallas import tpu as pltpu
from jax.sharding import PartitionSpec as P

NCOLD = 6
LOOK = 2
NHOT = 20
LOOKUPS = NCOLD * LOOK
E = 128
B = 256
ROWS = 256
SLOTS = 128
GROUP = 64
WIDE = NCOLD * E
PART = WIDE // 8
CROSS = 3456
PADDED = 3584
VCHUNKS = 14
VCOLS = 256
MESH = pl.DeviceIdType.MESH

row_rate = 0.1
dense_rate = 0.05
eps_value = 1e-08

f32 = jnp.float32
bf16 = jnp.bfloat16
i32 = jnp.int32
NT = (((1,), (1,)), ((), ()))


def place_of():
    table, rep = lax.axis_index("table"), lax.axis_index("replica")
    return table // 16, table % 16, rep


def dev(y, z, rep):
    return {"table": y * 16 + z, "replica": rep}


def member_of(y, z, rep):
    return y * 16 + rep * 2 + z % 2


def member_dev(member, z):
    return dev(member // 16, z - z % 2 + member % 2, (member // 2) % 8)


def peer(i, y, z, rep):
    py = (y + i // 16) % 4
    px = (rep // 2 + (i // 4) % 4) % 4
    pc = (rep + (i // 2) % 2) % 2
    pz = (z + i) % 2
    return py * 16 + px * 4 + pc * 2 + pz


def peer_back(i, y, z, rep):
    py = (y + 4 - i // 16) % 4
    px = (rep // 2 + 4 - (i // 4) % 4) % 4
    pc = (rep + (i // 2) % 2) % 2
    pz = (z + i) % 2
    return py * 16 + px * 4 + pc * 2 + pz


def greet(y, z, rep):
    bar = pltpu.get_barrier_semaphore()

    def group(i, carry):
        pl.semaphore_signal(
            bar, inc=1, device_id=member_dev(peer(i, y, z, rep), z), device_id_type=MESH
        )
        return carry

    lax.fori_loop(1, GROUP, group, 0)
    return bar


def tables(owner_ref, row_ref, pos, tab, rows):
    owners = lax.broadcasted_iota(i32, (GROUP, B), 0)
    named = jnp.zeros((GROUP, B), f32)
    table = jnp.zeros((GROUP, B), f32)
    row = jnp.zeros((GROUP, B), f32)
    for k in range(LOOKUPS):
        hit = owners == owner_ref[k : k + 1, :]
        named = jnp.where(hit, 1.0, named)
        table = jnp.where(hit, float(k // LOOK), table)
        if rows is not None:
            row = jnp.where(hit, row_ref[k : k + 1, :].astype(f32), row)
    before = jnp.where(
        lax.broadcasted_iota(i32, (B, B), 0) < lax.broadcasted_iota(i32, (B, B), 1), 1.0, 0.0
    ).astype(bf16)
    place = jnp.dot(named.astype(bf16), before, preferred_element_type=f32)
    pos[...] = jnp.where(named > 0.0, place, -1.0)
    tab[...] = table
    if rows is not None:
        rows[...] = row


def slots_of(pos, o):
    lines = lax.broadcasted_iota(i32, (SLOTS, B), 0).astype(f32)
    return jnp.where(lines == pos[pl.ds(o, 1), :], 1.0, 0.0).astype(bf16)


def rows_of(code):
    lines = lax.broadcasted_iota(i32, (ROWS, code.shape[1]), 0)
    return jnp.where(lines == code % ROWS, 1.0, 0.0).astype(bf16)


def forward_kernel(
    owner_ref, row_ref, part_ref, pooled_ref, asked_ref,
    held, replies, back, ask, pos, tab, rows, picks, pooled,
    held_send, held_recv, ask_send, ask_recv, rep_send, rep_recv, own_sem,
):
    y, z, rep = place_of()
    me = member_of(y, z, rep)
    bar = greet(y, z, rep)
    home = z // 2

    def holder(j):
        return (z + 2 * j) % 16

    def source(j):
        return rep * 2 + z % 2, (rep + j) % 8

    def greet_source(j, n):
        sz, srep = source(j)
        other = jnp.logical_or(sz != z, srep != rep)

        @pl.when(other)
        def _():
            pl.semaphore_signal(bar, inc=1, device_id=dev(y, sz, srep), device_id_type=MESH)

        return n

    lax.fori_loop(0, 8, greet_source, 0)
    self_holder = home == rep
    pl.semaphore_wait(bar, GROUP - 1 + 8 - jnp.where(self_holder, 1, 0).astype(i32))

    def part_copy(j):
        return pltpu.make_async_remote_copy(
            src_ref=part_ref,
            dst_ref=held.at[rep],
            send_sem=held_send.at[j],
            recv_sem=held_recv.at[rep],
            device_id=dev(y, holder(j), home),
            device_id_type=MESH,
        )

    def send_part(j, carry):
        other = jnp.logical_or(holder(j) != z, home != rep)

        @pl.when(other)
        def _():
            part_copy(j).start()

        return carry

    lax.fori_loop(0, 8, send_part, 0)
    own = pltpu.make_async_copy(part_ref, held.at[rep], own_sem)

    @pl.when(self_holder)
    def _():
        own.start()

    tables(owner_ref, row_ref, pos, tab, rows)
    lines16 = lax.broadcasted_iota(i32, (16, B), 0)

    def ask_copy(m):
        return pltpu.make_async_remote_copy(
            src_ref=ask.at[m],
            dst_ref=asked_ref.at[me],
            send_sem=ask_send.at[m],
            recv_sem=ask_recv.at[me],
            device_id=member_dev(m, z),
            device_id_type=MESH,
        )

    def ask_pair(p, carry):
        a, b = peer(2 * p, y, z, rep), peer(2 * p + 1, y, z, rep)
        pick_a, pick_b = slots_of(pos, a), slots_of(pos, b)
        picks[a] = pick_a
        picks[b] = pick_b
        lhs = jnp.where(lines16 == 0, rows[pl.ds(a, 1), :], 0.0)
        lhs = jnp.where(lines16 == 1, tab[pl.ds(a, 1), :], lhs)
        lhs = jnp.where(lines16 == 2, rows[pl.ds(b, 1), :], lhs)
        lhs = jnp.where(lines16 == 3, tab[pl.ds(b, 1), :], lhs).astype(bf16)
        got = lax.dot_general(
            lhs, jnp.concatenate([pick_a, pick_b], axis=0), NT, preferred_element_type=f32
        )
        code_a = (got[0:1, :SLOTS] + got[1:2, :SLOTS] * float(ROWS)).astype(i32)
        code_b = (got[2:3, SLOTS:] + got[3:4, SLOTS:] * float(ROWS)).astype(i32)
        ask[a] = jnp.broadcast_to(code_a, (8, SLOTS))
        ask[b] = jnp.broadcast_to(code_b, (8, SLOTS))

        @pl.when(p > 0)
        def _():
            ask_copy(a).start()

        @pl.when(p == 0)
        def _():
            asked_ref[me] = ask[me]

        ask_copy(b).start()
        return carry

    lax.fori_loop(0, GROUP // 2, ask_pair, 0)

    def await_part(j, carry):
        sz, srep = source(j)
        other = jnp.logical_or(sz != z, srep != rep)

        @pl.when(other)
        def _():
            pltpu.make_async_remote_copy(
                src_ref=part_ref,
                dst_ref=held.at[srep],
                send_sem=held_send.at[0],
                recv_sem=held_recv.at[srep],
                device_id=dev(y, sz, srep),
                device_id_type=MESH,
            ).wait_recv()

        return carry

    lax.fori_loop(0, 8, await_part, 0)

    @pl.when(self_holder)
    def _():
        own.wait()

    def reply_copy(m):
        return pltpu.make_async_remote_copy(
            src_ref=back.at[m],
            dst_ref=replies.at[me],
            send_sem=rep_send.at[m],
            recv_sem=rep_recv.at[me],
            device_id=member_dev(m, z),
            device_id_type=MESH,
        )

    def await_ask(m):
        pltpu.make_async_remote_copy(
            src_ref=ask.at[m],
            dst_ref=asked_ref.at[m],
            send_sem=ask_send.at[m],
            recv_sem=ask_recv.at[m],
            device_id=member_dev(m, z),
            device_id_type=MESH,
        ).wait_recv()

    def reply_pair(p, carry):
        a, b = peer_back(2 * p, y, z, rep), peer_back(2 * p + 1, y, z, rep)

        @pl.when(p > 0)
        def _():
            await_ask(a)

        await_ask(b)
        code = jnp.concatenate([asked_ref[a][0:1, :], asked_ref[b][0:1, :]], axis=1)
        table = code // ROWS
        found = jnp.dot(
            held[...].reshape(WIDE, ROWS), rows_of(code), preferred_element_type=f32
        )
        out = found[0:E]
        for t in range(1, NCOLD):
            out = jnp.where(table == t, found[t * E : (t + 1) * E], out)
        out = out.astype(bf16)
        back[a] = out[:, :SLOTS]
        back[b] = out[:, SLOTS:]

        @pl.when(p > 0)
        def _():
            reply_copy(a).start()

        @pl.when(p == 0)
        def _():
            replies[me] = back[me]

        reply_copy(b).start()
        return carry

    lax.fori_loop(0, GROUP // 2, reply_pair, 0)

    pooled[...] = jnp.zeros((WIDE, B), f32)

    def await_reply(m):
        pltpu.make_async_remote_copy(
            src_ref=back.at[m],
            dst_ref=replies.at[m],
            send_sem=rep_send.at[m],
            recv_sem=rep_recv.at[m],
            device_id=member_dev(m, z),
            device_id_type=MESH,
        ).wait_recv()

    def pool_pair(p, carry):
        a, b = peer(2 * p, y, z, rep), peer(2 * p + 1, y, z, rep)

        @pl.when(p > 0)
        def _():
            await_reply(a)

        await_reply(b)
        got_a = jnp.dot(replies[a], picks[a], preferred_element_type=f32)
        got_b = jnp.dot(replies[b], picks[b], preferred_element_type=f32)
        tab_a, tab_b = tab[pl.ds(a, 1), :], tab[pl.ds(b, 1), :]
        for t in range(NCOLD):
            more = jnp.where(tab_a == float(t), got_a, 0.0) + jnp.where(tab_b == float(t), got_b, 0.0)
            pooled[t * E : (t + 1) * E, :] += more
        return carry

    lax.fori_loop(0, GROUP // 2, pool_pair, 0)
    pooled_ref[...] = pooled[...].astype(bf16)

    def drain(i, carry):
        m = peer(i, y, z, rep)
        ask_copy(m).wait_send()
        reply_copy(m).wait_send()
        return carry

    lax.fori_loop(1, GROUP, drain, 0)

    def drain_part(j, carry):
        other = jnp.logical_or(holder(j) != z, home != rep)

        @pl.when(other)
        def _():
            part_copy(j).wait_send()

        return carry

    lax.fori_loop(0, 8, drain_part, 0)


def backward_kernel(
    owner_ref, dpool_ref, asked_ref, grad_ref,
    arrived, out, pos, tab, acc, part_out, part_in, whole,
    out_send, out_recv, part_send, part_recv, all_send, all_recv,
):
    y, z, rep = place_of()
    me = member_of(y, z, rep)
    bar = greet(y, z, rep)
    home = z // 2
    owner_z = rep * 2 + z % 2
    self_holder = home == rep

    def source(j):
        return (z + 2 * j) % 16, home

    def greet_source(j, n):
        sz, srep = source(j)
        other = jnp.logical_or(sz != z, srep != rep)

        @pl.when(other)
        def _():
            pl.semaphore_signal(bar, inc=1, device_id=dev(y, sz, srep), device_id_type=MESH)

        return n

    lax.fori_loop(0, 8, greet_source, 0)
    pl.semaphore_wait(bar, GROUP - 1 + 8 - jnp.where(self_holder, 1, 0).astype(i32))
    tables(owner_ref, None, pos, tab, None)

    def out_copy(m):
        return pltpu.make_async_remote_copy(
            src_ref=out.at[m],
            dst_ref=arrived.at[me],
            send_sem=out_send.at[m],
            recv_sem=out_recv.at[me],
            device_id=member_dev(m, z),
            device_id_type=MESH,
        )

    def pack(m):
        which = tab[pl.ds(m, 1), :]
        grads = dpool_ref[0:E, :]
        for t in range(1, NCOLD):
            grads = jnp.where(which == float(t), dpool_ref[t * E : (t + 1) * E, :], grads)
        out[m] = lax.dot_general(
            grads.astype(bf16), slots_of(pos, m), NT, preferred_element_type=f32
        ).astype(bf16)

    def pack_pair(p, carry):
        a, b = peer(2 * p, y, z, rep), peer(2 * p + 1, y, z, rep)
        pack(a)
        pack(b)

        @pl.when(p > 0)
        def _():
            out_copy(a).start()

        @pl.when(p == 0)
        def _():
            arrived[me] = out[me]

        out_copy(b).start()
        return carry

    lax.fori_loop(0, GROUP // 2, pack_pair, 0)
    acc[...] = jnp.zeros((WIDE, ROWS), f32)

    def await_out(m):
        pltpu.make_async_remote_copy(
            src_ref=out.at[m],
            dst_ref=arrived.at[m],
            send_sem=out_send.at[m],
            recv_sem=out_recv.at[m],
            device_id=member_dev(m, z),
            device_id_type=MESH,
        ).wait_recv()

    def add_pair(p, carry):
        a, b = peer_back(2 * p, y, z, rep), peer_back(2 * p + 1, y, z, rep)

        @pl.when(p > 0)
        def _():
            await_out(a)

        await_out(b)
        code = jnp.concatenate([asked_ref[a][0:1, :], asked_ref[b][0:1, :]], axis=1)
        table = code // ROWS
        grads = jnp.concatenate([arrived[a], arrived[b]], axis=1).astype(f32)
        lhs = jnp.concatenate(
            [jnp.where(table == t, grads, 0.0).astype(bf16) for t in range(NCOLD)], axis=0
        )
        acc[...] += lax.dot_general(lhs, rows_of(code), NT, preferred_element_type=f32)
        return carry

    lax.fori_loop(0, GROUP // 2, add_pair, 0)

    def part_copy(j):
        return pltpu.make_async_remote_copy(
            src_ref=part_out.at[j],
            dst_ref=part_in.at[home],
            send_sem=part_send.at[j],
            recv_sem=part_recv.at[home],
            device_id=dev(y, owner_z, j),
            device_id_type=MESH,
        )

    def send_part(j, carry):
        part_out[j] = acc[pl.ds(pl.multiple_of(j * PART, PART), PART), :].astype(bf16)
        other = jnp.logical_or(owner_z != z, j != rep)

        @pl.when(other)
        def _():
            part_copy(j).start()

        @pl.when(jnp.logical_not(other))
        def _():
            part_in[home] = part_out[j]

        return carry

    lax.fori_loop(0, 8, send_part, 0)

    def await_part(j, carry):
        sz, srep = source(j)
        other = jnp.logical_or(sz != z, srep != rep)

        @pl.when(other)
        def _():
            pltpu.make_async_remote_copy(
                src_ref=part_out.at[0],
                dst_ref=part_in.at[sz // 2],
                send_sem=part_send.at[0],
                recv_sem=part_recv.at[sz // 2],
                device_id=dev(y, sz, srep),
                device_id_type=MESH,
            ).wait_recv()

        return carry

    lax.fori_loop(0, 8, await_part, 0)
    total = part_in[0].astype(f32)
    for g in range(1, 8):
        total = total + part_in[g].astype(f32)
    whole[rep] = total.astype(bf16)

    def all_copy(j):
        return pltpu.make_async_remote_copy(
            src_ref=whole.at[rep],
            dst_ref=whole.at[rep],
            send_sem=all_send.at[j],
            recv_sem=all_recv.at[rep],
            device_id=dev(y, z, (rep + j) % 8),
            device_id_type=MESH,
        )

    def send_all(j, carry):
        all_copy(j).start()
        return carry

    lax.fori_loop(1, 8, send_all, 0)

    def await_all(j, carry):
        other = (rep + 8 - j) % 8
        pltpu.make_async_remote_copy(
            src_ref=whole.at[other],
            dst_ref=whole.at[other],
            send_sem=all_send.at[j],
            recv_sem=all_recv.at[other],
            device_id=dev(y, z, other),
            device_id_type=MESH,
        ).wait_recv()
        return carry

    lax.fori_loop(1, 8, await_all, 0)
    grad_ref[...] = whole[...].astype(f32)

    def drain(i, carry):
        out_copy(peer(i, y, z, rep)).wait_send()
        return carry

    lax.fori_loop(1, GROUP, drain, 0)

    def drain_part(j, carry):
        other = jnp.logical_or(owner_z != z, j != rep)

        @pl.when(other)
        def _():
            part_copy(j).wait_send()

        return carry

    lax.fori_loop(0, 8, drain_part, 0)

    def drain_all(j, carry):
        all_copy(j).wait_send()
        return carry

    lax.fori_loop(1, 8, drain_all, 0)


def dense_kernel(
    grad_ref, total_ref,
    core_in, pair, x_in, mine, y_in, column, z_in, strip,
    core_send, core_recv, x_send, x_recv, y_send, y_recv, z_send, z_recv, zb_send, zb_recv, yb_send, yb_recv,
):
    y, z, rep = place_of()
    x, c = rep // 2, rep % 2
    other_c = 1 - c
    bar = pltpu.get_barrier_semaphore()

    def signal(y_, z_, rep_):
        pl.semaphore_signal(bar, inc=1, device_id=dev(y_, z_, rep_), device_id_type=MESH)

    signal(y, z, x * 2 + other_c)
    for k in range(1, 4):
        signal(y, z, ((x + k) % 4) * 2 + c)
        signal((y + k) % 4, z, rep)
    for k in range(1, 16):
        signal(y, (z + k) % 16, rep)
    pl.semaphore_wait(bar, 1 + 3 + 3 + 15)

    core_copies = []
    for k in range(4):
        copy = pltpu.make_async_remote_copy(
            src_ref=grad_ref.at[2 * k + other_c],
            dst_ref=core_in.at[k],
            send_sem=core_send.at[k],
            recv_sem=core_recv.at[k],
            device_id=dev(y, z, x * 2 + other_c),
            device_id_type=MESH,
        )
        copy.start()
        core_copies.append(copy)
    for k in range(4):
        core_copies[k].wait_recv()
    for k in range(4):
        pair[k] = (grad_ref[2 * k + c].astype(f32) + core_in[k].astype(f32)).astype(bf16)

    x_copies = []
    for k in (2, 1, 3):
        to = (x + k) % 4
        copy = pltpu.make_async_remote_copy(
            src_ref=pair.at[to],
            dst_ref=x_in.at[k],
            send_sem=x_send.at[k],
            recv_sem=x_recv.at[k],
            device_id=dev(y, z, to * 2 + c),
            device_id_type=MESH,
        )
        copy.start()
        x_copies.append(copy)
    for copy in x_copies:
        copy.wait_recv()
    mine[...] = (
        pair[x].astype(f32) + x_in[1].astype(f32) + x_in[2].astype(f32) + x_in[3].astype(f32)
    )

    y_copies = []
    for k in (2, 1, 3):
        to = (y + k) % 4
        copy = pltpu.make_async_remote_copy(
            src_ref=mine.at[pl.ds(pl.multiple_of(to * 8, 8), 8), :],
            dst_ref=y_in.at[k],
            send_sem=y_send.at[k],
            recv_sem=y_recv.at[k],
            device_id=dev(to, z, rep),
            device_id_type=MESH,
        )
        copy.start()
        y_copies.append(copy)
    for copy in y_copies:
        copy.wait_recv()
    column[:, CROSS:] = jnp.zeros((8, PADDED - CROSS), f32)
    column[:, :CROSS] = (
        mine[pl.ds(pl.multiple_of(y * 8, 8), 8), :] + y_in[1] + y_in[2] + y_in[3]
    )

    def cols(j):
        return pl.ds(pl.multiple_of(j * VCOLS, VCOLS), VCOLS)

    def z_copy(k):
        to = (z + k) % 16
        return pltpu.make_async_remote_copy(
            src_ref=column.at[:, cols(to)],
            dst_ref=z_in.at[k],
            send_sem=z_send.at[k],
            recv_sem=z_recv.at[k],
            device_id=dev(y, to, rep),
            device_id_type=MESH,
        )

    def z_start(k, carry):
        @pl.when((z + k) % 16 < VCHUNKS)
        def _():
            z_copy(k).start()

        return carry

    lax.fori_loop(1, 16, z_start, 0)

    def zb_copy(k):
        return pltpu.make_async_remote_copy(
            src_ref=strip.at[:, cols(z)],
            dst_ref=strip.at[:, cols(z)],
            send_sem=zb_send.at[k],
            recv_sem=zb_recv.at[z],
            device_id=dev(y, (z + k) % 16, rep),
            device_id_type=MESH,
        )

    @pl.when(z < VCHUNKS)
    def _():
        def z_wait(k, carry):
            pltpu.make_async_remote_copy(
                src_ref=z_in.at[k],
                dst_ref=z_in.at[k],
                send_sem=z_send.at[k],
                recv_sem=z_recv.at[k],
                device_id=dev(y, (z + 16 - k) % 16, rep),
                device_id_type=MESH,
            ).wait_recv()
            return carry

        lax.fori_loop(1, 16, z_wait, 0)
        z_in[0] = column[:, cols(z)]
        total = z_in[0]
        for k in range(1, 16):
            total = total + z_in[k]
        strip[:, cols(z)] = total

        def zb_start(k, carry):
            zb_copy(k).start()
            return carry

        lax.fori_loop(1, 16, zb_start, 0)

    def zb_wait(k, carry):
        other = (z + 16 - k) % 16

        @pl.when(other < VCHUNKS)
        def _():
            pltpu.make_async_remote_copy(
                src_ref=strip.at[:, cols(other)],
                dst_ref=strip.at[:, cols(other)],
                send_sem=zb_send.at[k],
                recv_sem=zb_recv.at[other],
                device_id=dev(y, other, rep),
                device_id_type=MESH,
            ).wait_recv()

        return carry

    lax.fori_loop(1, 16, zb_wait, 0)

    def band(j):
        return pl.ds(pl.multiple_of(j * 8, 8), 8)

    total_ref[band(y), :] = strip[:, :CROSS]
    yb_copies = []
    for k in (2, 1, 3):
        copy = pltpu.make_async_remote_copy(
            src_ref=total_ref.at[band(y), :],
            dst_ref=total_ref.at[band(y), :],
            send_sem=yb_send.at[k],
            recv_sem=yb_recv.at[k],
            device_id=dev((y + k) % 4, z, rep),
            device_id_type=MESH,
        )
        copy.start()
        yb_copies.append(copy)
    for k in (2, 1, 3):
        came = band((y + 4 - k) % 4)
        pltpu.make_async_remote_copy(
            src_ref=total_ref.at[came, :],
            dst_ref=total_ref.at[came, :],
            send_sem=yb_send.at[k],
            recv_sem=yb_recv.at[k],
            device_id=dev((y + 4 - k) % 4, z, rep),
            device_id_type=MESH,
        ).wait_recv()
    for copy in core_copies + x_copies + y_copies + yb_copies:
        copy.wait_send()

    def z_drain(k, carry):
        @pl.when((z + k) % 16 < VCHUNKS)
        def _():
            z_copy(k).wait_send()

        @pl.when(z < VCHUNKS)
        def _():
            zb_copy(k).wait_send()

        return carry

    lax.fori_loop(1, 16, z_drain, 0)


def vmem():
    return pl.BlockSpec(memory_space=pltpu.VMEM)


def dma(n):
    return pltpu.SemaphoreType.DMA((n,))


def forward_call(owner, row, part):
    return pl.pallas_call(
        forward_kernel,
        out_shape=(
            jax.ShapeDtypeStruct((WIDE, B), bf16),
            jax.ShapeDtypeStruct((GROUP, 8, SLOTS), i32),
        ),
        in_specs=[vmem()] * 3,
        out_specs=(vmem(), vmem()),
        scratch_shapes=[
            pltpu.VMEM((8, PART, ROWS), bf16),
            pltpu.VMEM((GROUP, E, SLOTS), bf16),
            pltpu.VMEM((GROUP, E, SLOTS), bf16),
            pltpu.VMEM((GROUP, 8, SLOTS), i32),
            pltpu.VMEM((GROUP, B), f32),
            pltpu.VMEM((GROUP, B), f32),
            pltpu.VMEM((GROUP, B), f32),
            pltpu.VMEM((GROUP, SLOTS, B), bf16),
            pltpu.VMEM((WIDE, B), f32),
            dma(8), dma(8), dma(GROUP), dma(GROUP), dma(GROUP), dma(GROUP),
            pltpu.SemaphoreType.DMA,
        ],
        compiler_params=pltpu.CompilerParams(
            collective_id=0, has_side_effects=True, vmem_limit_bytes=40 << 20
        ),
    )(owner, row, part)


def backward_call(owner, dpool, asked):
    return pl.pallas_call(
        backward_kernel,
        out_shape=jax.ShapeDtypeStruct((8, PART, ROWS), f32),
        in_specs=[vmem()] * 3,
        out_specs=vmem(),
        scratch_shapes=[
            pltpu.VMEM((GROUP, E, SLOTS), bf16),
            pltpu.VMEM((GROUP, E, SLOTS), bf16),
            pltpu.VMEM((GROUP, B), f32),
            pltpu.VMEM((GROUP, B), f32),
            pltpu.VMEM((WIDE, ROWS), f32),
            pltpu.VMEM((8, PART, ROWS), bf16),
            pltpu.VMEM((8, PART, ROWS), bf16),
            pltpu.VMEM((8, PART, ROWS), bf16),
            dma(GROUP), dma(GROUP), dma(8), dma(8), dma(8), dma(8),
        ],
        compiler_params=pltpu.CompilerParams(
            collective_id=1, has_side_effects=True, vmem_limit_bytes=40 << 20
        ),
    )(owner, dpool, asked)


def dense_call(grad):
    return pl.pallas_call(
        dense_kernel,
        out_shape=jax.ShapeDtypeStruct((32, CROSS), f32),
        in_specs=[vmem()],
        out_specs=vmem(),
        scratch_shapes=[
            pltpu.VMEM((4, 32, CROSS), bf16),
            pltpu.VMEM((4, 32, CROSS), bf16),
            pltpu.VMEM((4, 32, CROSS), bf16),
            pltpu.VMEM((32, CROSS), f32),
            pltpu.VMEM((4, 8, CROSS), f32),
            pltpu.VMEM((8, PADDED), f32),
            pltpu.VMEM((16, 8, VCOLS), f32),
            pltpu.VMEM((8, PADDED), f32),
            dma(4), dma(4), dma(4), dma(4), dma(4), dma(4),
            dma(16), dma(16), dma(16), dma(16), dma(4), dma(4),
        ],
        compiler_params=pltpu.CompilerParams(
            collective_id=2, has_side_effects=True, vmem_limit_bytes=40 << 20
        ),
    )(grad)


def body(
    bottom,
    hot_ids,
    hot_tables,
    cold_owner,
    cold_row,
    cold_rows,
    cold_acc,
    u_weight,
    v_weight,
    v_acc,
    cross_bias,
    head,
    labels,
):
    rep = lax.axis_index("replica")
    owner_t, row_t = cold_owner.T, cold_row.T
    turned = cold_rows.reshape(NCOLD, ROWS, E).transpose(0, 2, 1).reshape(8, PART, ROWS)
    part = lax.dynamic_index_in_dim(turned, rep, 0, keepdims=False).astype(bf16)
    u_full, v_half = (
        lax.all_gather(u_weight, "replica", axis=0, tiled=True),
        lax.all_gather(v_weight.astype(bf16), "replica", axis=0, tiled=True),
    )
    pooled_t, asked = forward_call(owner_t, row_t, part)
    pooled = pooled_t.T
    hot_one = (hot_ids[:, :, None] == jnp.arange(128, dtype=i32)[None, None, :]).astype(bf16)
    hot = jnp.einsum("bjv,jve->bje", hot_one, hot_tables, preferred_element_type=f32).astype(bf16)
    first = jnp.concatenate([bottom, pooled, hot.reshape(B, NHOT * E)], axis=1)
    low = jnp.dot(first, u_full, preferred_element_type=f32).astype(bf16)
    mixing = jnp.dot(low, v_half, preferred_element_type=f32) + cross_bias[None, :]
    wide = first.astype(f32)
    crossed = wide * mixing + wide
    logit = jnp.sum(crossed * head[None, :], axis=1)
    dlogit = jax.nn.sigmoid(logit) - labels.astype(f32)
    dcross = dlogit[:, None] * head[None, :]
    dmix = (dcross * wide).astype(bf16)
    grad_local = lax.dot_general(low, dmix, (((0,), (0,)), ((), ())), preferred_element_type=f32)
    dlow = lax.dot_general(dmix, v_half, NT, preferred_element_type=f32).astype(bf16)
    span_end = E + WIDE
    dpool = dcross[:, E:span_end] * (mixing[:, E:span_end] + 1.0)
    dpool = dpool + lax.dot_general(dlow, u_full[E:span_end], NT, preferred_element_type=f32)
    dpool_t = dpool.T.astype(bf16).astype(f32)
    grad_rows = backward_call(owner_t, dpool_t, asked)
    grad_rows = grad_rows.reshape(NCOLD, E, ROWS).transpose(0, 2, 1).reshape(NCOLD * ROWS, E)
    new_cold_acc = cold_acc + jnp.mean(grad_rows * grad_rows, axis=1)
    new_cold_rows = cold_rows - row_rate * grad_rows / (jnp.sqrt(new_cold_acc)[:, None] + eps_value)
    grad_mine = dense_call(grad_local.astype(bf16).reshape(8, 32, CROSS))
    acc_dense = v_acc + jnp.mean(grad_mine * grad_mine, axis=1)
    new_v = v_weight - dense_rate * grad_mine / (jnp.sqrt(acc_dense)[:, None] + eps_value)
    return (new_cold_rows, new_cold_acc, new_v)


def solution(mesh):
    return jax.shard_map(
        body,
        mesh=mesh,
        in_specs=(
            P(("table", "replica"), None),
            P(("table", "replica"), None),
            P(),
            P(("table", "replica"), None),
            P(("table", "replica"), None),
            P("table", None),
            P("table"),
            P("replica", None),
            P("replica", None),
            P("replica"),
            P(),
            P(),
            P(("table", "replica")),
        ),
        out_specs=(P("table", None), P("table"), P("replica", None)),
        check_vma=False,
    )
```

```python
import functools
import jax
import jax.numpy as jnp
from jax import lax
from jax.experimental import pallas as pl
from jax.experimental.pallas import tpu as pltpu
from jax.sharding import PartitionSpec as P

NCOLD = 6
LOOK = 2
NHOT = 20
LOOKUPS = NCOLD * LOOK
E = 128
B = 256
ROWS = 256
SLOTS = 128
GROUP = 64
ITSELF = 40
PAIR_SELF = ITSELF // 2
WIDE = NCOLD * E
PART = WIDE // 8
CROSS = 3456
PADDED = 3584
COLS = 384
U_ROWS = 432
V_ROWS = 32
RANK = 256
VCHUNKS = 14
VCOLS = 256
MESH = pl.DeviceIdType.MESH

row_rate = 0.1
dense_rate = 0.05
eps_value = 1e-08

f32 = jnp.float32
bf16 = jnp.bfloat16
i32 = jnp.int32
NT = (((1,), (1,)), ((), ()))


def place_of():
    table, rep = lax.axis_index("table"), lax.axis_index("replica")
    return table // 16, table % 16, rep


def dev(y, z, rep):
    return {"table": y * 16 + z, "replica": rep}


def member_of(y, z, rep):
    return y * 16 + rep * 2 + z % 2


def member_dev(member, z):
    return dev(member // 16, z - z % 2 + member % 2, (member // 2) % 8)


def peer(i, y, z, rep):
    py = (y + 2 + i // 16) % 4
    px = (rep // 2 + 2 + (i // 4) % 4) % 4
    pc = (rep + (i // 2) % 2) % 2
    pz = (z + i) % 2
    return py * 16 + px * 4 + pc * 2 + pz


def peer_back(i, y, z, rep):
    py = (y + 6 - i // 16) % 4
    px = (rep // 2 + 6 - (i // 4) % 4) % 4
    pc = (rep + (i // 2) % 2) % 2
    pz = (z + i) % 2
    return py * 16 + px * 4 + pc * 2 + pz


def tables(owner_ref, row_ref, pos, tab, rows):
    owners = lax.broadcasted_iota(i32, (GROUP, B), 0)
    named = jnp.zeros((GROUP, B), f32)
    table = jnp.zeros((GROUP, B), f32)
    row = jnp.zeros((GROUP, B), f32)
    for k in range(LOOKUPS):
        hit = owners == owner_ref[k : k + 1, :]
        named = jnp.where(hit, 1.0, named)
        table = jnp.where(hit, float(k // LOOK), table)
        row = jnp.where(hit, row_ref[k : k + 1, :].astype(f32), row)
    before = jnp.where(
        lax.broadcasted_iota(i32, (B, B), 0) < lax.broadcasted_iota(i32, (B, B), 1), 1.0, 0.0
    ).astype(bf16)
    place = jnp.dot(named.astype(bf16), before, preferred_element_type=f32)
    pos[...] = jnp.where(named > 0.0, place, -1.0)
    tab[...] = table
    rows[...] = row


def slots_of(pos, o):
    lines = lax.broadcasted_iota(i32, (SLOTS, B), 0).astype(f32)
    return jnp.where(lines == pos[pl.ds(o, 1), :], 1.0, 0.0).astype(bf16)


def rows_of(code):
    lines = lax.broadcasted_iota(i32, (ROWS, code.shape[1]), 0)
    return jnp.where(lines == code % ROWS, 1.0, 0.0).astype(bf16)


def others(count, act):
    def step(i, carry):
        @pl.when(i != ITSELF)
        def _():
            act(i)

        return carry

    lax.fori_loop(0, count, step, 0)


def step_kernel(
    owner_ref, row_ref, part_ref, bottom_ref, ids_ref, hot_ref, u_ref, v_ref, bias_ref, head_ref, label_ref,
    grad_ref, total_ref,
    held, replies, back, ask, asked, pos, tab, rows, picks, pooled,
    u_full, v_full, first, mixed, low_t, dlow, dpool, grads,
    arrived, out, acc, part_out, part_in, whole,
    core_in, pair, x_in, mine, y_in, column, z_in, strip,
    held_send, held_recv, ask_send, ask_recv, rep_send, rep_recv, own_sem,
    w_send, w_recv, wc_send, wc_recv,
    out_send, out_recv, part_send, part_recv, all_send, all_recv,
    core_send, core_recv, x_send, x_recv, y_send, y_recv, z_send, z_recv, zb_send, zb_recv, yb_send, yb_recv,
):
    y, z, rep = place_of()
    x, c = rep // 2, rep % 2
    other_c = 1 - c
    sibling = x * 2 + other_c
    me = member_of(y, z, rep)
    home = z // 2
    owner_z = rep * 2 + z % 2
    self_holder = home == rep

    bar = pltpu.get_barrier_semaphore()

    def signal(y_, z_, rep_):
        pl.semaphore_signal(bar, inc=1, device_id=dev(y_, z_, rep_), device_id_type=MESH)

    def greet_member(i):
        pl.semaphore_signal(
            bar, inc=1, device_id=member_dev(peer(i, y, z, rep), z), device_id_type=MESH
        )

    others(GROUP, greet_member)

    def holder(j):
        return (z + 2 * j) % 16

    def source(j):
        return owner_z, (rep + j) % 8

    def greet_parts(j, carry):
        @pl.when(jnp.logical_or(holder(j) != z, home != rep))
        def _():
            signal(y, holder(j), home)

        sz, srep = source(j)

        @pl.when(jnp.logical_or(sz != z, srep != rep))
        def _():
            signal(y, sz, srep)

        return carry

    lax.fori_loop(0, 8, greet_parts, 0)

    def greet_z(k, carry):
        signal(y, (z + k) % 16, rep)
        return carry

    lax.fori_loop(1, 16, greet_z, 0)
    pl.semaphore_wait(bar, GROUP - 1 + 16 - jnp.where(self_holder, 2, 0).astype(i32) + 15)

    def part_copy(j):
        return pltpu.make_async_remote_copy(
            src_ref=part_ref,
            dst_ref=held.at[rep],
            send_sem=held_send.at[j],
            recv_sem=held_recv.at[rep],
            device_id=dev(y, holder(j), home),
            device_id_type=MESH,
        )

    def send_part(j, carry):
        @pl.when(jnp.logical_or(holder(j) != z, home != rep))
        def _():
            part_copy(j).start()

        return carry

    lax.fori_loop(0, 8, send_part, 0)
    own = pltpu.make_async_copy(part_ref, held.at[rep], own_sem.at[0])

    @pl.when(self_holder)
    def _():
        own.start()

    def u_at(r):
        return u_full.at[pl.ds(pl.multiple_of(r * U_ROWS, 16), U_ROWS), :]

    def v_at(r):
        return v_full.at[pl.ds(pl.multiple_of(r * V_ROWS, 16), V_ROWS), :]

    def weight_copies(src_u, src_v, r, sends, recvs, slot, y_, z_, rep_):
        return [
            pltpu.make_async_remote_copy(
                src_ref=src,
                dst_ref=dst,
                send_sem=sends.at[2 * slot + i],
                recv_sem=recvs.at[2 * slot + i],
                device_id=dev(y_, z_, rep_),
                device_id_type=MESH,
            )
            for i, (src, dst) in enumerate([(src_u, u_at(r)), (src_v, v_at(r))])
        ]

    w_copies = []
    for k in (2, 1, 3):
        to = ((x + k) % 4) * 2 + c
        w_copies += weight_copies(u_ref, v_ref, rep, w_send, w_recv, k, y, z, to)
    w_copies += weight_copies(u_ref, v_ref, rep, w_send, w_recv, 0, y, z, sibling)
    for copy in w_copies:
        copy.start()
    own_u = pltpu.make_async_copy(u_ref, u_at(rep), own_sem.at[1])
    own_v = pltpu.make_async_copy(v_ref, v_at(rep), own_sem.at[2])
    own_u.start()
    own_v.start()

    tables(owner_ref, row_ref, pos, tab, rows)
    lines16 = lax.broadcasted_iota(i32, (16, B), 0)

    def ask_copy(m):
        return pltpu.make_async_remote_copy(
            src_ref=ask.at[m],
            dst_ref=asked.at[me],
            send_sem=ask_send.at[m],
            recv_sem=ask_recv.at[me],
            device_id=member_dev(m, z),
            device_id_type=MESH,
        )

    def ask_pair(p, carry):
        a, b = peer(2 * p, y, z, rep), peer(2 * p + 1, y, z, rep)
        pick_a, pick_b = slots_of(pos, a), slots_of(pos, b)
        picks[a] = pick_a
        picks[b] = pick_b
        lhs = jnp.where(lines16 == 0, rows[pl.ds(a, 1), :], 0.0)
        lhs = jnp.where(lines16 == 1, tab[pl.ds(a, 1), :], lhs)
        lhs = jnp.where(lines16 == 2, rows[pl.ds(b, 1), :], lhs)
        lhs = jnp.where(lines16 == 3, tab[pl.ds(b, 1), :], lhs).astype(bf16)
        got = lax.dot_general(
            lhs, jnp.concatenate([pick_a, pick_b], axis=0), NT, preferred_element_type=f32
        )
        code_a = (got[0:1, :SLOTS] + got[1:2, :SLOTS] * float(ROWS)).astype(i32)
        code_b = (got[2:3, SLOTS:] + got[3:4, SLOTS:] * float(ROWS)).astype(i32)
        ask[a] = jnp.broadcast_to(code_a, (8, SLOTS))
        ask[b] = jnp.broadcast_to(code_b, (8, SLOTS))

        @pl.when(p != PAIR_SELF)
        def _():
            ask_copy(a).start()

        @pl.when(p == PAIR_SELF)
        def _():
            asked[me] = ask[me]

        ask_copy(b).start()
        return carry

    lax.fori_loop(0, GROUP // 2, ask_pair, 0)

    first[:, 0:E] = bottom_ref[...]
    lanes = lax.broadcasted_iota(i32, (B, E), 1)
    for j in range(NHOT):
        one = jnp.where(lanes == ids_ref[:, j : j + 1], 1.0, 0.0).astype(bf16)
        at = E + WIDE + j * E
        first[:, at : at + E] = jnp.dot(one, hot_ref[j], preferred_element_type=f32).astype(bf16)

    wc_copies = []
    for k in (1, 3, 2):
        came = ((x + 4 - k) % 4) * 2 + c
        for copy in weight_copies(u_at(came), v_at(came), came, w_send, w_recv, k, y, z, came):
            copy.wait_recv()
        forward = weight_copies(u_at(came), v_at(came), came, wc_send, wc_recv, k, y, z, sibling)
        for copy in forward:
            copy.start()
        wc_copies += forward

    def await_part(j, carry):
        sz, srep = source(j)

        @pl.when(jnp.logical_or(sz != z, srep != rep))
        def _():
            pltpu.make_async_remote_copy(
                src_ref=part_ref,
                dst_ref=held.at[srep],
                send_sem=held_send.at[0],
                recv_sem=held_recv.at[srep],
                device_id=dev(y, sz, srep),
                device_id_type=MESH,
            ).wait_recv()

        return carry

    lax.fori_loop(0, 8, await_part, 0)

    @pl.when(self_holder)
    def _():
        own.wait()

    def reply_copy(m):
        return pltpu.make_async_remote_copy(
            src_ref=back.at[m],
            dst_ref=replies.at[me],
            send_sem=rep_send.at[m],
            recv_sem=rep_recv.at[me],
            device_id=member_dev(m, z),
            device_id_type=MESH,
        )

    def await_ask(m):
        pltpu.make_async_remote_copy(
            src_ref=ask.at[m],
            dst_ref=asked.at[m],
            send_sem=ask_send.at[m],
            recv_sem=ask_recv.at[m],
            device_id=member_dev(m, z),
            device_id_type=MESH,
        ).wait_recv()

    def reply_pair(p, carry):
        a, b = peer_back(2 * p, y, z, rep), peer_back(2 * p + 1, y, z, rep)

        @pl.when(p != PAIR_SELF)
        def _():
            await_ask(a)

        await_ask(b)
        code = jnp.concatenate([asked[a][0:1, :], asked[b][0:1, :]], axis=1)
        table = code // ROWS
        found = jnp.dot(
            held[...].reshape(WIDE, ROWS), rows_of(code), preferred_element_type=f32
        )
        got = found[0:E]
        for t in range(1, NCOLD):
            got = jnp.where(table == t, found[t * E : (t + 1) * E], got)
        got = got.astype(bf16)
        back[a] = got[:, :SLOTS]
        back[b] = got[:, SLOTS:]

        @pl.when(p != PAIR_SELF)
        def _():
            reply_copy(a).start()

        @pl.when(p == PAIR_SELF)
        def _():
            replies[me] = back[me]

        reply_copy(b).start()
        return carry

    lax.fori_loop(0, GROUP // 2, reply_pair, 0)

    for k in range(4):
        came = ((x + 4 - k) % 4) * 2 + other_c
        sends, recvs = (w_send, w_recv) if k == 0 else (wc_send, wc_recv)
        for copy in weight_copies(u_at(came), v_at(came), came, sends, recvs, k, y, z, sibling):
            copy.wait_recv()
    own_u.wait()
    own_v.wait()
    hot_at = E + WIDE
    low = jnp.dot(first[:, 0:E], u_full[0:E, :], preferred_element_type=f32)
    low = low + jnp.dot(first[:, hot_at:], u_full[hot_at:, :], preferred_element_type=f32)

    pooled[...] = jnp.zeros((WIDE, B), f32)

    def await_reply(m):
        pltpu.make_async_remote_copy(
            src_ref=back.at[m],
            dst_ref=replies.at[m],
            send_sem=rep_send.at[m],
            recv_sem=rep_recv.at[m],
            device_id=member_dev(m, z),
            device_id_type=MESH,
        ).wait_recv()

    def pool_pair(p, carry):
        a, b = peer(2 * p, y, z, rep), peer(2 * p + 1, y, z, rep)

        @pl.when(p != PAIR_SELF)
        def _():
            await_reply(a)

        await_reply(b)
        got_a = jnp.dot(replies[a], picks[a], preferred_element_type=f32)
        got_b = jnp.dot(replies[b], picks[b], preferred_element_type=f32)
        tab_a, tab_b = tab[pl.ds(a, 1), :], tab[pl.ds(b, 1), :]
        for t in range(NCOLD):
            more = jnp.where(tab_a == float(t), got_a, 0.0) + jnp.where(
                tab_b == float(t), got_b, 0.0
            )
            pooled[t * E : (t + 1) * E, :] += more
        return carry

    lax.fori_loop(0, GROUP // 2, pool_pair, 0)
    for t in range(NCOLD):
        first[:, E + t * E : E + (t + 1) * E] = pooled[t * E : (t + 1) * E, :].T.astype(bf16)

    low = low + jnp.dot(first[:, E:hot_at], u_full[E:hot_at, :], preferred_element_type=f32)
    low_half = low.astype(bf16)
    low_t[...] = low.T.astype(bf16)

    def cols(i, width):
        return pl.ds(pl.multiple_of(i * width, width), width)

    def forward_cols(i, sums):
        at = cols(i, COLS)
        mixing = jnp.dot(low_half, v_full[:, at], preferred_element_type=f32) + bias_ref[:, at]
        wide = first[:, at].astype(f32)
        crossed = (wide * mixing + wide) * head_ref[:, at]
        mixed[:, at] = mixing
        for q in range(COLS // E):
            sums = sums + crossed[:, q * E : (q + 1) * E]
        return sums

    sums = lax.fori_loop(0, CROSS // COLS, forward_cols, jnp.zeros((B, E), f32))
    logit = jnp.sum(sums, axis=1, keepdims=True)
    dlogit = jax.nn.sigmoid(logit) - label_ref[...].astype(f32)

    dlow[...] = jnp.zeros((B, RANK), f32)

    def backward_cols(i, carry):
        at = cols(i, COLS)
        dmix = (dlogit * head_ref[:, at] * first[:, at].astype(f32)).astype(bf16)
        dlow[...] += lax.dot_general(dmix, v_full[:, at], NT, preferred_element_type=f32)
        grads[:, at] = jnp.dot(low_t[...], dmix, preferred_element_type=f32).astype(bf16)
        return carry

    lax.fori_loop(0, CROSS // COLS, backward_cols, 0)
    dlow_half = dlow[...].astype(bf16)
    for t in range(NCOLD):
        lo, hi = E + t * E, E + (t + 1) * E
        direct = dlogit * head_ref[:, lo:hi] * (mixed[:, lo:hi] + 1.0)
        through = lax.dot_general(u_full[lo:hi, :], dlow_half, NT, preferred_element_type=f32)
        dpool[t * E : (t + 1) * E, :] = (direct.T + through).astype(bf16).astype(f32)

    def v_rows(r):
        return pl.ds(pl.multiple_of(r * V_ROWS, V_ROWS), V_ROWS)

    core_copies = []
    for k in range(4):
        copy = pltpu.make_async_remote_copy(
            src_ref=grads.at[v_rows(2 * k + other_c), :],
            dst_ref=core_in.at[k],
            send_sem=core_send.at[k],
            recv_sem=core_recv.at[k],
            device_id=dev(y, z, sibling),
            device_id_type=MESH,
        )
        copy.start()
        core_copies.append(copy)

    def out_copy(m):
        return pltpu.make_async_remote_copy(
            src_ref=out.at[m],
            dst_ref=arrived.at[me],
            send_sem=out_send.at[m],
            recv_sem=out_recv.at[me],
            device_id=member_dev(m, z),
            device_id_type=MESH,
        )

    def pack(m):
        which = tab[pl.ds(m, 1), :]
        chosen = dpool[0:E, :]
        for t in range(1, NCOLD):
            chosen = jnp.where(which == float(t), dpool[t * E : (t + 1) * E, :], chosen)
        out[m] = lax.dot_general(
            chosen.astype(bf16), picks[m], NT, preferred_element_type=f32
        ).astype(bf16)

    def pack_pair(p, carry):
        a, b = peer(2 * p, y, z, rep), peer(2 * p + 1, y, z, rep)
        pack(a)
        pack(b)

        @pl.when(p != PAIR_SELF)
        def _():
            out_copy(a).start()

        @pl.when(p == PAIR_SELF)
        def _():
            arrived[me] = out[me]

        out_copy(b).start()
        return carry

    lax.fori_loop(0, GROUP // 2, pack_pair, 0)

    for k in range(4):
        core_copies[k].wait_recv()
        pair[k] = (
            grads[v_rows(2 * k + c), :].astype(f32) + core_in[k].astype(f32)
        ).astype(bf16)
    x_copies = []
    for k in (2, 1, 3):
        to = (x + k) % 4
        copy = pltpu.make_async_remote_copy(
            src_ref=pair.at[to],
            dst_ref=x_in.at[k],
            send_sem=x_send.at[k],
            recv_sem=x_recv.at[k],
            device_id=dev(y, z, to * 2 + c),
            device_id_type=MESH,
        )
        copy.start()
        x_copies.append(copy)

    acc[...] = jnp.zeros((WIDE, ROWS), f32)

    def await_out(m):
        pltpu.make_async_remote_copy(
            src_ref=out.at[m],
            dst_ref=arrived.at[m],
            send_sem=out_send.at[m],
            recv_sem=out_recv.at[m],
            device_id=member_dev(m, z),
            device_id_type=MESH,
        ).wait_recv()

    def add_pair(p, carry):
        a, b = peer_back(2 * p, y, z, rep), peer_back(2 * p + 1, y, z, rep)

        @pl.when(p != PAIR_SELF)
        def _():
            await_out(a)

        await_out(b)
        code = jnp.concatenate([asked[a][0:1, :], asked[b][0:1, :]], axis=1)
        table = code // ROWS
        came = jnp.concatenate([arrived[a], arrived[b]], axis=1).astype(f32)
        lhs = jnp.concatenate(
            [jnp.where(table == t, came, 0.0).astype(bf16) for t in range(NCOLD)], axis=0
        )
        acc[...] += lax.dot_general(lhs, rows_of(code), NT, preferred_element_type=f32)
        return carry

    lax.fori_loop(0, GROUP // 2, add_pair, 0)

    def sum_copy(j):
        return pltpu.make_async_remote_copy(
            src_ref=part_out.at[j],
            dst_ref=part_in.at[home],
            send_sem=part_send.at[j],
            recv_sem=part_recv.at[home],
            device_id=dev(y, owner_z, j),
            device_id_type=MESH,
        )

    def send_sum(j, carry):
        part_out[j] = acc[pl.ds(pl.multiple_of(j * PART, PART), PART), :].astype(bf16)
        other = jnp.logical_or(owner_z != z, j != rep)

        @pl.when(other)
        def _():
            sum_copy(j).start()

        @pl.when(jnp.logical_not(other))
        def _():
            part_in[home] = part_out[j]

        return carry

    lax.fori_loop(0, 8, send_sum, 0)

    for copy in x_copies:
        copy.wait_recv()
    mine[...] = (
        pair[x].astype(f32) + x_in[1].astype(f32) + x_in[2].astype(f32) + x_in[3].astype(f32)
    )

    def band(j):
        return pl.ds(pl.multiple_of(j * 8, 8), 8)

    y_copies = []
    for k in (2, 1, 3):
        to = (y + k) % 4
        copy = pltpu.make_async_remote_copy(
            src_ref=mine.at[band(to), :],
            dst_ref=y_in.at[k],
            send_sem=y_send.at[k],
            recv_sem=y_recv.at[k],
            device_id=dev(to, z, rep),
            device_id_type=MESH,
        )
        copy.start()
        y_copies.append(copy)
    for copy in y_copies:
        copy.wait_recv()
    column[:, CROSS:] = jnp.zeros((8, PADDED - CROSS), f32)
    column[:, :CROSS] = mine[band(y), :] + y_in[1] + y_in[2] + y_in[3]

    def z_copy(k):
        to = (z + k) % 16
        return pltpu.make_async_remote_copy(
            src_ref=column.at[:, cols(to, VCOLS)],
            dst_ref=z_in.at[k],
            send_sem=z_send.at[k],
            recv_sem=z_recv.at[k],
            device_id=dev(y, to, rep),
            device_id_type=MESH,
        )

    def z_start(k, carry):
        @pl.when((z + k) % 16 < VCHUNKS)
        def _():
            z_copy(k).start()

        return carry

    lax.fori_loop(1, 16, z_start, 0)

    def await_sum(j, carry):
        sz = holder(j)

        @pl.when(jnp.logical_or(sz != z, home != rep))
        def _():
            pltpu.make_async_remote_copy(
                src_ref=part_out.at[0],
                dst_ref=part_in.at[sz // 2],
                send_sem=part_send.at[0],
                recv_sem=part_recv.at[sz // 2],
                device_id=dev(y, sz, home),
                device_id_type=MESH,
            ).wait_recv()

        return carry

    lax.fori_loop(0, 8, await_sum, 0)
    total = part_in[0].astype(f32)
    for g in range(1, 8):
        total = total + part_in[g].astype(f32)
    whole[rep] = total.astype(bf16)

    def all_copy(j):
        return pltpu.make_async_remote_copy(
            src_ref=whole.at[rep],
            dst_ref=whole.at[rep],
            send_sem=all_send.at[j],
            recv_sem=all_recv.at[rep],
            device_id=dev(y, z, (rep + j) % 8),
            device_id_type=MESH,
        )

    def send_all(j, carry):
        all_copy(j).start()
        return carry

    lax.fori_loop(1, 8, send_all, 0)

    def zb_copy(k):
        return pltpu.make_async_remote_copy(
            src_ref=strip.at[:, cols(z, VCOLS)],
            dst_ref=strip.at[:, cols(z, VCOLS)],
            send_sem=zb_send.at[k],
            recv_sem=zb_recv.at[z],
            device_id=dev(y, (z + k) % 16, rep),
            device_id_type=MESH,
        )

    @pl.when(z < VCHUNKS)
    def _():
        def z_wait(k, carry):
            pltpu.make_async_remote_copy(
                src_ref=z_in.at[k],
                dst_ref=z_in.at[k],
                send_sem=z_send.at[k],
                recv_sem=z_recv.at[k],
                device_id=dev(y, (z + 16 - k) % 16, rep),
                device_id_type=MESH,
            ).wait_recv()
            return carry

        lax.fori_loop(1, 16, z_wait, 0)
        summed = column[:, cols(z, VCOLS)]
        for k in range(1, 16):
            summed = summed + z_in[k]
        strip[:, cols(z, VCOLS)] = summed

        def zb_start(k, carry):
            zb_copy(k).start()
            return carry

        lax.fori_loop(1, 16, zb_start, 0)

    def zb_wait(k, carry):
        other = (z + 16 - k) % 16

        @pl.when(other < VCHUNKS)
        def _():
            pltpu.make_async_remote_copy(
                src_ref=strip.at[:, cols(other, VCOLS)],
                dst_ref=strip.at[:, cols(other, VCOLS)],
                send_sem=zb_send.at[k],
                recv_sem=zb_recv.at[other],
                device_id=dev(y, other, rep),
                device_id_type=MESH,
            ).wait_recv()

        return carry

    lax.fori_loop(1, 16, zb_wait, 0)

    total_ref[band(y), :] = strip[:, :CROSS]
    yb_copies = []
    for k in (2, 1, 3):
        copy = pltpu.make_async_remote_copy(
            src_ref=total_ref.at[band(y), :],
            dst_ref=total_ref.at[band(y), :],
            send_sem=yb_send.at[k],
            recv_sem=yb_recv.at[k],
            device_id=dev((y + k) % 4, z, rep),
            device_id_type=MESH,
        )
        copy.start()
        yb_copies.append(copy)

    def await_all(j, carry):
        other = (rep + 8 - j) % 8
        pltpu.make_async_remote_copy(
            src_ref=whole.at[other],
            dst_ref=whole.at[other],
            send_sem=all_send.at[j],
            recv_sem=all_recv.at[other],
            device_id=dev(y, z, other),
            device_id_type=MESH,
        ).wait_recv()
        return carry

    lax.fori_loop(1, 8, await_all, 0)
    grad_ref[...] = whole[...].astype(f32)
    for k in (2, 1, 3):
        came = band((y + 4 - k) % 4)
        pltpu.make_async_remote_copy(
            src_ref=total_ref.at[came, :],
            dst_ref=total_ref.at[came, :],
            send_sem=yb_send.at[k],
            recv_sem=yb_recv.at[k],
            device_id=dev((y + 4 - k) % 4, z, rep),
            device_id_type=MESH,
        ).wait_recv()

    for copy in w_copies + wc_copies + core_copies + x_copies + y_copies + yb_copies:
        copy.wait_send()

    def drain(i):
        m = peer(i, y, z, rep)
        ask_copy(m).wait_send()
        reply_copy(m).wait_send()
        out_copy(m).wait_send()

    others(GROUP, drain)

    def drain_parts(j, carry):
        @pl.when(jnp.logical_or(holder(j) != z, home != rep))
        def _():
            part_copy(j).wait_send()

        @pl.when(jnp.logical_or(owner_z != z, j != rep))
        def _():
            sum_copy(j).wait_send()

        return carry

    lax.fori_loop(0, 8, drain_parts, 0)

    def drain_all(j, carry):
        all_copy(j).wait_send()
        return carry

    lax.fori_loop(1, 8, drain_all, 0)

    def drain_z(k, carry):
        @pl.when((z + k) % 16 < VCHUNKS)
        def _():
            z_copy(k).wait_send()

        @pl.when(z < VCHUNKS)
        def _():
            zb_copy(k).wait_send()

        return carry

    lax.fori_loop(1, 16, drain_z, 0)


def vmem():
    return pl.BlockSpec(memory_space=pltpu.VMEM)


def dma(n):
    return pltpu.SemaphoreType.DMA((n,))


def step_call(*args):
    return pl.pallas_call(
        step_kernel,
        out_shape=(
            jax.ShapeDtypeStruct((8, PART, ROWS), f32),
            jax.ShapeDtypeStruct((V_ROWS, CROSS), f32),
        ),
        in_specs=[vmem()] * 11,
        out_specs=(vmem(), vmem()),
        scratch_shapes=[
            pltpu.VMEM((8, PART, ROWS), bf16),
            pltpu.VMEM((GROUP, E, SLOTS), bf16),
            pltpu.VMEM((GROUP, E, SLOTS), bf16),
            pltpu.VMEM((GROUP, 8, SLOTS), i32),
            pltpu.VMEM((GROUP, 8, SLOTS), i32),
            pltpu.VMEM((GROUP, B), f32),
            pltpu.VMEM((GROUP, B), f32),
            pltpu.VMEM((GROUP, B), f32),
            pltpu.VMEM((GROUP, SLOTS, B), bf16),
            pltpu.VMEM((WIDE, B), f32),
            pltpu.VMEM((CROSS, RANK), bf16),
            pltpu.VMEM((RANK, CROSS), bf16),
            pltpu.VMEM((B, CROSS), bf16),
            pltpu.VMEM((B, CROSS), f32),
            pltpu.VMEM((RANK, B), bf16),
            pltpu.VMEM((B, RANK), f32),
            pltpu.VMEM((WIDE, B), f32),
            pltpu.VMEM((RANK, CROSS), bf16),
            pltpu.VMEM((GROUP, E, SLOTS), bf16),
            pltpu.VMEM((GROUP, E, SLOTS), bf16),
            pltpu.VMEM((WIDE, ROWS), f32),
            pltpu.VMEM((8, PART, ROWS), bf16),
            pltpu.VMEM((8, PART, ROWS), bf16),
            pltpu.VMEM((8, PART, ROWS), bf16),
            pltpu.VMEM((4, V_ROWS, CROSS), bf16),
            pltpu.VMEM((4, V_ROWS, CROSS), bf16),
            pltpu.VMEM((4, V_ROWS, CROSS), bf16),
            pltpu.VMEM((V_ROWS, CROSS), f32),
            pltpu.VMEM((4, 8, CROSS), f32),
            pltpu.VMEM((8, PADDED), f32),
            pltpu.VMEM((16, 8, VCOLS), f32),
            pltpu.VMEM((8, PADDED), f32),
            dma(8), dma(8), dma(GROUP), dma(GROUP), dma(GROUP), dma(GROUP), dma(3),
            dma(8), dma(8), dma(8), dma(8),
            dma(GROUP), dma(GROUP), dma(8), dma(8), dma(8), dma(8),
            dma(4), dma(4), dma(4), dma(4), dma(4), dma(4),
            dma(16), dma(16), dma(16), dma(16), dma(4), dma(4),
        ],
        compiler_params=pltpu.CompilerParams(
            collective_id=0, has_side_effects=True, vmem_limit_bytes=56 << 20
        ),
    )(*args)


def body(
    bottom,
    hot_ids,
    hot_tables,
    cold_owner,
    cold_row,
    cold_rows,
    cold_acc,
    u_weight,
    v_weight,
    v_acc,
    cross_bias,
    head,
    labels,
):
    rep = lax.axis_index("replica")
    turned = cold_rows.reshape(NCOLD, ROWS, E).transpose(0, 2, 1).reshape(8, PART, ROWS)
    part = lax.dynamic_index_in_dim(turned, rep, 0, keepdims=False).astype(bf16)
    grad_rows, grad_mine = step_call(
        cold_owner.T, cold_row.T, part, bottom, hot_ids, hot_tables, u_weight,
        v_weight.astype(bf16), cross_bias[None, :], head[None, :], labels[:, None],
    )
    grad_rows = grad_rows.reshape(NCOLD, E, ROWS).transpose(0, 2, 1).reshape(NCOLD * ROWS, E)
    new_cold_acc = cold_acc + jnp.mean(grad_rows * grad_rows, axis=1)
    new_cold_rows = cold_rows - row_rate * grad_rows / (jnp.sqrt(new_cold_acc)[:, None] + eps_value)
    acc_dense = v_acc + jnp.mean(grad_mine * grad_mine, axis=1)
    new_v = v_weight - dense_rate * grad_mine / (jnp.sqrt(acc_dense)[:, None] + eps_value)
    return (new_cold_rows, new_cold_acc, new_v)


def solution(mesh):
    return jax.shard_map(
        body,
        mesh=mesh,
        in_specs=(
            P(("table", "replica"), None),
            P(("table", "replica"), None),
            P(),
            P(("table", "replica"), None),
            P(("table", "replica"), None),
            P("table", None),
            P("table"),
            P("replica", None),
            P("replica", None),
            P("replica"),
            P(),
            P(),
            P(("table", "replica")),
        ),
        out_specs=(P("table", None), P("table"), P("replica", None)),
        check_vma=False,
    )
```

```python
import functools
import jax
import jax.numpy as jnp
from jax import lax
from jax.experimental import pallas as pl
from jax.experimental.pallas import tpu as pltpu
from jax.sharding import PartitionSpec as P

NCOLD = 6
LOOK = 2
NHOT = 20
LOOKUPS = NCOLD * LOOK
E = 128
B = 256
ROWS = 256
SLOTS = 128
GROUP = 64
ITSELF = 40
PAIR_SELF = ITSELF // 2
WIDE = NCOLD * E
PART = WIDE // 8
CROSS = 3456
PADDED = 3584
COLS = 384
U_ROWS = 432
V_ROWS = 32
RANK = 256
VCHUNKS = 14
VCOLS = 256
MESH = pl.DeviceIdType.MESH

row_rate = 0.1
dense_rate = 0.05
eps_value = 1e-08

f32 = jnp.float32
bf16 = jnp.bfloat16
i32 = jnp.int32
NT = (((1,), (1,)), ((), ()))


def place_of():
    table, rep = lax.axis_index("table"), lax.axis_index("replica")
    return table >> 4, table & 15, rep


def dev(y, z, rep):
    return {"table": y * 16 + z, "replica": rep}


def held_z(z, rep):
    return 2 * ((((rep & 1) << 2) + (rep >> 1) - (z >> 1)) & 7) + (z & 1)


def holding_rep(z, owner_z):
    at = ((owner_z >> 1) + (z >> 1)) & 7
    return ((at & 3) << 1) + (at >> 2)


def member_of(y, z, rep):
    return y * 16 + held_z(z, rep)


def member_dev(member, z):
    mz = (z - (z & 1)) + (member & 1)
    return dev(member >> 4, mz, holding_rep(mz, member & 15))


def peer(i, y, z, rep):
    px = ((rep >> 1) + 2 + (i >> 2)) & 3
    pc = (rep + (i >> 1)) & 1
    pz = (z - (z & 1)) + ((z + i) & 1)
    return member_of((y + 2 + (i >> 4)) & 3, pz, px * 2 + pc)


def peer_back(i, y, z, rep):
    px = ((rep >> 1) + 6 - ((i >> 2) & 3)) & 3
    pc = (rep + (i >> 1)) & 1
    pz = (z - (z & 1)) + ((z + i) & 1)
    return member_of((y + 6 - (i >> 4)) & 3, pz, px * 2 + pc)


def tables(owner_ref, row_ref, pos, tab, rows):
    owners = lax.broadcasted_iota(i32, (GROUP, B), 0)
    named = jnp.zeros((GROUP, B), f32)
    table = jnp.zeros((GROUP, B), f32)
    row = jnp.zeros((GROUP, B), f32)
    for k in range(LOOKUPS):
        hit = owners == owner_ref[k : k + 1, :]
        named = jnp.where(hit, 1.0, named)
        table = jnp.where(hit, float(k // LOOK), table)
        row = jnp.where(hit, row_ref[k : k + 1, :].astype(f32), row)
    before = jnp.where(
        lax.broadcasted_iota(i32, (B, B), 0) < lax.broadcasted_iota(i32, (B, B), 1), 1.0, 0.0
    ).astype(bf16)
    place = jnp.dot(named.astype(bf16), before, preferred_element_type=f32)
    pos[...] = jnp.where(named > 0.0, place, -1.0)
    tab[...] = table
    rows[...] = row


def slots_of(pos, o):
    lines = lax.broadcasted_iota(i32, (SLOTS, B), 0).astype(f32)
    return jnp.where(lines == pos[pl.ds(o, 1), :], 1.0, 0.0).astype(bf16)


def rows_of(code):
    lines = lax.broadcasted_iota(i32, (ROWS, code.shape[1]), 0)
    return jnp.where(lines == code & (ROWS - 1), 1.0, 0.0).astype(bf16)


def others(count, act):
    def step(i, carry):
        @pl.when(i != ITSELF)
        def _():
            act(i)

        return carry

    lax.fori_loop(0, count, step, 0)


def step_kernel(
    owner_ref, row_ref, part_ref, bottom_ref, ids_ref, hot_hbm, u_ref, v_wide, bias_ref, head_ref, label_ref,
    grad_ref, total_ref,
    hot_ref, v_ref, held, replies, back, ask, asked, pos, tab, rows, picks, pooled,
    u_full, v_full, first, mixed, low_t, dlow, dpool, grads,
    arrived, out, acc, part_out, part_in, whole,
    core_in, pair, x_in, mine, y_in, column, z_in, strip,
    held_send, held_recv, ask_send, ask_recv, rep_send, rep_recv, own_sem,
    w_send, w_recv, wc_send, wc_recv,
    out_send, out_recv, part_send, part_recv, all_send, all_recv,
    core_send, core_recv, x_send, x_recv, y_send, y_recv, z_send, z_recv, zb_send, zb_recv, yb_send, yb_recv,
):
    y, z, rep = place_of()
    x, c = rep >> 1, rep & 1
    other_c = 1 - c
    sibling = x * 2 + other_c
    me = member_of(y, z, rep)
    group = z >> 1
    owner_z = held_z(z, rep)
    self_holder = owner_z == z

    hot_copy = pltpu.make_async_copy(hot_hbm, hot_ref, own_sem.at[3])
    hot_copy.start()

    bar = pltpu.get_barrier_semaphore()

    def signal(y_, z_, rep_):
        pl.semaphore_signal(bar, inc=1, device_id=dev(y_, z_, rep_), device_id_type=MESH)

    def greet_member(i):
        pl.semaphore_signal(
            bar, inc=1, device_id=member_dev(peer(i, y, z, rep), z), device_id_type=MESH
        )

    others(GROUP, greet_member)

    def holder(j):
        hz = (z + 2 * j) & 15
        return hz, holding_rep(hz, z)

    def is_other(at):
        return jnp.logical_or(at[0] != z, at[1] != rep)

    def source(j):
        return owner_z, (rep + j) & 7

    def greet_parts(j, carry):
        @pl.when(is_other(holder(j)))
        def _():
            signal(y, *holder(j))

        @pl.when(is_other(source(j)))
        def _():
            signal(y, *source(j))

        return carry

    lax.fori_loop(0, 8, greet_parts, 0)

    def greet_z(k, carry):
        signal(y, (z + k) & 15, rep)
        return carry

    lax.fori_loop(1, 16, greet_z, 0)
    v_ref[...] = v_wide[...].astype(bf16)
    tables(owner_ref, row_ref, pos, tab, rows)
    pl.semaphore_wait(bar, GROUP - 1 + 16 - jnp.where(self_holder, 2, 0).astype(i32) + 15)

    def part_copy(j):
        return pltpu.make_async_remote_copy(
            src_ref=part_ref,
            dst_ref=held.at[rep],
            send_sem=held_send.at[j],
            recv_sem=held_recv.at[rep],
            device_id=dev(y, *holder(j)),
            device_id_type=MESH,
        )

    def send_part(j, carry):
        @pl.when(is_other(holder(j)))
        def _():
            part_copy(j).start()

        return carry

    lax.fori_loop(0, 8, send_part, 0)
    own = pltpu.make_async_copy(part_ref, held.at[rep], own_sem.at[0])

    @pl.when(self_holder)
    def _():
        own.start()

    def u_at(r):
        return u_full.at[pl.ds(pl.multiple_of(r * U_ROWS, 16), U_ROWS), :]

    def v_at(r):
        return v_full.at[pl.ds(pl.multiple_of(r * V_ROWS, 16), V_ROWS), :]

    def weight_copies(src_u, src_v, r, sends, recvs, slot, y_, z_, rep_):
        return [
            pltpu.make_async_remote_copy(
                src_ref=src,
                dst_ref=dst,
                send_sem=sends.at[2 * slot + i],
                recv_sem=recvs.at[2 * slot + i],
                device_id=dev(y_, z_, rep_),
                device_id_type=MESH,
            )
            for i, (src, dst) in enumerate([(src_u, u_at(r)), (src_v, v_at(r))])
        ]

    w_copies = []
    for k in (2, 1, 3):
        to = ((x + k) & 3) * 2 + c
        w_copies += weight_copies(u_ref, v_ref, rep, w_send, w_recv, k, y, z, to)
    w_copies += weight_copies(u_ref, v_ref, rep, w_send, w_recv, 0, y, z, sibling)
    for copy in w_copies:
        copy.start()
    own_u = pltpu.make_async_copy(u_ref, u_at(rep), own_sem.at[1])
    own_v = pltpu.make_async_copy(v_ref, v_at(rep), own_sem.at[2])
    own_u.start()
    own_v.start()

    lines16 = lax.broadcasted_iota(i32, (16, B), 0)

    def ask_copy(m):
        return pltpu.make_async_remote_copy(
            src_ref=ask.at[m],
            dst_ref=asked.at[me],
            send_sem=ask_send.at[m],
            recv_sem=ask_recv.at[me],
            device_id=member_dev(m, z),
            device_id_type=MESH,
        )

    def ask_pair(p, carry):
        a, b = peer(2 * p, y, z, rep), peer(2 * p + 1, y, z, rep)
        pick_a, pick_b = slots_of(pos, a), slots_of(pos, b)
        picks[a] = pick_a
        picks[b] = pick_b
        lhs = jnp.where(lines16 == 0, rows[pl.ds(a, 1), :], 0.0)
        lhs = jnp.where(lines16 == 1, tab[pl.ds(a, 1), :], lhs)
        lhs = jnp.where(lines16 == 2, rows[pl.ds(b, 1), :], lhs)
        lhs = jnp.where(lines16 == 3, tab[pl.ds(b, 1), :], lhs).astype(bf16)
        got = lax.dot_general(
            lhs, jnp.concatenate([pick_a, pick_b], axis=0), NT, preferred_element_type=f32
        )
        code_a = (got[0:1, :SLOTS] + got[1:2, :SLOTS] * float(ROWS)).astype(i32)
        code_b = (got[2:3, SLOTS:] + got[3:4, SLOTS:] * float(ROWS)).astype(i32)
        ask[a] = jnp.broadcast_to(code_a, (8, SLOTS))
        ask[b] = jnp.broadcast_to(code_b, (8, SLOTS))

        @pl.when(p != PAIR_SELF)
        def _():
            ask_copy(a).start()

        @pl.when(p == PAIR_SELF)
        def _():
            asked[me] = ask[me]

        ask_copy(b).start()
        return carry

    lax.fori_loop(0, GROUP // 2, ask_pair, 0)

    first[:, 0:E] = bottom_ref[...]
    hot_copy.wait()
    ids = ids_ref[...].astype(f32).T
    lanes = lax.broadcasted_iota(i32, (B, E), 1).astype(f32)
    for j in range(NHOT):
        one = jnp.where(lanes == ids[:, j : j + 1], 1.0, 0.0).astype(bf16)
        at = E + WIDE + j * E
        first[:, at : at + E] = jnp.dot(one, hot_ref[j], preferred_element_type=f32).astype(bf16)

    wc_copies = []
    for k in (1, 3, 2):
        came = ((x + 4 - k) & 3) * 2 + c
        for copy in weight_copies(u_at(came), v_at(came), came, w_send, w_recv, k, y, z, came):
            copy.wait_recv()
        forward = weight_copies(u_at(came), v_at(came), came, wc_send, wc_recv, k, y, z, sibling)
        for copy in forward:
            copy.start()
        wc_copies += forward

    def await_part(j, carry):
        sz, srep = source(j)

        @pl.when(is_other((sz, srep)))
        def _():
            pltpu.make_async_remote_copy(
                src_ref=part_ref,
                dst_ref=held.at[srep],
                send_sem=held_send.at[0],
                recv_sem=held_recv.at[srep],
                device_id=dev(y, sz, srep),
                device_id_type=MESH,
            ).wait_recv()

        return carry

    lax.fori_loop(0, 8, await_part, 0)

    @pl.when(self_holder)
    def _():
        own.wait()

    def reply_copy(m):
        return pltpu.make_async_remote_copy(
            src_ref=back.at[m],
            dst_ref=replies.at[me],
            send_sem=rep_send.at[m],
            recv_sem=rep_recv.at[me],
            device_id=member_dev(m, z),
            device_id_type=MESH,
        )

    def await_ask(m):
        pltpu.make_async_remote_copy(
            src_ref=ask.at[m],
            dst_ref=asked.at[m],
            send_sem=ask_send.at[m],
            recv_sem=ask_recv.at[m],
            device_id=member_dev(m, z),
            device_id_type=MESH,
        ).wait_recv()

    def reply_pair(p, carry):
        a, b = peer_back(2 * p, y, z, rep), peer_back(2 * p + 1, y, z, rep)

        @pl.when(p != PAIR_SELF)
        def _():
            await_ask(a)

        await_ask(b)
        code = jnp.concatenate([asked[a][0:1, :], asked[b][0:1, :]], axis=1)
        table = code >> 8
        found = jnp.dot(
            held[...].reshape(WIDE, ROWS), rows_of(code), preferred_element_type=f32
        )
        got = found[0:E]
        for t in range(1, NCOLD):
            got = jnp.where(table == t, found[t * E : (t + 1) * E], got)
        got = got.astype(bf16)
        back[a] = got[:, :SLOTS]
        back[b] = got[:, SLOTS:]

        @pl.when(p != PAIR_SELF)
        def _():
            reply_copy(a).start()

        @pl.when(p == PAIR_SELF)
        def _():
            replies[me] = back[me]

        reply_copy(b).start()
        return carry

    lax.fori_loop(0, GROUP // 2, reply_pair, 0)

    for k in range(4):
        came = ((x + 4 - k) & 3) * 2 + other_c
        sends, recvs = (w_send, w_recv) if k == 0 else (wc_send, wc_recv)
        for copy in weight_copies(u_at(came), v_at(came), came, sends, recvs, k, y, z, sibling):
            copy.wait_recv()
    own_u.wait()
    own_v.wait()
    hot_at = E + WIDE
    low = jnp.dot(first[:, 0:E], u_full[0:E, :], preferred_element_type=f32)
    low = low + jnp.dot(first[:, hot_at:], u_full[hot_at:, :], preferred_element_type=f32)

    pooled[...] = jnp.zeros((WIDE, B), f32)

    def await_reply(m):
        pltpu.make_async_remote_copy(
            src_ref=back.at[m],
            dst_ref=replies.at[m],
            send_sem=rep_send.at[m],
            recv_sem=rep_recv.at[m],
            device_id=member_dev(m, z),
            device_id_type=MESH,
        ).wait_recv()

    def pool_pair(p, carry):
        a, b = peer(2 * p, y, z, rep), peer(2 * p + 1, y, z, rep)

        @pl.when(p != PAIR_SELF)
        def _():
            await_reply(a)

        await_reply(b)
        got_a = jnp.dot(replies[a], picks[a], preferred_element_type=f32)
        got_b = jnp.dot(replies[b], picks[b], preferred_element_type=f32)
        tab_a, tab_b = tab[pl.ds(a, 1), :], tab[pl.ds(b, 1), :]
        for t in range(NCOLD):
            more = jnp.where(tab_a == float(t), got_a, 0.0) + jnp.where(
                tab_b == float(t), got_b, 0.0
            )
            pooled[t * E : (t + 1) * E, :] += more
        return carry

    lax.fori_loop(0, GROUP // 2, pool_pair, 0)
    for t in range(NCOLD):
        first[:, E + t * E : E + (t + 1) * E] = pooled[t * E : (t + 1) * E, :].T.astype(bf16)

    low = low + jnp.dot(first[:, E:hot_at], u_full[E:hot_at, :], preferred_element_type=f32)
    low_half = low.astype(bf16)
    low_t[...] = low.T.astype(bf16)

    def cols(i, width):
        return pl.ds(pl.multiple_of(i * width, width), width)

    def line(ref, i):
        n = COLS // E
        return jnp.concatenate([ref[pl.ds(i * n + q, 1), :] for q in range(n)], axis=1)

    def forward_cols(i, sums):
        at = cols(i, COLS)
        mixing = jnp.dot(low_half, v_full[:, at], preferred_element_type=f32) + line(bias_ref, i)
        wide = first[:, at].astype(f32)
        crossed = (wide * mixing + wide) * line(head_ref, i)
        mixed[:, at] = mixing
        for q in range(COLS // E):
            sums = sums + crossed[:, q * E : (q + 1) * E]
        return sums

    sums = lax.fori_loop(0, CROSS // COLS, forward_cols, jnp.zeros((B, E), f32))
    logit = jnp.sum(sums, axis=1, keepdims=True)
    label = jnp.concatenate([label_ref[0:1, :], label_ref[1:2, :]], axis=1).astype(f32)
    label = jnp.broadcast_to(label, (8, B)).T
    dlogit = jax.nn.sigmoid(logit) - label[:, 0:1]

    dlow[...] = jnp.zeros((B, RANK), f32)

    def backward_cols(i, carry):
        at = cols(i, COLS)
        dmix = (dlogit * line(head_ref, i) * first[:, at].astype(f32)).astype(bf16)
        dlow[...] += lax.dot_general(dmix, v_full[:, at], NT, preferred_element_type=f32)
        grads[:, at] = jnp.dot(low_t[...], dmix, preferred_element_type=f32).astype(bf16)
        return carry

    lax.fori_loop(0, CROSS // COLS, backward_cols, 0)
    dlow_half = dlow[...].astype(bf16)
    for t in range(NCOLD):
        lo, hi = E + t * E, E + (t + 1) * E
        direct = dlogit * head_ref[t + 1 : t + 2, :] * (mixed[:, lo:hi] + 1.0)
        through = lax.dot_general(u_full[lo:hi, :], dlow_half, NT, preferred_element_type=f32)
        dpool[t * E : (t + 1) * E, :] = (direct.T + through).astype(bf16).astype(f32)

    def v_rows(r):
        return pl.ds(pl.multiple_of(r * V_ROWS, V_ROWS), V_ROWS)

    core_copies = []
    for k in range(4):
        copy = pltpu.make_async_remote_copy(
            src_ref=grads.at[v_rows(2 * k + other_c), :],
            dst_ref=core_in.at[k],
            send_sem=core_send.at[k],
            recv_sem=core_recv.at[k],
            device_id=dev(y, z, sibling),
            device_id_type=MESH,
        )
        copy.start()
        core_copies.append(copy)

    def out_copy(m):
        return pltpu.make_async_remote_copy(
            src_ref=out.at[m],
            dst_ref=arrived.at[me],
            send_sem=out_send.at[m],
            recv_sem=out_recv.at[me],
            device_id=member_dev(m, z),
            device_id_type=MESH,
        )

    def pack(m):
        which = tab[pl.ds(m, 1), :]
        chosen = dpool[0:E, :]
        for t in range(1, NCOLD):
            chosen = jnp.where(which == float(t), dpool[t * E : (t + 1) * E, :], chosen)
        out[m] = lax.dot_general(
            chosen.astype(bf16), picks[m], NT, preferred_element_type=f32
        ).astype(bf16)

    def pack_pair(p, carry):
        a, b = peer(2 * p, y, z, rep), peer(2 * p + 1, y, z, rep)
        pack(a)
        pack(b)

        @pl.when(p != PAIR_SELF)
        def _():
            out_copy(a).start()

        @pl.when(p == PAIR_SELF)
        def _():
            arrived[me] = out[me]

        out_copy(b).start()
        return carry

    lax.fori_loop(0, 16, pack_pair, 0)

    for k in range(4):
        core_copies[k].wait_recv()
        pair[k] = (
            grads[v_rows(2 * k + c), :].astype(f32) + core_in[k].astype(f32)
        ).astype(bf16)
    x_copies = []
    for k in (2, 1, 3):
        to = (x + k) & 3
        copy = pltpu.make_async_remote_copy(
            src_ref=pair.at[to],
            dst_ref=x_in.at[k],
            send_sem=x_send.at[k],
            recv_sem=x_recv.at[k],
            device_id=dev(y, z, to * 2 + c),
            device_id_type=MESH,
        )
        copy.start()
        x_copies.append(copy)

    lax.fori_loop(16, 32, pack_pair, 0)


    acc[...] = jnp.zeros((WIDE, ROWS), f32)

    def await_out(m):
        pltpu.make_async_remote_copy(
            src_ref=out.at[m],
            dst_ref=arrived.at[m],
            send_sem=out_send.at[m],
            recv_sem=out_recv.at[m],
            device_id=member_dev(m, z),
            device_id_type=MESH,
        ).wait_recv()

    def add_pair(p, carry):
        a, b = peer_back(2 * p, y, z, rep), peer_back(2 * p + 1, y, z, rep)

        @pl.when(p != PAIR_SELF)
        def _():
            await_out(a)

        await_out(b)
        code = jnp.concatenate([asked[a][0:1, :], asked[b][0:1, :]], axis=1)
        table = code >> 8
        came = jnp.concatenate([arrived[a], arrived[b]], axis=1).astype(f32)
        lhs = jnp.concatenate(
            [jnp.where(table == t, came, 0.0).astype(bf16) for t in range(NCOLD)], axis=0
        )
        acc[...] += lax.dot_general(lhs, rows_of(code), NT, preferred_element_type=f32)
        return carry

    lax.fori_loop(0, 12, add_pair, 0)

    for copy in x_copies:
        copy.wait_recv()
    mine[...] = (
        pair[x].astype(f32) + x_in[1].astype(f32) + x_in[2].astype(f32) + x_in[3].astype(f32)
    )

    def band(j):
        return pl.ds(pl.multiple_of(j * 8, 8), 8)

    y_copies = []
    for k in (2, 1, 3):
        to = (y + k) & 3
        copy = pltpu.make_async_remote_copy(
            src_ref=mine.at[band(to), :],
            dst_ref=y_in.at[k],
            send_sem=y_send.at[k],
            recv_sem=y_recv.at[k],
            device_id=dev(to, z, rep),
            device_id_type=MESH,
        )
        copy.start()
        y_copies.append(copy)
    lax.fori_loop(12, 20, add_pair, 0)
    for copy in y_copies:
        copy.wait_recv()
    column[:, CROSS:] = jnp.zeros((8, PADDED - CROSS), f32)
    column[:, :CROSS] = mine[band(y), :] + y_in[1] + y_in[2] + y_in[3]

    def z_copy(k):
        to = (z + k) & 15
        return pltpu.make_async_remote_copy(
            src_ref=column.at[:, cols(to, VCOLS)],
            dst_ref=z_in.at[k],
            send_sem=z_send.at[k],
            recv_sem=z_recv.at[k],
            device_id=dev(y, to, rep),
            device_id_type=MESH,
        )

    def z_start(k, carry):
        @pl.when((z + k) & 15 < VCHUNKS)
        def _():
            z_copy(k).start()

        return carry

    lax.fori_loop(1, 16, z_start, 0)

    lax.fori_loop(20, 28, add_pair, 0)

    def zb_copy(k):
        return pltpu.make_async_remote_copy(
            src_ref=strip.at[:, cols(z, VCOLS)],
            dst_ref=strip.at[:, cols(z, VCOLS)],
            send_sem=zb_send.at[k],
            recv_sem=zb_recv.at[z],
            device_id=dev(y, (z + k) & 15, rep),
            device_id_type=MESH,
        )

    @pl.when(z < VCHUNKS)
    def _():
        def z_wait(k, carry):
            pltpu.make_async_remote_copy(
                src_ref=z_in.at[k],
                dst_ref=z_in.at[k],
                send_sem=z_send.at[k],
                recv_sem=z_recv.at[k],
                device_id=dev(y, (z + 16 - k) & 15, rep),
                device_id_type=MESH,
            ).wait_recv()
            return carry

        lax.fori_loop(1, 16, z_wait, 0)
        summed = column[:, cols(z, VCOLS)]
        for k in range(1, 16):
            summed = summed + z_in[k]
        strip[:, cols(z, VCOLS)] = summed

        def zb_start(k, carry):
            zb_copy(k).start()
            return carry

        lax.fori_loop(1, 16, zb_start, 0)

    lax.fori_loop(28, 32, add_pair, 0)


    def sum_copy(j):
        return pltpu.make_async_remote_copy(
            src_ref=part_out.at[j],
            dst_ref=part_in.at[group],
            send_sem=part_send.at[j],
            recv_sem=part_recv.at[group],
            device_id=dev(y, owner_z, j),
            device_id_type=MESH,
        )

    def send_sum(j, carry):
        part_out[j] = acc[pl.ds(pl.multiple_of(j * PART, PART), PART), :].astype(bf16)
        other = jnp.logical_or(owner_z != z, j != rep)

        @pl.when(other)
        def _():
            sum_copy(j).start()

        @pl.when(jnp.logical_not(other))
        def _():
            part_in[group] = part_out[j]

        return carry

    lax.fori_loop(0, 8, send_sum, 0)

    def zb_wait(k, carry):
        other = (z + 16 - k) & 15

        @pl.when(other < VCHUNKS)
        def _():
            pltpu.make_async_remote_copy(
                src_ref=strip.at[:, cols(other, VCOLS)],
                dst_ref=strip.at[:, cols(other, VCOLS)],
                send_sem=zb_send.at[k],
                recv_sem=zb_recv.at[other],
                device_id=dev(y, other, rep),
                device_id_type=MESH,
            ).wait_recv()

        return carry

    lax.fori_loop(1, 16, zb_wait, 0)

    total_ref[band(y), :] = strip[:, :CROSS]
    yb_copies = []
    for k in (2, 1, 3):
        copy = pltpu.make_async_remote_copy(
            src_ref=total_ref.at[band(y), :],
            dst_ref=total_ref.at[band(y), :],
            send_sem=yb_send.at[k],
            recv_sem=yb_recv.at[k],
            device_id=dev((y + k) & 3, z, rep),
            device_id_type=MESH,
        )
        copy.start()
        yb_copies.append(copy)

    def drain(i):
        m = peer(i, y, z, rep)
        ask_copy(m).wait_send()
        reply_copy(m).wait_send()
        out_copy(m).wait_send()

    others(GROUP, drain)

    def await_sum(j, carry):
        sz, srep = holder(j)

        @pl.when(is_other((sz, srep)))
        def _():
            pltpu.make_async_remote_copy(
                src_ref=part_out.at[0],
                dst_ref=part_in.at[sz >> 1],
                send_sem=part_send.at[0],
                recv_sem=part_recv.at[sz >> 1],
                device_id=dev(y, sz, srep),
                device_id_type=MESH,
            ).wait_recv()

        return carry

    lax.fori_loop(0, 8, await_sum, 0)
    total = part_in[0].astype(f32)
    for g in range(1, 8):
        total = total + part_in[g].astype(f32)
    whole[rep] = total.astype(bf16)

    def all_copy(j):
        return pltpu.make_async_remote_copy(
            src_ref=whole.at[rep],
            dst_ref=whole.at[rep],
            send_sem=all_send.at[j],
            recv_sem=all_recv.at[rep],
            device_id=dev(y, z, (rep + j) & 7),
            device_id_type=MESH,
        )

    def send_all(j, carry):
        all_copy(j).start()
        return carry

    lax.fori_loop(1, 8, send_all, 0)

    def await_all(j, carry):
        other = (rep + 8 - j) & 7
        pltpu.make_async_remote_copy(
            src_ref=whole.at[other],
            dst_ref=whole.at[other],
            send_sem=all_send.at[j],
            recv_sem=all_recv.at[other],
            device_id=dev(y, z, other),
            device_id_type=MESH,
        ).wait_recv()
        return carry

    lax.fori_loop(1, 8, await_all, 0)
    grad_ref[...] = whole[...].astype(f32)
    for k in (2, 1, 3):
        came = band((y + 4 - k) & 3)
        pltpu.make_async_remote_copy(
            src_ref=total_ref.at[came, :],
            dst_ref=total_ref.at[came, :],
            send_sem=yb_send.at[k],
            recv_sem=yb_recv.at[k],
            device_id=dev((y + 4 - k) & 3, z, rep),
            device_id_type=MESH,
        ).wait_recv()

    for copy in w_copies + wc_copies + core_copies + x_copies + y_copies + yb_copies:
        copy.wait_send()

    def drain_parts(j, carry):
        @pl.when(is_other(holder(j)))
        def _():
            part_copy(j).wait_send()

        @pl.when(jnp.logical_or(owner_z != z, j != rep))
        def _():
            sum_copy(j).wait_send()

        return carry

    lax.fori_loop(0, 8, drain_parts, 0)

    def drain_all(j, carry):
        all_copy(j).wait_send()
        return carry

    lax.fori_loop(1, 8, drain_all, 0)

    def drain_z(k, carry):
        @pl.when((z + k) & 15 < VCHUNKS)
        def _():
            z_copy(k).wait_send()

        @pl.when(z < VCHUNKS)
        def _():
            zb_copy(k).wait_send()

        return carry

    lax.fori_loop(1, 16, drain_z, 0)


def vmem():
    return pl.BlockSpec(memory_space=pltpu.VMEM)


def hbm():
    return pl.BlockSpec(memory_space=pl.ANY)


def dma(n):
    return pltpu.SemaphoreType.DMA((n,))


def step_call(*args):
    return pl.pallas_call(
        step_kernel,
        out_shape=(
            jax.ShapeDtypeStruct((8, PART, ROWS), f32),
            jax.ShapeDtypeStruct((V_ROWS, CROSS), f32),
        ),
        in_specs=[
            vmem(), vmem(), hbm(), vmem(), vmem(), hbm(), hbm(), vmem(), vmem(), vmem(), vmem(),
        ],
        out_specs=(vmem(), vmem()),
        scratch_shapes=[
            pltpu.VMEM((NHOT, E, E), bf16),
            pltpu.VMEM((V_ROWS, CROSS), bf16),
            pltpu.VMEM((8, PART, ROWS), bf16),
            pltpu.VMEM((GROUP, E, SLOTS), bf16),
            pltpu.VMEM((GROUP, E, SLOTS), bf16),
            pltpu.VMEM((GROUP, 8, SLOTS), i32),
            pltpu.VMEM((GROUP, 8, SLOTS), i32),
            pltpu.VMEM((GROUP, B), f32),
            pltpu.VMEM((GROUP, B), f32),
            pltpu.VMEM((GROUP, B), f32),
            pltpu.VMEM((GROUP, SLOTS, B), bf16),
            pltpu.VMEM((WIDE, B), f32),
            pltpu.VMEM((CROSS, RANK), bf16),
            pltpu.VMEM((RANK, CROSS), bf16),
            pltpu.VMEM((B, CROSS), bf16),
            pltpu.VMEM((B, CROSS), f32),
            pltpu.VMEM((RANK, B), bf16),
            pltpu.VMEM((B, RANK), f32),
            pltpu.VMEM((WIDE, B), f32),
            pltpu.VMEM((RANK, CROSS), bf16),
            pltpu.VMEM((GROUP, E, SLOTS), bf16),
            pltpu.VMEM((GROUP, E, SLOTS), bf16),
            pltpu.VMEM((WIDE, ROWS), f32),
            pltpu.VMEM((8, PART, ROWS), bf16),
            pltpu.VMEM((8, PART, ROWS), bf16),
            pltpu.VMEM((8, PART, ROWS), bf16),
            pltpu.VMEM((4, V_ROWS, CROSS), bf16),
            pltpu.VMEM((4, V_ROWS, CROSS), bf16),
            pltpu.VMEM((4, V_ROWS, CROSS), bf16),
            pltpu.VMEM((V_ROWS, CROSS), f32),
            pltpu.VMEM((4, 8, CROSS), f32),
            pltpu.VMEM((8, PADDED), f32),
            pltpu.VMEM((16, 8, VCOLS), f32),
            pltpu.VMEM((8, PADDED), f32),
            dma(8), dma(8), dma(GROUP), dma(GROUP), dma(GROUP), dma(GROUP), dma(4),
            dma(8), dma(8), dma(8), dma(8),
            dma(GROUP), dma(GROUP), dma(8), dma(8), dma(8), dma(8),
            dma(4), dma(4), dma(4), dma(4), dma(4), dma(4),
            dma(16), dma(16), dma(16), dma(16), dma(4), dma(4),
        ],
        compiler_params=pltpu.CompilerParams(
            collective_id=0, has_side_effects=True, vmem_limit_bytes=56 << 20
        ),
    )(*args)


def body(
    bottom,
    hot_ids,
    hot_tables,
    cold_owner,
    cold_row,
    cold_rows,
    cold_acc,
    u_weight,
    v_weight,
    v_acc,
    cross_bias,
    head,
    labels,
):
    rep = lax.axis_index("replica")
    turned = cold_rows.reshape(NCOLD, ROWS, E).transpose(0, 2, 1).reshape(8, PART, ROWS)
    part = lax.dynamic_index_in_dim(turned, rep, 0, keepdims=False).astype(bf16)
    grad_rows, grad_mine = step_call(
        cold_owner.T, cold_row.T, part, bottom, hot_ids.T, hot_tables, u_weight, v_weight,
        cross_bias.reshape(CROSS // E, E), head.reshape(CROSS // E, E), labels.reshape(2, E),
    )
    grad_rows = grad_rows.reshape(NCOLD, E, ROWS).transpose(0, 2, 1).reshape(NCOLD * ROWS, E)
    new_cold_acc = cold_acc + jnp.mean(grad_rows * grad_rows, axis=1)
    new_cold_rows = cold_rows - row_rate * grad_rows / (jnp.sqrt(new_cold_acc)[:, None] + eps_value)
    acc_dense = v_acc + jnp.mean(grad_mine * grad_mine, axis=1)
    new_v = v_weight - dense_rate * grad_mine / (jnp.sqrt(acc_dense)[:, None] + eps_value)
    return (new_cold_rows, new_cold_acc, new_v)


def solution(mesh):
    return jax.shard_map(
        body,
        mesh=mesh,
        in_specs=(
            P(("table", "replica"), None),
            P(("table", "replica"), None),
            P(),
            P(("table", "replica"), None),
            P(("table", "replica"), None),
            P("table", None),
            P("table"),
            P("replica", None),
            P("replica", None),
            P("replica"),
            P(),
            P(),
            P(("table", "replica")),
        ),
        out_specs=(P("table", None), P("table"), P("replica", None)),
        check_vma=False,
    )
```

```python
import functools
import jax
import jax.numpy as jnp
from jax import lax
from jax.experimental import pallas as pl
from jax.experimental.pallas import tpu as pltpu
from jax.sharding import PartitionSpec as P

NCOLD = 6
LOOK = 2
NHOT = 20
LOOKUPS = NCOLD * LOOK
E = 128
B = 256
ROWS = 256
SLOTS = 128
GROUP = 64
ITSELF = 40
PAIR_SELF = ITSELF // 2
V_START = 24
WIDE = NCOLD * E
PART = WIDE // 8
CROSS = 3456
PADDED = 3584
COLS = 384
U_ROWS = 432
U_PIECE = 112
V_PIECE = 896
V_ROWS = 32
RANK = 256
VCHUNKS = 14
MESH = pl.DeviceIdType.MESH

row_rate = 0.1
dense_rate = 0.05
eps_value = 1e-08

f32 = jnp.float32
bf16 = jnp.bfloat16
i32 = jnp.int32
NT = (((1,), (1,)), ((), ()))


def place_of():
    table, rep = lax.axis_index("table"), lax.axis_index("replica")
    return table >> 4, table & 15, rep


def dev(y, z, rep):
    return {"table": y * 16 + z, "replica": rep}


def held_z(z, rep):
    return 2 * ((((rep & 1) << 2) + (rep >> 1) - (z >> 1)) & 7) + (z & 1)


def holding_rep(z, owner_z):
    at = ((owner_z >> 1) + (z >> 1)) & 7
    return ((at & 3) << 1) + (at >> 2)


def member_of(y, z, rep):
    return y * 16 + held_z(z, rep)


def member_dev(member, z):
    mz = (z - (z & 1)) + (member & 1)
    return dev(member >> 4, mz, holding_rep(mz, member & 15))


def peer(i, y, z, rep):
    px = ((rep >> 1) + 2 + (i >> 2)) & 3
    pc = (rep + (i >> 1)) & 1
    pz = (z - (z & 1)) + ((z + i) & 1)
    return member_of((y + 2 + (i >> 4)) & 3, pz, px * 2 + pc)


def peer_back(i, y, z, rep):
    px = ((rep >> 1) + 6 - ((i >> 2) & 3)) & 3
    pc = (rep + (i >> 1)) & 1
    pz = (z - (z & 1)) + ((z + i) & 1)
    return member_of((y + 6 - (i >> 4)) & 3, pz, px * 2 + pc)


def tables(owner_ref, row_ref, pos, tab, rows):
    owners = lax.broadcasted_iota(i32, (GROUP, B), 0)
    named = jnp.zeros((GROUP, B), f32)
    table = jnp.zeros((GROUP, B), f32)
    row = jnp.zeros((GROUP, B), f32)
    for k in range(LOOKUPS):
        hit = owners == owner_ref[k : k + 1, :]
        named = jnp.where(hit, 1.0, named)
        table = jnp.where(hit, float(k // LOOK), table)
        row = jnp.where(hit, row_ref[k : k + 1, :].astype(f32), row)
    before = jnp.where(
        lax.broadcasted_iota(i32, (B, B), 0) < lax.broadcasted_iota(i32, (B, B), 1), 1.0, 0.0
    ).astype(bf16)
    place = jnp.dot(named.astype(bf16), before, preferred_element_type=f32)
    pos[...] = jnp.where(named > 0.0, place, -1.0)
    tab[...] = table
    rows[...] = row


def slots_of(pos, o):
    lines = lax.broadcasted_iota(i32, (SLOTS, B), 0).astype(f32)
    return jnp.where(lines == pos[pl.ds(o, 1), :], 1.0, 0.0).astype(bf16)


def rows_of(code):
    lines = lax.broadcasted_iota(i32, (ROWS, code.shape[1]), 0)
    return jnp.where(lines == code & (ROWS - 1), 1.0, 0.0).astype(bf16)


def others(count, act):
    def step(i, carry):
        @pl.when(i != ITSELF)
        def _():
            act(i)

        return carry

    lax.fori_loop(0, count, step, 0)


def step_kernel(
    owner_ref, row_ref, part_ref, bottom_ref, ids_ref, hot_hbm, u_ref, v_wide, bias_ref, head_ref, label_ref,
    grad_ref, total_ref,
    hot_ref, v_ref, held, replies, back, ask, asked, pos, tab, rows, picks, pooled,
    u_full, v_full, first, mixed, low_t, dlow, dpool, grads,
    arrived, out, acc, part_out, part_in, whole,
    core_in, pair, y_in, band, x_in, mine, z_in, strip, summed,
    held_send, held_recv, ask_send, ask_recv, rep_send, rep_recv, own_sem,
    w_send, w_recv, wy_send, wy_recv, wc_send, wc_recv,
    out_send, out_recv, part_send, part_recv, all_send, all_recv,
    core_send, core_recv, x_send, x_recv, y_send, y_recv, z_send, z_recv, zb_send, zb_recv, yb_send, yb_recv,
):
    y, z, rep = place_of()
    x, c = rep >> 1, rep & 1
    other_c = 1 - c
    sibling = x * 2 + other_c
    me = member_of(y, z, rep)
    group = z >> 1
    owner_z = held_z(z, rep)
    self_holder = owner_z == z

    hot_copy = pltpu.make_async_copy(hot_hbm, hot_ref, own_sem.at[3])
    hot_copy.start()

    bar = pltpu.get_barrier_semaphore()

    def signal(y_, z_, rep_):
        pl.semaphore_signal(bar, inc=1, device_id=dev(y_, z_, rep_), device_id_type=MESH)

    def greet_member(i):
        pl.semaphore_signal(
            bar, inc=1, device_id=member_dev(peer(i, y, z, rep), z), device_id_type=MESH
        )

    others(GROUP, greet_member)

    def holder(j):
        hz = (z + 2 * j) & 15
        return hz, holding_rep(hz, z)

    def is_other(at):
        return jnp.logical_or(at[0] != z, at[1] != rep)

    def source(j):
        return owner_z, (rep + j) & 7

    def greet_parts(j, carry):
        @pl.when(is_other(holder(j)))
        def _():
            signal(y, *holder(j))

        @pl.when(is_other(source(j)))
        def _():
            signal(y, *source(j))

        return carry

    lax.fori_loop(0, 8, greet_parts, 0)

    def greet_z(k, carry):
        signal(y, (z + k) & 15, rep)
        return carry

    lax.fori_loop(1, 16, greet_z, 0)
    v_ref[...] = v_wide[...].astype(bf16)
    tables(owner_ref, row_ref, pos, tab, rows)
    pl.semaphore_wait(bar, GROUP - 1 + 16 - jnp.where(self_holder, 2, 0).astype(i32) + 15)

    def part_copy(j):
        return pltpu.make_async_remote_copy(
            src_ref=part_ref,
            dst_ref=held.at[rep],
            send_sem=held_send.at[j],
            recv_sem=held_recv.at[rep],
            device_id=dev(y, *holder(j)),
            device_id_type=MESH,
        )

    def send_part(j, carry):
        @pl.when(is_other(holder(j)))
        def _():
            part_copy(j).start()

        return carry

    lax.fori_loop(0, 8, send_part, 0)
    own = pltpu.make_async_copy(part_ref, held.at[rep], own_sem.at[0])

    @pl.when(self_holder)
    def _():
        own.start()

    def u_at(r):
        return u_full.at[pl.ds(pl.multiple_of(r * U_ROWS, 16), U_ROWS), :]

    def v_at(r):
        return v_full.at[pl.ds(pl.multiple_of(r * V_ROWS, 16), V_ROWS), :]

    def weight_copies(src_u, src_v, r, sends, recvs, slot, y_, z_, rep_):
        return [
            pltpu.make_async_remote_copy(
                src_ref=src,
                dst_ref=dst,
                send_sem=sends.at[2 * slot + i],
                recv_sem=recvs.at[2 * slot + i],
                device_id=dev(y_, z_, rep_),
                device_id_type=MESH,
            )
            for i, (src, dst) in enumerate([(src_u, u_at(r)), (src_v, v_at(r))])
        ]

    def quarter(q, act):
        @pl.when(q < 3)
        def _():
            act(U_PIECE, V_PIECE)

        @pl.when(q == 3)
        def _():
            act(U_ROWS - 3 * U_PIECE, CROSS - 3 * V_PIECE)

    def u_piece(ref, base, q, n):
        return ref.at[pl.ds(pl.multiple_of(base + q * U_PIECE, 16), n), :]

    def v_piece(ref, base, q, n):
        at = pl.ds(pl.multiple_of(q * V_PIECE, V_PIECE), n)
        return ref.at[pl.ds(pl.multiple_of(base, 16), V_ROWS), at]

    def x_weights(k, r, to, act):
        def run(u_n, v_n):
            pairs = [
                (u_piece(u_ref, 0, y, u_n), u_piece(u_full, r * U_ROWS, y, u_n)),
                (v_piece(v_ref, 0, y, v_n), v_piece(v_full, r * V_ROWS, y, v_n)),
            ]
            for i, (src, dst) in enumerate(pairs):
                act(
                    pltpu.make_async_remote_copy(
                        src_ref=src,
                        dst_ref=dst,
                        send_sem=w_send.at[2 * k + i],
                        recv_sem=w_recv.at[2 * k + i],
                        device_id=dev(y, z, to),
                        device_id_type=MESH,
                    )
                )

        quarter(y, run)

    def y_weights(k, n, q, to, act):
        r = ((x + 4 - k) & 3) * 2 + c

        def run(u_n, v_n):
            for i, ref in enumerate(
                [u_piece(u_full, r * U_ROWS, q, u_n), v_piece(v_full, r * V_ROWS, q, v_n)]
            ):
                sem = (k * 4 + n) * 2 + i
                act(
                    pltpu.make_async_remote_copy(
                        src_ref=ref,
                        dst_ref=ref,
                        send_sem=wy_send.at[sem],
                        recv_sem=wy_recv.at[sem],
                        device_id=dev(to, z, rep),
                        device_id_type=MESH,
                    )
                )

        quarter(q, run)

    for k in (2, 1, 3):
        x_weights(k, rep, ((x + k) & 3) * 2 + c, lambda copy: copy.start())
    w_copies = weight_copies(u_ref, v_ref, rep, w_send, w_recv, 0, y, z, sibling)
    for copy in w_copies:
        copy.start()
    own_u = pltpu.make_async_copy(u_ref, u_at(rep), own_sem.at[1])
    own_v = pltpu.make_async_copy(v_ref, v_at(rep), own_sem.at[2])
    own_u.start()
    own_v.start()

    lines16 = lax.broadcasted_iota(i32, (16, B), 0)

    def ask_copy(m):
        return pltpu.make_async_remote_copy(
            src_ref=ask.at[m],
            dst_ref=asked.at[me],
            send_sem=ask_send.at[m],
            recv_sem=ask_recv.at[me],
            device_id=member_dev(m, z),
            device_id_type=MESH,
        )

    def ask_pair(p, carry):
        a, b = peer(2 * p, y, z, rep), peer(2 * p + 1, y, z, rep)
        pick_a, pick_b = slots_of(pos, a), slots_of(pos, b)
        picks[a] = pick_a
        picks[b] = pick_b
        lhs = jnp.where(lines16 == 0, rows[pl.ds(a, 1), :], 0.0)
        lhs = jnp.where(lines16 == 1, tab[pl.ds(a, 1), :], lhs)
        lhs = jnp.where(lines16 == 2, rows[pl.ds(b, 1), :], lhs)
        lhs = jnp.where(lines16 == 3, tab[pl.ds(b, 1), :], lhs).astype(bf16)
        got = lax.dot_general(
            lhs, jnp.concatenate([pick_a, pick_b], axis=0), NT, preferred_element_type=f32
        )
        code_a = (got[0:1, :SLOTS] + got[1:2, :SLOTS] * float(ROWS)).astype(i32)
        code_b = (got[2:3, SLOTS:] + got[3:4, SLOTS:] * float(ROWS)).astype(i32)
        ask[a] = jnp.broadcast_to(code_a, (8, SLOTS))
        ask[b] = jnp.broadcast_to(code_b, (8, SLOTS))

        @pl.when(p != PAIR_SELF)
        def _():
            ask_copy(a).start()

        @pl.when(p == PAIR_SELF)
        def _():
            asked[me] = ask[me]

        ask_copy(b).start()
        return carry

    lax.fori_loop(0, GROUP // 2, ask_pair, 0)

    first[:, 0:E] = bottom_ref[...]
    hot_copy.wait()
    ids = ids_ref[...].astype(f32).T
    lanes = lax.broadcasted_iota(i32, (B, E), 1).astype(f32)
    for j in range(NHOT):
        one = jnp.where(lanes == ids[:, j : j + 1], 1.0, 0.0).astype(bf16)
        at = E + WIDE + j * E
        first[:, at : at + E] = jnp.dot(one, hot_ref[j], preferred_element_type=f32).astype(bf16)

    for k in (1, 3, 2):
        came = ((x + 4 - k) & 3) * 2 + c
        x_weights(k, came, came, lambda copy: copy.wait_recv())
        for n in (2, 1, 3):
            y_weights(k, n, y, (y + n) & 3, lambda copy: copy.start())

    def await_part(j, carry):
        sz, srep = source(j)

        @pl.when(is_other((sz, srep)))
        def _():
            pltpu.make_async_remote_copy(
                src_ref=part_ref,
                dst_ref=held.at[srep],
                send_sem=held_send.at[0],
                recv_sem=held_recv.at[srep],
                device_id=dev(y, sz, srep),
                device_id_type=MESH,
            ).wait_recv()

        return carry

    lax.fori_loop(0, 8, await_part, 0)

    @pl.when(self_holder)
    def _():
        own.wait()

    def reply_copy(m):
        return pltpu.make_async_remote_copy(
            src_ref=back.at[m],
            dst_ref=replies.at[me],
            send_sem=rep_send.at[m],
            recv_sem=rep_recv.at[me],
            device_id=member_dev(m, z),
            device_id_type=MESH,
        )

    def await_ask(m):
        pltpu.make_async_remote_copy(
            src_ref=ask.at[m],
            dst_ref=asked.at[m],
            send_sem=ask_send.at[m],
            recv_sem=ask_recv.at[m],
            device_id=member_dev(m, z),
            device_id_type=MESH,
        ).wait_recv()

    def reply_pair(p, carry):
        a, b = peer_back(2 * p, y, z, rep), peer_back(2 * p + 1, y, z, rep)

        @pl.when(p != PAIR_SELF)
        def _():
            await_ask(a)

        await_ask(b)
        code = jnp.concatenate([asked[a][0:1, :], asked[b][0:1, :]], axis=1)
        table = code >> 8
        found = jnp.dot(
            held[...].reshape(WIDE, ROWS), rows_of(code), preferred_element_type=f32
        )
        got = found[0:E]
        for t in range(1, NCOLD):
            got = jnp.where(table == t, found[t * E : (t + 1) * E], got)
        got = got.astype(bf16)
        back[a] = got[:, :SLOTS]
        back[b] = got[:, SLOTS:]

        @pl.when(p != PAIR_SELF)
        def _():
            reply_copy(a).start()

        @pl.when(p == PAIR_SELF)
        def _():
            replies[me] = back[me]

        reply_copy(b).start()
        return carry

    lax.fori_loop(0, GROUP // 2, reply_pair, 0)

    wc_copies = []
    for k in (1, 3, 2):
        for n in (1, 3, 2):
            came = (y + 4 - n) & 3
            y_weights(k, n, came, came, lambda copy: copy.wait_recv())
        came = ((x + 4 - k) & 3) * 2 + c
        forward = weight_copies(u_at(came), v_at(came), came, wc_send, wc_recv, k, y, z, sibling)
        for copy in forward:
            copy.start()
        wc_copies += forward

    pooled[...] = jnp.zeros((WIDE, B), f32)

    def await_reply(m):
        pltpu.make_async_remote_copy(
            src_ref=back.at[m],
            dst_ref=replies.at[m],
            send_sem=rep_send.at[m],
            recv_sem=rep_recv.at[m],
            device_id=member_dev(m, z),
            device_id_type=MESH,
        ).wait_recv()

    def pool_pair(p, carry):
        a, b = peer(2 * p, y, z, rep), peer(2 * p + 1, y, z, rep)

        @pl.when(p != PAIR_SELF)
        def _():
            await_reply(a)

        await_reply(b)
        got_a = jnp.dot(replies[a], picks[a], preferred_element_type=f32)
        got_b = jnp.dot(replies[b], picks[b], preferred_element_type=f32)
        tab_a, tab_b = tab[pl.ds(a, 1), :], tab[pl.ds(b, 1), :]
        for t in range(NCOLD):
            more = jnp.where(tab_a == float(t), got_a, 0.0) + jnp.where(
                tab_b == float(t), got_b, 0.0
            )
            pooled[t * E : (t + 1) * E, :] += more
        return carry

    lax.fori_loop(0, 20, pool_pair, 0)

    for k in range(4):
        came = ((x + 4 - k) & 3) * 2 + other_c
        sends, recvs = (w_send, w_recv) if k == 0 else (wc_send, wc_recv)
        for copy in weight_copies(u_at(came), v_at(came), came, sends, recvs, k, y, z, sibling):
            copy.wait_recv()
    own_u.wait()
    own_v.wait()
    hot_at = E + WIDE
    low = jnp.dot(first[:, 0:E], u_full[0:E, :], preferred_element_type=f32)
    low = low + jnp.dot(first[:, hot_at:], u_full[hot_at:, :], preferred_element_type=f32)

    lax.fori_loop(20, 32, pool_pair, 0)
    for t in range(NCOLD):
        first[:, E + t * E : E + (t + 1) * E] = pooled[t * E : (t + 1) * E, :].T.astype(bf16)

    low = low + jnp.dot(first[:, E:hot_at], u_full[E:hot_at, :], preferred_element_type=f32)
    low_half = low.astype(bf16)
    low_t[...] = low.T.astype(bf16)

    def cols(i, width):
        return pl.ds(pl.multiple_of(i * width, width), width)

    def line(ref, i):
        n = COLS // E
        return jnp.concatenate([ref[pl.ds(i * n + q, 1), :] for q in range(n)], axis=1)

    def forward_cols(i, sums):
        at = cols(i, COLS)
        mixing = jnp.dot(low_half, v_full[:, at], preferred_element_type=f32) + line(bias_ref, i)
        wide = first[:, at].astype(f32)
        crossed = (wide * mixing + wide) * line(head_ref, i)
        mixed[:, at] = mixing
        for q in range(COLS // E):
            sums = sums + crossed[:, q * E : (q + 1) * E]
        return sums

    sums = lax.fori_loop(0, CROSS // COLS, forward_cols, jnp.zeros((B, E), f32))
    logit = jnp.sum(sums, axis=1, keepdims=True)
    label = jnp.concatenate([label_ref[0:1, :], label_ref[1:2, :]], axis=1).astype(f32)
    label = jnp.broadcast_to(label, (8, B)).T
    dlogit = jax.nn.sigmoid(logit) - label[:, 0:1]

    dlow[...] = jnp.zeros((B, RANK), f32)
    grads[:, CROSS:] = jnp.zeros((RANK, PADDED - CROSS), bf16)

    def backward_cols(i, carry):
        at = cols(i, COLS)
        dmix = (dlogit * line(head_ref, i) * first[:, at].astype(f32)).astype(bf16)
        dlow[...] += lax.dot_general(dmix, v_full[:, at], NT, preferred_element_type=f32)
        grads[:, at] = jnp.dot(low_t[...], dmix, preferred_element_type=f32).astype(bf16)
        return carry

    lax.fori_loop(0, CROSS // COLS, backward_cols, 0)
    dlow_half = dlow[...].astype(bf16)
    for t in range(NCOLD):
        lo, hi = E + t * E, E + (t + 1) * E
        direct = dlogit * head_ref[t + 1 : t + 2, :] * (mixed[:, lo:hi] + 1.0)
        through = lax.dot_general(u_full[lo:hi, :], dlow_half, NT, preferred_element_type=f32)
        dpool[t * E : (t + 1) * E, :] = (direct.T + through).astype(bf16).astype(f32)

    def v_rows(r):
        return pl.ds(pl.multiple_of(r * V_ROWS, V_ROWS), V_ROWS)

    core_copies = []
    for k in range(4):
        copy = pltpu.make_async_remote_copy(
            src_ref=grads.at[v_rows(2 * k + other_c), :],
            dst_ref=core_in.at[k],
            send_sem=core_send.at[k],
            recv_sem=core_recv.at[k],
            device_id=dev(y, z, sibling),
            device_id_type=MESH,
        )
        copy.start()
        core_copies.append(copy)

    def out_copy(m):
        return pltpu.make_async_remote_copy(
            src_ref=out.at[m],
            dst_ref=arrived.at[me],
            send_sem=out_send.at[m],
            recv_sem=out_recv.at[me],
            device_id=member_dev(m, z),
            device_id_type=MESH,
        )

    def pack(m):
        which = tab[pl.ds(m, 1), :]
        chosen = dpool[0:E, :]
        for t in range(1, NCOLD):
            chosen = jnp.where(which == float(t), dpool[t * E : (t + 1) * E, :], chosen)
        out[m] = lax.dot_general(
            chosen.astype(bf16), picks[m], NT, preferred_element_type=f32
        ).astype(bf16)

    def pack_pair(p, carry):
        a, b = peer(2 * p, y, z, rep), peer(2 * p + 1, y, z, rep)
        pack(a)
        pack(b)

        @pl.when(p != PAIR_SELF)
        def _():
            out_copy(a).start()

        @pl.when(p == PAIR_SELF)
        def _():
            arrived[me] = out[me]

        out_copy(b).start()
        return carry

    lax.fori_loop(0, 32, pack_pair, 0)

    for k in range(4):
        core_copies[k].wait_recv()
        pair[k] = (grads[v_rows(2 * k + c), :].astype(f32) + core_in[k].astype(f32)).astype(bf16)


    acc[...] = jnp.zeros((WIDE, ROWS), f32)

    def await_out(m):
        pltpu.make_async_remote_copy(
            src_ref=out.at[m],
            dst_ref=arrived.at[m],
            send_sem=out_send.at[m],
            recv_sem=out_recv.at[m],
            device_id=member_dev(m, z),
            device_id_type=MESH,
        ).wait_recv()

    def add_pair(p, carry):
        a, b = peer_back(2 * p, y, z, rep), peer_back(2 * p + 1, y, z, rep)

        @pl.when(p != PAIR_SELF)
        def _():
            await_out(a)

        await_out(b)
        code = jnp.concatenate([asked[a][0:1, :], asked[b][0:1, :]], axis=1)
        table = code >> 8
        came = jnp.concatenate([arrived[a], arrived[b]], axis=1).astype(f32)
        lhs = jnp.concatenate(
            [jnp.where(table == t, came, 0.0).astype(bf16) for t in range(NCOLD)], axis=0
        )
        acc[...] += lax.dot_general(lhs, rows_of(code), NT, preferred_element_type=f32)
        return carry

    lax.fori_loop(0, V_START, add_pair, 0)

    def piece(j):
        return pl.ds(pl.multiple_of(j * V_PIECE, V_PIECE), V_PIECE)

    y_copies = []
    for k in (2, 1, 3):
        to = (y + k) & 3
        copy = pltpu.make_async_remote_copy(
            src_ref=pair.at[:, :, piece(to)],
            dst_ref=y_in.at[k],
            send_sem=y_send.at[k],
            recv_sem=y_recv.at[k],
            device_id=dev(to, z, rep),
            device_id_type=MESH,
        )
        copy.start()
        y_copies.append(copy)
    lax.fori_loop(V_START, 32, add_pair, 0)


    def sum_copy(j):
        return pltpu.make_async_remote_copy(
            src_ref=part_out.at[j],
            dst_ref=part_in.at[group],
            send_sem=part_send.at[j],
            recv_sem=part_recv.at[group],
            device_id=dev(y, owner_z, j),
            device_id_type=MESH,
        )

    def send_sum(j, carry):
        part_out[j] = acc[pl.ds(pl.multiple_of(j * PART, PART), PART), :].astype(bf16)
        other = jnp.logical_or(owner_z != z, j != rep)

        @pl.when(other)
        def _():
            sum_copy(j).start()

        @pl.when(jnp.logical_not(other))
        def _():
            part_in[group] = part_out[j]

        return carry

    lax.fori_loop(0, 8, send_sum, 0)

    for copy in y_copies:
        copy.wait_recv()
    for k in range(4):
        band[k] = (
            pair[k, :, piece(y)].astype(f32)
            + y_in[1, k].astype(f32)
            + y_in[2, k].astype(f32)
            + y_in[3, k].astype(f32)
        )
    x_copies = []
    for k in (2, 1, 3):
        to = (x + k) & 3
        copy = pltpu.make_async_remote_copy(
            src_ref=band.at[to],
            dst_ref=x_in.at[k],
            send_sem=x_send.at[k],
            recv_sem=x_recv.at[k],
            device_id=dev(y, z, to * 2 + c),
            device_id_type=MESH,
        )
        copy.start()
        x_copies.append(copy)
    for copy in x_copies:
        copy.wait_recv()
    mine[...] = band[x] + x_in[1] + x_in[2] + x_in[3]

    def block(ref, j):
        return ref.at[
            pl.ds(pl.multiple_of((j & 1) * 16, 16), 16), pl.ds(pl.multiple_of((j >> 1) * E, E), E)
        ]

    def z_copy(k):
        to = (z + k) & 15
        return pltpu.make_async_remote_copy(
            src_ref=block(mine, to),
            dst_ref=z_in.at[k],
            send_sem=z_send.at[k],
            recv_sem=z_recv.at[k],
            device_id=dev(y, to, rep),
            device_id_type=MESH,
        )

    def z_start(k, carry):
        @pl.when((z + k) & 15 < VCHUNKS)
        def _():
            z_copy(k).start()

        return carry

    lax.fori_loop(1, 16, z_start, 0)

    def zb_copy(k):
        return pltpu.make_async_remote_copy(
            src_ref=block(strip, z),
            dst_ref=block(strip, z),
            send_sem=zb_send.at[k],
            recv_sem=zb_recv.at[z],
            device_id=dev(y, (z + k) & 15, rep),
            device_id_type=MESH,
        )

    @pl.when(z < VCHUNKS)
    def _():
        def z_wait(k, carry):
            pltpu.make_async_remote_copy(
                src_ref=z_in.at[k],
                dst_ref=z_in.at[k],
                send_sem=z_send.at[k],
                recv_sem=z_recv.at[k],
                device_id=dev(y, (z + 16 - k) & 15, rep),
                device_id_type=MESH,
            ).wait_recv()
            return carry

        lax.fori_loop(1, 16, z_wait, 0)
        got = block(mine, z)[...]
        for k in range(1, 16):
            got = got + z_in[k]
        block(strip, z)[...] = got

        def zb_start(k, carry):
            zb_copy(k).start()
            return carry

        lax.fori_loop(1, 16, zb_start, 0)

    def drain(i):
        m = peer(i, y, z, rep)
        ask_copy(m).wait_send()
        reply_copy(m).wait_send()
        out_copy(m).wait_send()

    others(GROUP, drain)

    def await_sum(j, carry):
        sz, srep = holder(j)

        @pl.when(is_other((sz, srep)))
        def _():
            pltpu.make_async_remote_copy(
                src_ref=part_out.at[0],
                dst_ref=part_in.at[sz >> 1],
                send_sem=part_send.at[0],
                recv_sem=part_recv.at[sz >> 1],
                device_id=dev(y, sz, srep),
                device_id_type=MESH,
            ).wait_recv()

        return carry

    lax.fori_loop(0, 8, await_sum, 0)
    total = part_in[0].astype(f32)
    for g in range(1, 8):
        total = total + part_in[g].astype(f32)
    whole[rep] = total.astype(bf16)

    def all_copy(j):
        return pltpu.make_async_remote_copy(
            src_ref=whole.at[rep],
            dst_ref=whole.at[rep],
            send_sem=all_send.at[j],
            recv_sem=all_recv.at[rep],
            device_id=dev(y, z, (rep + j) & 7),
            device_id_type=MESH,
        )

    def send_all(j, carry):
        all_copy(j).start()
        return carry

    lax.fori_loop(1, 8, send_all, 0)

    def zb_wait(k, carry):
        other = (z + 16 - k) & 15

        @pl.when(other < VCHUNKS)
        def _():
            pltpu.make_async_remote_copy(
                src_ref=block(strip, other),
                dst_ref=block(strip, other),
                send_sem=zb_send.at[k],
                recv_sem=zb_recv.at[other],
                device_id=dev(y, other, rep),
                device_id_type=MESH,
            ).wait_recv()

        return carry

    lax.fori_loop(1, 16, zb_wait, 0)
    summed[:, piece(y)] = strip[...]
    yb_copies = []
    for k in (2, 1, 3):
        copy = pltpu.make_async_remote_copy(
            src_ref=summed.at[:, piece(y)],
            dst_ref=summed.at[:, piece(y)],
            send_sem=yb_send.at[k],
            recv_sem=yb_recv.at[k],
            device_id=dev((y + k) & 3, z, rep),
            device_id_type=MESH,
        )
        copy.start()
        yb_copies.append(copy)

    def await_all(j, carry):
        other = (rep + 8 - j) & 7
        pltpu.make_async_remote_copy(
            src_ref=whole.at[other],
            dst_ref=whole.at[other],
            send_sem=all_send.at[j],
            recv_sem=all_recv.at[other],
            device_id=dev(y, z, other),
            device_id_type=MESH,
        ).wait_recv()
        return carry

    lax.fori_loop(1, 8, await_all, 0)
    grad_ref[...] = whole[...].astype(f32)
    for k in (1, 3, 2):
        came = piece((y + 4 - k) & 3)
        pltpu.make_async_remote_copy(
            src_ref=summed.at[:, came],
            dst_ref=summed.at[:, came],
            send_sem=yb_send.at[k],
            recv_sem=yb_recv.at[k],
            device_id=dev((y + 4 - k) & 3, z, rep),
            device_id_type=MESH,
        ).wait_recv()
    total_ref[...] = summed[:, :CROSS]

    for k in (1, 2, 3):
        x_weights(k, rep, ((x + k) & 3) * 2 + c, lambda copy: copy.wait_send())
        for n in (1, 2, 3):
            y_weights(k, n, y, (y + n) & 3, lambda copy: copy.wait_send())
    for copy in w_copies + wc_copies + core_copies + x_copies + y_copies + yb_copies:
        copy.wait_send()

    def drain_parts(j, carry):
        @pl.when(is_other(holder(j)))
        def _():
            part_copy(j).wait_send()

        @pl.when(jnp.logical_or(owner_z != z, j != rep))
        def _():
            sum_copy(j).wait_send()

        return carry

    lax.fori_loop(0, 8, drain_parts, 0)

    def drain_all(j, carry):
        all_copy(j).wait_send()
        return carry

    lax.fori_loop(1, 8, drain_all, 0)

    def drain_z(k, carry):
        @pl.when((z + k) & 15 < VCHUNKS)
        def _():
            z_copy(k).wait_send()

        @pl.when(z < VCHUNKS)
        def _():
            zb_copy(k).wait_send()

        return carry

    lax.fori_loop(1, 16, drain_z, 0)


def vmem():
    return pl.BlockSpec(memory_space=pltpu.VMEM)


def hbm():
    return pl.BlockSpec(memory_space=pl.ANY)


def dma(n):
    return pltpu.SemaphoreType.DMA((n,))


def step_call(*args):
    return pl.pallas_call(
        step_kernel,
        out_shape=(
            jax.ShapeDtypeStruct((8, PART, ROWS), f32),
            jax.ShapeDtypeStruct((V_ROWS, CROSS), f32),
        ),
        in_specs=[
            vmem(), vmem(), hbm(), vmem(), vmem(), hbm(), hbm(), vmem(), vmem(), vmem(), vmem(),
        ],
        out_specs=(vmem(), vmem()),
        scratch_shapes=[
            pltpu.VMEM((NHOT, E, E), bf16),
            pltpu.VMEM((V_ROWS, CROSS), bf16),
            pltpu.VMEM((8, PART, ROWS), bf16),
            pltpu.VMEM((GROUP, E, SLOTS), bf16),
            pltpu.VMEM((GROUP, E, SLOTS), bf16),
            pltpu.VMEM((GROUP, 8, SLOTS), i32),
            pltpu.VMEM((GROUP, 8, SLOTS), i32),
            pltpu.VMEM((GROUP, B), f32),
            pltpu.VMEM((GROUP, B), f32),
            pltpu.VMEM((GROUP, B), f32),
            pltpu.VMEM((GROUP, SLOTS, B), bf16),
            pltpu.VMEM((WIDE, B), f32),
            pltpu.VMEM((CROSS, RANK), bf16),
            pltpu.VMEM((RANK, CROSS), bf16),
            pltpu.VMEM((B, CROSS), bf16),
            pltpu.VMEM((B, CROSS), f32),
            pltpu.VMEM((RANK, B), bf16),
            pltpu.VMEM((B, RANK), f32),
            pltpu.VMEM((WIDE, B), f32),
            pltpu.VMEM((RANK, PADDED), bf16),
            pltpu.VMEM((GROUP, E, SLOTS), bf16),
            pltpu.VMEM((GROUP, E, SLOTS), bf16),
            pltpu.VMEM((WIDE, ROWS), f32),
            pltpu.VMEM((8, PART, ROWS), bf16),
            pltpu.VMEM((8, PART, ROWS), bf16),
            pltpu.VMEM((8, PART, ROWS), bf16),
            pltpu.VMEM((4, V_ROWS, PADDED), bf16),
            pltpu.VMEM((4, V_ROWS, PADDED), bf16),
            pltpu.VMEM((4, 4, V_ROWS, V_PIECE), bf16),
            pltpu.VMEM((4, V_ROWS, V_PIECE), f32),
            pltpu.VMEM((4, V_ROWS, V_PIECE), f32),
            pltpu.VMEM((V_ROWS, V_PIECE), f32),
            pltpu.VMEM((16, 16, E), f32),
            pltpu.VMEM((V_ROWS, V_PIECE), f32),
            pltpu.VMEM((V_ROWS, PADDED), f32),
            dma(8), dma(8), dma(GROUP), dma(GROUP), dma(GROUP), dma(GROUP), dma(4),
            dma(8), dma(8), dma(32), dma(32), dma(8), dma(8),
            dma(GROUP), dma(GROUP), dma(8), dma(8), dma(8), dma(8),
            dma(4), dma(4), dma(4), dma(4), dma(4), dma(4),
            dma(16), dma(16), dma(16), dma(16), dma(4), dma(4),
        ],
        compiler_params=pltpu.CompilerParams(
            collective_id=0, has_side_effects=True, vmem_limit_bytes=56 << 20
        ),
    )(*args)


def body(
    bottom,
    hot_ids,
    hot_tables,
    cold_owner,
    cold_row,
    cold_rows,
    cold_acc,
    u_weight,
    v_weight,
    v_acc,
    cross_bias,
    head,
    labels,
):
    rep = lax.axis_index("replica")
    turned = cold_rows.reshape(NCOLD, ROWS, E).transpose(0, 2, 1).reshape(8, PART, ROWS)
    part = lax.dynamic_index_in_dim(turned, rep, 0, keepdims=False).astype(bf16)
    grad_rows, grad_mine = step_call(
        cold_owner.T, cold_row.T, part, bottom, hot_ids.T, hot_tables, u_weight, v_weight,
        cross_bias.reshape(CROSS // E, E), head.reshape(CROSS // E, E), labels.reshape(2, E),
    )
    grad_rows = grad_rows.reshape(NCOLD, E, ROWS).transpose(0, 2, 1).reshape(NCOLD * ROWS, E)
    new_cold_acc = cold_acc + jnp.mean(grad_rows * grad_rows, axis=1)
    new_cold_rows = cold_rows - row_rate * grad_rows / (jnp.sqrt(new_cold_acc)[:, None] + eps_value)
    acc_dense = v_acc + jnp.mean(grad_mine * grad_mine, axis=1)
    new_v = v_weight - dense_rate * grad_mine / (jnp.sqrt(acc_dense)[:, None] + eps_value)
    return (new_cold_rows, new_cold_acc, new_v)


def solution(mesh):
    return jax.shard_map(
        body,
        mesh=mesh,
        in_specs=(
            P(("table", "replica"), None),
            P(("table", "replica"), None),
            P(),
            P(("table", "replica"), None),
            P(("table", "replica"), None),
            P("table", None),
            P("table"),
            P("replica", None),
            P("replica", None),
            P("replica"),
            P(),
            P(),
            P(("table", "replica")),
        ),
        out_specs=(P("table", None), P("table"), P("replica", None)),
        check_vma=False,
    )
```

```python
import functools
import jax
import jax.numpy as jnp
from jax import lax
from jax.experimental import pallas as pl
from jax.experimental.pallas import tpu as pltpu
from jax.sharding import PartitionSpec as P

NCOLD = 6
LOOK = 2
NHOT = 20
LOOKUPS = NCOLD * LOOK
E = 128
B = 256
ROWS = 256
SLOTS = 128
GROUP = 64
ITSELF = 8
PAIR_SELF = ITSELF // 2
V_START = 24
WIDE = NCOLD * E
PART = WIDE // 8
CROSS = 3456
PADDED = 3584
COLS = 384
U_ROWS = 432
U_PIECE = 112
V_PIECE = 896
V_ROWS = 32
RANK = 256
VCHUNKS = 14
MESH = pl.DeviceIdType.MESH

row_rate = 0.1
dense_rate = 0.05
eps_value = 1e-08

f32 = jnp.float32
bf16 = jnp.bfloat16
i32 = jnp.int32
NT = (((1,), (1,)), ((), ()))


def place_of():
    table, rep = lax.axis_index("table"), lax.axis_index("replica")
    return table >> 4, table & 15, rep


def dev(y, z, rep):
    return {"table": y * 16 + z, "replica": rep}


def held_z(z, rep):
    return 2 * ((((rep & 1) << 2) + (rep >> 1) - (z >> 1)) & 7) + (z & 1)


def holding_rep(z, owner_z):
    at = ((owner_z >> 1) + (z >> 1)) & 7
    return ((at & 3) << 1) + (at >> 2)


def member_of(y, z, rep):
    return y * 16 + held_z(z, rep)


def member_dev(member, z):
    mz = (z - (z & 1)) + (member & 1)
    return dev(member >> 4, mz, holding_rep(mz, member & 15))


def peer(i, y, z, rep):
    px = ((rep >> 1) + 2 + (i >> 2)) & 3
    pc = (rep + (i >> 1)) & 1
    pz = (z - (z & 1)) + ((z + i) & 1)
    return (y + 2 + (i >> 4) + (i >> 2)) & 3, pz, px * 2 + pc


def peer_back(i, y, z, rep):
    px = ((rep >> 1) + 6 - ((i >> 2) & 3)) & 3
    pc = (rep + (i >> 1)) & 1
    pz = (z - (z & 1)) + ((z + i) & 1)
    return (y + 6 - (((i >> 4) + (i >> 2)) & 3)) & 3, pz, px * 2 + pc


def tables(owner_ref, row_ref, pos, tab, rows):
    owners = lax.broadcasted_iota(i32, (GROUP, B), 0)
    named = jnp.zeros((GROUP, B), f32)
    table = jnp.zeros((GROUP, B), f32)
    row = jnp.zeros((GROUP, B), f32)
    for k in range(LOOKUPS):
        hit = owners == owner_ref[k : k + 1, :]
        named = jnp.where(hit, 1.0, named)
        table = jnp.where(hit, float(k // LOOK), table)
        row = jnp.where(hit, row_ref[k : k + 1, :].astype(f32), row)
    before = jnp.where(
        lax.broadcasted_iota(i32, (B, B), 0) < lax.broadcasted_iota(i32, (B, B), 1), 1.0, 0.0
    ).astype(bf16)
    place = jnp.dot(named.astype(bf16), before, preferred_element_type=f32)
    pos[...] = jnp.where(named > 0.0, place, -1.0)
    tab[...] = table
    rows[...] = row


def slots_of(pos, o):
    lines = lax.broadcasted_iota(i32, (SLOTS, B), 0).astype(f32)
    return jnp.where(lines == pos[pl.ds(o, 1), :], 1.0, 0.0).astype(bf16)


def rows_of(code):
    lines = lax.broadcasted_iota(i32, (ROWS, code.shape[1]), 0)
    return jnp.where(lines == code & (ROWS - 1), 1.0, 0.0).astype(bf16)


def others(count, act):
    def step(i, carry):
        @pl.when(i != ITSELF)
        def _():
            act(i)

        return carry

    lax.fori_loop(0, count, step, 0)


def step_kernel(
    owner_ref, row_ref, part_ref, bottom_ref, ids_ref, hot_hbm, u_ref, v_wide, bias_ref, head_ref, label_ref,
    grad_ref, total_ref,
    hot_ref, v_ref, held, replies, back, ask, asked, pos, tab, rows, picks, pooled,
    u_full, v_full, first, mixed, low_t, dlow, dpool, grads,
    arrived, out, acc, part_out, part_in, whole,
    core_in, pair, y_in, band, x_in, mine, z_in, strip, summed,
    held_send, held_recv, ask_send, ask_recv, rep_send, rep_recv, own_sem,
    w_send, w_recv, wy_send, wy_recv, wc_send, wc_recv,
    out_send, out_recv, part_send, part_recv, all_send, all_recv,
    core_send, core_recv, x_send, x_recv, y_send, y_recv, z_send, z_recv, zb_send, zb_recv, yb_send, yb_recv,
):
    y, z, rep = place_of()
    x, c = rep >> 1, rep & 1
    other_c = 1 - c
    sibling = x * 2 + other_c
    me = member_of(y, z, rep)
    group = z >> 1
    owner_z = held_z(z, rep)
    self_holder = owner_z == z

    hot_copy = pltpu.make_async_copy(hot_hbm, hot_ref, own_sem.at[3])
    hot_copy.start()

    bar = pltpu.get_barrier_semaphore()

    def signal(y_, z_, rep_):
        pl.semaphore_signal(bar, inc=1, device_id=dev(y_, z_, rep_), device_id_type=MESH)

    def greet_member(i):
        signal(*peer(i, y, z, rep))

    others(GROUP, greet_member)

    def holder(j):
        hz = (z + 2 * j) & 15
        return hz, holding_rep(hz, z)

    def is_other(at):
        return jnp.logical_or(at[0] != z, at[1] != rep)

    def source(j):
        return owner_z, (rep + j) & 7

    def greet_parts(j, carry):
        @pl.when(is_other(holder(j)))
        def _():
            signal(y, *holder(j))

        @pl.when(is_other(source(j)))
        def _():
            signal(y, *source(j))

        return carry

    lax.fori_loop(0, 8, greet_parts, 0)

    def greet_z(k, carry):
        signal(y, (z + k) & 15, rep)
        return carry

    lax.fori_loop(1, 16, greet_z, 0)
    v_ref[...] = v_wide[...].astype(bf16)
    tables(owner_ref, row_ref, pos, tab, rows)
    pl.semaphore_wait(bar, GROUP - 1 + 16 - jnp.where(self_holder, 2, 0).astype(i32) + 15)

    def part_copy(j):
        return pltpu.make_async_remote_copy(
            src_ref=part_ref,
            dst_ref=held.at[rep],
            send_sem=held_send.at[j],
            recv_sem=held_recv.at[rep],
            device_id=dev(y, *holder(j)),
            device_id_type=MESH,
        )

    def send_part(j, carry):
        @pl.when(is_other(holder(j)))
        def _():
            part_copy(j).start()

        return carry

    lax.fori_loop(0, 8, send_part, 0)
    own = pltpu.make_async_copy(part_ref, held.at[rep], own_sem.at[0])

    @pl.when(self_holder)
    def _():
        own.start()

    def u_at(r):
        return u_full.at[pl.ds(pl.multiple_of(r * U_ROWS, 16), U_ROWS), :]

    def v_at(r):
        return v_full.at[pl.ds(pl.multiple_of(r * V_ROWS, 16), V_ROWS), :]

    def weight_copies(src_u, src_v, r, sends, recvs, slot, y_, z_, rep_):
        return [
            pltpu.make_async_remote_copy(
                src_ref=src,
                dst_ref=dst,
                send_sem=sends.at[2 * slot + i],
                recv_sem=recvs.at[2 * slot + i],
                device_id=dev(y_, z_, rep_),
                device_id_type=MESH,
            )
            for i, (src, dst) in enumerate([(src_u, u_at(r)), (src_v, v_at(r))])
        ]

    def quarter(q, act):
        @pl.when(q < 3)
        def _():
            act(U_PIECE, V_PIECE)

        @pl.when(q == 3)
        def _():
            act(U_ROWS - 3 * U_PIECE, CROSS - 3 * V_PIECE)

    def u_piece(ref, base, q, n):
        return ref.at[pl.ds(pl.multiple_of(base + q * U_PIECE, 16), n), :]

    def v_piece(ref, base, q, n):
        at = pl.ds(pl.multiple_of(q * V_PIECE, V_PIECE), n)
        return ref.at[pl.ds(pl.multiple_of(base, 16), V_ROWS), at]

    def x_weights(k, r, to, act):
        def run(u_n, v_n):
            pairs = [
                (u_piece(u_ref, 0, y, u_n), u_piece(u_full, r * U_ROWS, y, u_n)),
                (v_piece(v_ref, 0, y, v_n), v_piece(v_full, r * V_ROWS, y, v_n)),
            ]
            for i, (src, dst) in enumerate(pairs):
                act(
                    pltpu.make_async_remote_copy(
                        src_ref=src,
                        dst_ref=dst,
                        send_sem=w_send.at[2 * k + i],
                        recv_sem=w_recv.at[2 * k + i],
                        device_id=dev(y, z, to),
                        device_id_type=MESH,
                    )
                )

        quarter(y, run)

    def y_weights(k, n, q, to, act):
        r = ((x + 4 - k) & 3) * 2 + c

        def run(u_n, v_n):
            for i, ref in enumerate(
                [u_piece(u_full, r * U_ROWS, q, u_n), v_piece(v_full, r * V_ROWS, q, v_n)]
            ):
                sem = (k * 4 + n) * 2 + i
                act(
                    pltpu.make_async_remote_copy(
                        src_ref=ref,
                        dst_ref=ref,
                        send_sem=wy_send.at[sem],
                        recv_sem=wy_recv.at[sem],
                        device_id=dev(to, z, rep),
                        device_id_type=MESH,
                    )
                )

        quarter(q, run)

    for k in (2, 1, 3):
        x_weights(k, rep, ((x + k) & 3) * 2 + c, lambda copy: copy.start())
    w_copies = weight_copies(u_ref, v_ref, rep, w_send, w_recv, 0, y, z, sibling)
    for copy in w_copies:
        copy.start()
    own_u = pltpu.make_async_copy(u_ref, u_at(rep), own_sem.at[1])
    own_v = pltpu.make_async_copy(v_ref, v_at(rep), own_sem.at[2])
    own_u.start()
    own_v.start()

    lines16 = lax.broadcasted_iota(i32, (16, B), 0)

    def ask_copy(place):
        m = member_of(*place)
        return pltpu.make_async_remote_copy(
            src_ref=ask.at[m],
            dst_ref=asked.at[me],
            send_sem=ask_send.at[m],
            recv_sem=ask_recv.at[me],
            device_id=dev(*place),
            device_id_type=MESH,
        )

    def ask_pair(p, carry):
        at_a, at_b = peer(2 * p, y, z, rep), peer(2 * p + 1, y, z, rep)
        a, b = member_of(*at_a), member_of(*at_b)
        pick_a, pick_b = slots_of(pos, a), slots_of(pos, b)
        picks[a] = pick_a
        picks[b] = pick_b
        lhs = jnp.where(lines16 == 0, rows[pl.ds(a, 1), :], 0.0)
        lhs = jnp.where(lines16 == 1, tab[pl.ds(a, 1), :], lhs)
        lhs = jnp.where(lines16 == 2, rows[pl.ds(b, 1), :], lhs)
        lhs = jnp.where(lines16 == 3, tab[pl.ds(b, 1), :], lhs).astype(bf16)
        got = lax.dot_general(
            lhs, jnp.concatenate([pick_a, pick_b], axis=0), NT, preferred_element_type=f32
        )
        code_a = (got[0:1, :SLOTS] + got[1:2, :SLOTS] * float(ROWS)).astype(i32)
        code_b = (got[2:3, SLOTS:] + got[3:4, SLOTS:] * float(ROWS)).astype(i32)
        ask[a] = jnp.broadcast_to(code_a, (8, SLOTS))
        ask[b] = jnp.broadcast_to(code_b, (8, SLOTS))

        @pl.when(p != PAIR_SELF)
        def _():
            ask_copy(at_a).start()

        @pl.when(p == PAIR_SELF)
        def _():
            asked[me] = ask[me]

        ask_copy(at_b).start()
        return carry

    lax.fori_loop(0, GROUP // 2, ask_pair, 0)

    first[:, 0:E] = bottom_ref[...]
    hot_copy.wait()
    ids = ids_ref[...].astype(f32).T
    lanes = lax.broadcasted_iota(i32, (B, E), 1).astype(f32)
    for j in range(NHOT):
        one = jnp.where(lanes == ids[:, j : j + 1], 1.0, 0.0).astype(bf16)
        at = E + WIDE + j * E
        first[:, at : at + E] = jnp.dot(one, hot_ref[j], preferred_element_type=f32).astype(bf16)

    for k in (1, 3, 2):
        came = ((x + 4 - k) & 3) * 2 + c
        x_weights(k, came, came, lambda copy: copy.wait_recv())
        for n in (2, 1, 3):
            y_weights(k, n, y, (y + n) & 3, lambda copy: copy.start())

    def await_part(j, carry):
        sz, srep = source(j)

        @pl.when(is_other((sz, srep)))
        def _():
            pltpu.make_async_remote_copy(
                src_ref=part_ref,
                dst_ref=held.at[srep],
                send_sem=held_send.at[0],
                recv_sem=held_recv.at[srep],
                device_id=dev(y, sz, srep),
                device_id_type=MESH,
            ).wait_recv()

        return carry

    lax.fori_loop(0, 8, await_part, 0)

    @pl.when(self_holder)
    def _():
        own.wait()

    def reply_copy(place):
        m = member_of(*place)
        return pltpu.make_async_remote_copy(
            src_ref=back.at[m],
            dst_ref=replies.at[me],
            send_sem=rep_send.at[m],
            recv_sem=rep_recv.at[me],
            device_id=dev(*place),
            device_id_type=MESH,
        )

    def await_ask(m):
        pltpu.make_async_remote_copy(
            src_ref=ask.at[m],
            dst_ref=asked.at[m],
            send_sem=ask_send.at[m],
            recv_sem=ask_recv.at[m],
            device_id=member_dev(m, z),
            device_id_type=MESH,
        ).wait_recv()

    def reply_pair(p, carry):
        at_a, at_b = peer_back(2 * p, y, z, rep), peer_back(2 * p + 1, y, z, rep)
        a, b = member_of(*at_a), member_of(*at_b)

        @pl.when(p != PAIR_SELF)
        def _():
            await_ask(a)

        await_ask(b)
        code = jnp.concatenate([asked[a][0:1, :], asked[b][0:1, :]], axis=1)
        table = code >> 8
        found = jnp.dot(
            held[...].reshape(WIDE, ROWS), rows_of(code), preferred_element_type=f32
        )
        got = found[0:E]
        for t in range(1, NCOLD):
            got = jnp.where(table == t, found[t * E : (t + 1) * E], got)
        got = got.astype(bf16)
        back[a] = got[:, :SLOTS]
        back[b] = got[:, SLOTS:]

        @pl.when(p != PAIR_SELF)
        def _():
            reply_copy(at_a).start()

        @pl.when(p == PAIR_SELF)
        def _():
            replies[me] = back[me]

        reply_copy(at_b).start()
        return carry

    lax.fori_loop(0, GROUP // 2, reply_pair, 0)

    wc_copies = []
    for k in (1, 3, 2):
        for n in (1, 3, 2):
            came = (y + 4 - n) & 3
            y_weights(k, n, came, came, lambda copy: copy.wait_recv())
        came = ((x + 4 - k) & 3) * 2 + c
        forward = weight_copies(u_at(came), v_at(came), came, wc_send, wc_recv, k, y, z, sibling)
        for copy in forward:
            copy.start()
        wc_copies += forward

    pooled[...] = jnp.zeros((WIDE, B), f32)

    def await_reply(m):
        pltpu.make_async_remote_copy(
            src_ref=back.at[m],
            dst_ref=replies.at[m],
            send_sem=rep_send.at[m],
            recv_sem=rep_recv.at[m],
            device_id=member_dev(m, z),
            device_id_type=MESH,
        ).wait_recv()

    def pool_pair(p, carry):
        at_a, at_b = peer(2 * p, y, z, rep), peer(2 * p + 1, y, z, rep)
        a, b = member_of(*at_a), member_of(*at_b)

        @pl.when(p != PAIR_SELF)
        def _():
            await_reply(a)

        await_reply(b)
        got_a = jnp.dot(replies[a], picks[a], preferred_element_type=f32)
        got_b = jnp.dot(replies[b], picks[b], preferred_element_type=f32)
        tab_a, tab_b = tab[pl.ds(a, 1), :], tab[pl.ds(b, 1), :]
        for t in range(NCOLD):
            more = jnp.where(tab_a == float(t), got_a, 0.0) + jnp.where(
                tab_b == float(t), got_b, 0.0
            )
            pooled[t * E : (t + 1) * E, :] += more
        return carry

    lax.fori_loop(0, 20, pool_pair, 0)

    for k in range(4):
        came = ((x + 4 - k) & 3) * 2 + other_c
        sends, recvs = (w_send, w_recv) if k == 0 else (wc_send, wc_recv)
        for copy in weight_copies(u_at(came), v_at(came), came, sends, recvs, k, y, z, sibling):
            copy.wait_recv()
    own_u.wait()
    own_v.wait()
    hot_at = E + WIDE
    low = jnp.dot(first[:, 0:E], u_full[0:E, :], preferred_element_type=f32)
    low = low + jnp.dot(first[:, hot_at:], u_full[hot_at:, :], preferred_element_type=f32)

    lax.fori_loop(20, 32, pool_pair, 0)
    for t in range(NCOLD):
        first[:, E + t * E : E + (t + 1) * E] = pooled[t * E : (t + 1) * E, :].T.astype(bf16)

    low = low + jnp.dot(first[:, E:hot_at], u_full[E:hot_at, :], preferred_element_type=f32)
    low_half = low.astype(bf16)
    low_t[...] = low.T.astype(bf16)

    def cols(i, width):
        return pl.ds(pl.multiple_of(i * width, width), width)

    def line(ref, i):
        n = COLS // E
        return jnp.concatenate([ref[pl.ds(i * n + q, 1), :] for q in range(n)], axis=1)

    def forward_cols(i, sums):
        at = cols(i, COLS)
        mixing = jnp.dot(low_half, v_full[:, at], preferred_element_type=f32) + line(bias_ref, i)
        wide = first[:, at].astype(f32)
        crossed = (wide * mixing + wide) * line(head_ref, i)
        mixed[:, at] = mixing
        for q in range(COLS // E):
            sums = sums + crossed[:, q * E : (q + 1) * E]
        return sums

    sums = lax.fori_loop(0, CROSS // COLS, forward_cols, jnp.zeros((B, E), f32))
    logit = jnp.sum(sums, axis=1, keepdims=True)
    label = jnp.concatenate([label_ref[0:1, :], label_ref[1:2, :]], axis=1).astype(f32)
    label = jnp.broadcast_to(label, (8, B)).T
    dlogit = jax.nn.sigmoid(logit) - label[:, 0:1]

    dlow[...] = jnp.zeros((B, RANK), f32)
    grads[:, CROSS:] = jnp.zeros((RANK, PADDED - CROSS), bf16)

    def backward_cols(i, carry):
        at = cols(i, COLS)
        dmix = (dlogit * line(head_ref, i) * first[:, at].astype(f32)).astype(bf16)
        dlow[...] += lax.dot_general(dmix, v_full[:, at], NT, preferred_element_type=f32)
        grads[:, at] = jnp.dot(low_t[...], dmix, preferred_element_type=f32).astype(bf16)
        return carry

    lax.fori_loop(0, CROSS // COLS, backward_cols, 0)
    dlow_half = dlow[...].astype(bf16)
    for t in range(NCOLD):
        lo, hi = E + t * E, E + (t + 1) * E
        direct = dlogit * head_ref[t + 1 : t + 2, :] * (mixed[:, lo:hi] + 1.0)
        through = lax.dot_general(u_full[lo:hi, :], dlow_half, NT, preferred_element_type=f32)
        dpool[t * E : (t + 1) * E, :] = (direct.T + through).astype(bf16).astype(f32)

    def v_rows(r):
        return pl.ds(pl.multiple_of(r * V_ROWS, V_ROWS), V_ROWS)

    core_copies = []
    for k in range(4):
        copy = pltpu.make_async_remote_copy(
            src_ref=grads.at[v_rows(2 * k + other_c), :],
            dst_ref=core_in.at[k],
            send_sem=core_send.at[k],
            recv_sem=core_recv.at[k],
            device_id=dev(y, z, sibling),
            device_id_type=MESH,
        )
        copy.start()
        core_copies.append(copy)

    def out_copy(place):
        m = member_of(*place)
        return pltpu.make_async_remote_copy(
            src_ref=out.at[m],
            dst_ref=arrived.at[me],
            send_sem=out_send.at[m],
            recv_sem=out_recv.at[me],
            device_id=dev(*place),
            device_id_type=MESH,
        )

    def pack(m):
        which = tab[pl.ds(m, 1), :]
        chosen = dpool[0:E, :]
        for t in range(1, NCOLD):
            chosen = jnp.where(which == float(t), dpool[t * E : (t + 1) * E, :], chosen)
        out[m] = lax.dot_general(
            chosen.astype(bf16), picks[m], NT, preferred_element_type=f32
        ).astype(bf16)

    def pack_pair(p, carry):
        at_a, at_b = peer(2 * p, y, z, rep), peer(2 * p + 1, y, z, rep)
        a, b = member_of(*at_a), member_of(*at_b)
        pack(a)
        pack(b)

        @pl.when(p != PAIR_SELF)
        def _():
            out_copy(at_a).start()

        @pl.when(p == PAIR_SELF)
        def _():
            arrived[me] = out[me]

        out_copy(at_b).start()
        return carry

    lax.fori_loop(0, 32, pack_pair, 0)

    for k in range(4):
        core_copies[k].wait_recv()
        pair[k] = (grads[v_rows(2 * k + c), :].astype(f32) + core_in[k].astype(f32)).astype(bf16)


    acc[...] = jnp.zeros((WIDE, ROWS), f32)

    def await_out(m):
        pltpu.make_async_remote_copy(
            src_ref=out.at[m],
            dst_ref=arrived.at[m],
            send_sem=out_send.at[m],
            recv_sem=out_recv.at[m],
            device_id=member_dev(m, z),
            device_id_type=MESH,
        ).wait_recv()

    def add_pair(p, carry):
        at_a, at_b = peer_back(2 * p, y, z, rep), peer_back(2 * p + 1, y, z, rep)
        a, b = member_of(*at_a), member_of(*at_b)

        @pl.when(p != PAIR_SELF)
        def _():
            await_out(a)

        await_out(b)
        code = jnp.concatenate([asked[a][0:1, :], asked[b][0:1, :]], axis=1)
        table = code >> 8
        came = jnp.concatenate([arrived[a], arrived[b]], axis=1).astype(f32)
        lhs = jnp.concatenate(
            [jnp.where(table == t, came, 0.0).astype(bf16) for t in range(NCOLD)], axis=0
        )
        acc[...] += lax.dot_general(lhs, rows_of(code), NT, preferred_element_type=f32)
        return carry

    lax.fori_loop(0, V_START, add_pair, 0)

    def piece(j):
        return pl.ds(pl.multiple_of(j * V_PIECE, V_PIECE), V_PIECE)

    y_copies = []
    for k in (2, 1, 3):
        to = (y + k) & 3
        copy = pltpu.make_async_remote_copy(
            src_ref=pair.at[:, :, piece(to)],
            dst_ref=y_in.at[k],
            send_sem=y_send.at[k],
            recv_sem=y_recv.at[k],
            device_id=dev(to, z, rep),
            device_id_type=MESH,
        )
        copy.start()
        y_copies.append(copy)
    lax.fori_loop(V_START, 32, add_pair, 0)


    def sum_copy(j):
        return pltpu.make_async_remote_copy(
            src_ref=part_out.at[j],
            dst_ref=part_in.at[group],
            send_sem=part_send.at[j],
            recv_sem=part_recv.at[group],
            device_id=dev(y, owner_z, j),
            device_id_type=MESH,
        )

    def send_sum(j, carry):
        part_out[j] = acc[pl.ds(pl.multiple_of(j * PART, PART), PART), :].astype(bf16)
        other = jnp.logical_or(owner_z != z, j != rep)

        @pl.when(other)
        def _():
            sum_copy(j).start()

        @pl.when(jnp.logical_not(other))
        def _():
            part_in[group] = part_out[j]

        return carry

    lax.fori_loop(0, 8, send_sum, 0)

    for copy in y_copies:
        copy.wait_recv()
    for k in range(4):
        band[k] = (
            pair[k, :, piece(y)].astype(f32)
            + y_in[1, k].astype(f32)
            + y_in[2, k].astype(f32)
            + y_in[3, k].astype(f32)
        )
    x_copies = []
    for k in (2, 1, 3):
        to = (x + k) & 3
        copy = pltpu.make_async_remote_copy(
            src_ref=band.at[to],
            dst_ref=x_in.at[k],
            send_sem=x_send.at[k],
            recv_sem=x_recv.at[k],
            device_id=dev(y, z, to * 2 + c),
            device_id_type=MESH,
        )
        copy.start()
        x_copies.append(copy)
    for copy in x_copies:
        copy.wait_recv()
    mine[...] = band[x] + x_in[1] + x_in[2] + x_in[3]

    def block(ref, j):
        return ref.at[
            pl.ds(pl.multiple_of((j & 1) * 16, 16), 16), pl.ds(pl.multiple_of((j >> 1) * E, E), E)
        ]

    def z_copy(k):
        to = (z + k) & 15
        return pltpu.make_async_remote_copy(
            src_ref=block(mine, to),
            dst_ref=z_in.at[k],
            send_sem=z_send.at[k],
            recv_sem=z_recv.at[k],
            device_id=dev(y, to, rep),
            device_id_type=MESH,
        )

    def z_start(k, carry):
        @pl.when((z + k) & 15 < VCHUNKS)
        def _():
            z_copy(k).start()

        return carry

    lax.fori_loop(1, 16, z_start, 0)

    def zb_copy(k):
        return pltpu.make_async_remote_copy(
            src_ref=block(strip, z),
            dst_ref=block(strip, z),
            send_sem=zb_send.at[k],
            recv_sem=zb_recv.at[z],
            device_id=dev(y, (z + k) & 15, rep),
            device_id_type=MESH,
        )

    @pl.when(z < VCHUNKS)
    def _():
        def z_wait(k, carry):
            pltpu.make_async_remote_copy(
                src_ref=z_in.at[k],
                dst_ref=z_in.at[k],
                send_sem=z_send.at[k],
                recv_sem=z_recv.at[k],
                device_id=dev(y, (z + 16 - k) & 15, rep),
                device_id_type=MESH,
            ).wait_recv()
            return carry

        lax.fori_loop(1, 16, z_wait, 0)
        got = block(mine, z)[...]
        for k in range(1, 16):
            got = got + z_in[k]
        block(strip, z)[...] = got

        def zb_start(k, carry):
            zb_copy(k).start()
            return carry

        lax.fori_loop(1, 16, zb_start, 0)

    def drain(i):
        m = peer(i, y, z, rep)
        ask_copy(m).wait_send()
        reply_copy(m).wait_send()
        out_copy(m).wait_send()

    others(GROUP, drain)

    def await_sum(j, carry):
        sz, srep = holder(j)

        @pl.when(is_other((sz, srep)))
        def _():
            pltpu.make_async_remote_copy(
                src_ref=part_out.at[0],
                dst_ref=part_in.at[sz >> 1],
                send_sem=part_send.at[0],
                recv_sem=part_recv.at[sz >> 1],
                device_id=dev(y, sz, srep),
                device_id_type=MESH,
            ).wait_recv()

        return carry

    lax.fori_loop(0, 8, await_sum, 0)
    total = part_in[0].astype(f32)
    for g in range(1, 8):
        total = total + part_in[g].astype(f32)
    whole[rep] = total.astype(bf16)

    def all_copy(j):
        return pltpu.make_async_remote_copy(
            src_ref=whole.at[rep],
            dst_ref=whole.at[rep],
            send_sem=all_send.at[j],
            recv_sem=all_recv.at[rep],
            device_id=dev(y, z, (rep + j) & 7),
            device_id_type=MESH,
        )

    def send_all(j, carry):
        all_copy(j).start()
        return carry

    lax.fori_loop(1, 8, send_all, 0)

    def zb_wait(k, carry):
        other = (z + 16 - k) & 15

        @pl.when(other < VCHUNKS)
        def _():
            pltpu.make_async_remote_copy(
                src_ref=block(strip, other),
                dst_ref=block(strip, other),
                send_sem=zb_send.at[k],
                recv_sem=zb_recv.at[other],
                device_id=dev(y, other, rep),
                device_id_type=MESH,
            ).wait_recv()

        return carry

    lax.fori_loop(1, 16, zb_wait, 0)
    summed[:, piece(y)] = strip[...]
    yb_copies = []
    for k in (2, 1, 3):
        copy = pltpu.make_async_remote_copy(
            src_ref=summed.at[:, piece(y)],
            dst_ref=summed.at[:, piece(y)],
            send_sem=yb_send.at[k],
            recv_sem=yb_recv.at[k],
            device_id=dev((y + k) & 3, z, rep),
            device_id_type=MESH,
        )
        copy.start()
        yb_copies.append(copy)

    def await_all(j, carry):
        other = (rep + 8 - j) & 7
        pltpu.make_async_remote_copy(
            src_ref=whole.at[other],
            dst_ref=whole.at[other],
            send_sem=all_send.at[j],
            recv_sem=all_recv.at[other],
            device_id=dev(y, z, other),
            device_id_type=MESH,
        ).wait_recv()
        return carry

    lax.fori_loop(1, 8, await_all, 0)
    grad_ref[...] = whole[...].astype(f32)
    for k in (1, 3, 2):
        came = piece((y + 4 - k) & 3)
        pltpu.make_async_remote_copy(
            src_ref=summed.at[:, came],
            dst_ref=summed.at[:, came],
            send_sem=yb_send.at[k],
            recv_sem=yb_recv.at[k],
            device_id=dev((y + 4 - k) & 3, z, rep),
            device_id_type=MESH,
        ).wait_recv()
    total_ref[...] = summed[:, :CROSS]

    for k in (1, 2, 3):
        x_weights(k, rep, ((x + k) & 3) * 2 + c, lambda copy: copy.wait_send())
        for n in (1, 2, 3):
            y_weights(k, n, y, (y + n) & 3, lambda copy: copy.wait_send())
    for copy in w_copies + wc_copies + core_copies + x_copies + y_copies + yb_copies:
        copy.wait_send()

    def drain_parts(j, carry):
        @pl.when(is_other(holder(j)))
        def _():
            part_copy(j).wait_send()

        @pl.when(jnp.logical_or(owner_z != z, j != rep))
        def _():
            sum_copy(j).wait_send()

        return carry

    lax.fori_loop(0, 8, drain_parts, 0)

    def drain_all(j, carry):
        all_copy(j).wait_send()
        return carry

    lax.fori_loop(1, 8, drain_all, 0)

    def drain_z(k, carry):
        @pl.when((z + k) & 15 < VCHUNKS)
        def _():
            z_copy(k).wait_send()

        @pl.when(z < VCHUNKS)
        def _():
            zb_copy(k).wait_send()

        return carry

    lax.fori_loop(1, 16, drain_z, 0)


def vmem():
    return pl.BlockSpec(memory_space=pltpu.VMEM)


def hbm():
    return pl.BlockSpec(memory_space=pl.ANY)


def dma(n):
    return pltpu.SemaphoreType.DMA((n,))


def step_call(*args):
    return pl.pallas_call(
        step_kernel,
        out_shape=(
            jax.ShapeDtypeStruct((8, PART, ROWS), f32),
            jax.ShapeDtypeStruct((V_ROWS, CROSS), f32),
        ),
        in_specs=[
            vmem(), vmem(), hbm(), vmem(), vmem(), hbm(), hbm(), vmem(), vmem(), vmem(), vmem(),
        ],
        out_specs=(vmem(), vmem()),
        scratch_shapes=[
            pltpu.VMEM((NHOT, E, E), bf16),
            pltpu.VMEM((V_ROWS, CROSS), bf16),
            pltpu.VMEM((8, PART, ROWS), bf16),
            pltpu.VMEM((GROUP, E, SLOTS), bf16),
            pltpu.VMEM((GROUP, E, SLOTS), bf16),
            pltpu.VMEM((GROUP, 8, SLOTS), i32),
            pltpu.VMEM((GROUP, 8, SLOTS), i32),
            pltpu.VMEM((GROUP, B), f32),
            pltpu.VMEM((GROUP, B), f32),
            pltpu.VMEM((GROUP, B), f32),
            pltpu.VMEM((GROUP, SLOTS, B), bf16),
            pltpu.VMEM((WIDE, B), f32),
            pltpu.VMEM((CROSS, RANK), bf16),
            pltpu.VMEM((RANK, CROSS), bf16),
            pltpu.VMEM((B, CROSS), bf16),
            pltpu.VMEM((B, CROSS), f32),
            pltpu.VMEM((RANK, B), bf16),
            pltpu.VMEM((B, RANK), f32),
            pltpu.VMEM((WIDE, B), f32),
            pltpu.VMEM((RANK, PADDED), bf16),
            pltpu.VMEM((GROUP, E, SLOTS), bf16),
            pltpu.VMEM((GROUP, E, SLOTS), bf16),
            pltpu.VMEM((WIDE, ROWS), f32),
            pltpu.VMEM((8, PART, ROWS), bf16),
            pltpu.VMEM((8, PART, ROWS), bf16),
            pltpu.VMEM((8, PART, ROWS), bf16),
            pltpu.VMEM((4, V_ROWS, PADDED), bf16),
            pltpu.VMEM((4, V_ROWS, PADDED), bf16),
            pltpu.VMEM((4, 4, V_ROWS, V_PIECE), bf16),
            pltpu.VMEM((4, V_ROWS, V_PIECE), f32),
            pltpu.VMEM((4, V_ROWS, V_PIECE), f32),
            pltpu.VMEM((V_ROWS, V_PIECE), f32),
            pltpu.VMEM((16, 16, E), f32),
            pltpu.VMEM((V_ROWS, V_PIECE), f32),
            pltpu.VMEM((V_ROWS, PADDED), f32),
            dma(8), dma(8), dma(GROUP), dma(GROUP), dma(GROUP), dma(GROUP), dma(4),
            dma(8), dma(8), dma(32), dma(32), dma(8), dma(8),
            dma(GROUP), dma(GROUP), dma(8), dma(8), dma(8), dma(8),
            dma(4), dma(4), dma(4), dma(4), dma(4), dma(4),
            dma(16), dma(16), dma(16), dma(16), dma(4), dma(4),
        ],
        compiler_params=pltpu.CompilerParams(
            collective_id=0, has_side_effects=True, vmem_limit_bytes=56 << 20
        ),
    )(*args)


def body(
    bottom,
    hot_ids,
    hot_tables,
    cold_owner,
    cold_row,
    cold_rows,
    cold_acc,
    u_weight,
    v_weight,
    v_acc,
    cross_bias,
    head,
    labels,
):
    rep = lax.axis_index("replica")
    turned = cold_rows.reshape(NCOLD, ROWS, E).transpose(0, 2, 1).reshape(8, PART, ROWS)
    part = lax.dynamic_index_in_dim(turned, rep, 0, keepdims=False).astype(bf16)
    grad_rows, grad_mine = step_call(
        cold_owner.T, cold_row.T, part, bottom, hot_ids.T, hot_tables, u_weight, v_weight,
        cross_bias.reshape(CROSS // E, E), head.reshape(CROSS // E, E), labels.reshape(2, E),
    )
    grad_rows = grad_rows.reshape(NCOLD, E, ROWS).transpose(0, 2, 1).reshape(NCOLD * ROWS, E)
    new_cold_acc = cold_acc + jnp.mean(grad_rows * grad_rows, axis=1)
    new_cold_rows = cold_rows - row_rate * grad_rows / (jnp.sqrt(new_cold_acc)[:, None] + eps_value)
    acc_dense = v_acc + jnp.mean(grad_mine * grad_mine, axis=1)
    new_v = v_weight - dense_rate * grad_mine / (jnp.sqrt(acc_dense)[:, None] + eps_value)
    return (new_cold_rows, new_cold_acc, new_v)


def solution(mesh):
    return jax.shard_map(
        body,
        mesh=mesh,
        in_specs=(
            P(("table", "replica"), None),
            P(("table", "replica"), None),
            P(),
            P(("table", "replica"), None),
            P(("table", "replica"), None),
            P("table", None),
            P("table"),
            P("replica", None),
            P("replica", None),
            P("replica"),
            P(),
            P(),
            P(("table", "replica")),
        ),
        out_specs=(P("table", None), P("table"), P("replica", None)),
        check_vma=False,
    )
```

```python
import functools
import jax
import jax.numpy as jnp
from jax import lax
from jax.experimental import pallas as pl
from jax.experimental.pallas import tpu as pltpu
from jax.sharding import PartitionSpec as P

NCOLD = 6
LOOK = 2
NHOT = 20
LOOKUPS = NCOLD * LOOK
E = 128
B = 256
ROWS = 256
SLOTS = 128
GROUP = 64
ITSELF = 8
PAIR_SELF = ITSELF // 2
V_START = 16
WIDE = NCOLD * E
PART = WIDE // 8
CROSS = 3456
PADDED = 3584
COLS = 384
U_ROWS = 432
U_PIECE = 112
V_PIECE = 896
V_ROWS = 32
RANK = 256
VCHUNKS = 14
MESH = pl.DeviceIdType.MESH

row_rate = 0.1
dense_rate = 0.05
eps_value = 1e-08

f32 = jnp.float32
bf16 = jnp.bfloat16
i32 = jnp.int32
NT = (((1,), (1,)), ((), ()))


def place_of():
    table, rep = lax.axis_index("table"), lax.axis_index("replica")
    return table >> 4, table & 15, rep


def dev(y, z, rep):
    return {"table": y * 16 + z, "replica": rep}


def held_z(z, rep):
    return 2 * ((((rep & 1) << 2) + (rep >> 1) - (z >> 1)) & 7) + (z & 1)


def holding_rep(z, owner_z):
    at = ((owner_z >> 1) + (z >> 1)) & 7
    return ((at & 3) << 1) + (at >> 2)


def member_of(y, z, rep):
    return y * 16 + held_z(z, rep)


def member_dev(member, z):
    mz = (z - (z & 1)) + (member & 1)
    return dev(member >> 4, mz, holding_rep(mz, member & 15))


def peer(i, y, z, rep):
    px = ((rep >> 1) + 2 + (i >> 2)) & 3
    pc = (rep + (i >> 1)) & 1
    pz = (z - (z & 1)) + ((z + i) & 1)
    return (y + 2 + (i >> 4) + (i >> 2)) & 3, pz, px * 2 + pc


def peer_back(i, y, z, rep):
    px = ((rep >> 1) + 6 - ((i >> 2) & 3)) & 3
    pc = (rep + (i >> 1)) & 1
    pz = (z - (z & 1)) + ((z + i) & 1)
    return (y + 6 - (((i >> 4) + (i >> 2)) & 3)) & 3, pz, px * 2 + pc


def tables(owner_ref, row_ref, pos, tab, rows):
    owners = lax.broadcasted_iota(i32, (GROUP, B), 0)
    named = jnp.zeros((GROUP, B), f32)
    table = jnp.zeros((GROUP, B), f32)
    row = jnp.zeros((GROUP, B), f32)
    for k in range(LOOKUPS):
        hit = owners == owner_ref[k : k + 1, :]
        named = jnp.where(hit, 1.0, named)
        table = jnp.where(hit, float(k // LOOK), table)
        row = jnp.where(hit, row_ref[k : k + 1, :].astype(f32), row)
    before = jnp.where(
        lax.broadcasted_iota(i32, (B, B), 0) < lax.broadcasted_iota(i32, (B, B), 1), 1.0, 0.0
    ).astype(bf16)
    place = jnp.dot(named.astype(bf16), before, preferred_element_type=f32)
    pos[...] = jnp.where(named > 0.0, place, -1.0)
    tab[...] = table
    rows[...] = row


def slots_of(pos, o):
    lines = lax.broadcasted_iota(i32, (SLOTS, B), 0).astype(f32)
    return jnp.where(lines == pos[pl.ds(o, 1), :], 1.0, 0.0).astype(bf16)


def rows_of(code):
    lines = lax.broadcasted_iota(i32, (ROWS, code.shape[1]), 0)
    return jnp.where(lines == code & (ROWS - 1), 1.0, 0.0).astype(bf16)


def others(count, act):
    def step(i, carry):
        @pl.when(i != ITSELF)
        def _():
            act(i)

        return carry

    lax.fori_loop(0, count, step, 0)


def step_kernel(
    owner_ref, row_ref, part_ref, bottom_ref, ids_ref, hot_hbm, u_ref, v_wide, bias_ref, head_ref, label_ref,
    grad_ref, total_ref,
    hot_ref, v_ref, held, replies, back, ask, asked, pos, tab, rows, picks, pooled,
    u_full, v_full, first, mixed, low_kept, dlow, dpool, grads,
    arrived, out, acc, part_out, part_in, whole,
    core_in, pair, y_in, band, x_in, mine, z_in, strip, summed,
    held_send, held_recv, ask_send, ask_recv, rep_send, rep_recv, own_sem,
    w_send, w_recv, wy_send, wy_recv, wc_send, wc_recv,
    out_send, out_recv, part_send, part_recv, all_send, all_recv,
    core_send, core_recv, x_send, x_recv, y_send, y_recv, z_send, z_recv, zb_send, zb_recv, yb_send, yb_recv,
):
    y, z, rep = place_of()
    x, c = rep >> 1, rep & 1
    other_c = 1 - c
    sibling = x * 2 + other_c
    me = member_of(y, z, rep)
    group = z >> 1
    owner_z = held_z(z, rep)
    self_holder = owner_z == z

    hot_copy = pltpu.make_async_copy(hot_hbm, hot_ref, own_sem.at[3])
    hot_copy.start()

    bar = pltpu.get_barrier_semaphore()

    def signal(y_, z_, rep_):
        pl.semaphore_signal(bar, inc=1, device_id=dev(y_, z_, rep_), device_id_type=MESH)

    def greet_member(i):
        signal(*peer(i, y, z, rep))

    others(GROUP, greet_member)

    def holder(j):
        hz = (z + 2 * j) & 15
        return hz, holding_rep(hz, z)

    def is_other(at):
        return jnp.logical_or(at[0] != z, at[1] != rep)

    def source(j):
        return owner_z, (rep + j) & 7

    def greet_parts(j, carry):
        @pl.when(is_other(holder(j)))
        def _():
            signal(y, *holder(j))

        @pl.when(is_other(source(j)))
        def _():
            signal(y, *source(j))

        return carry

    lax.fori_loop(0, 8, greet_parts, 0)

    def greet_z(k, carry):
        signal(y, (z + k) & 15, rep)
        return carry

    lax.fori_loop(1, 16, greet_z, 0)
    v_ref[...] = v_wide[...].astype(bf16)
    tables(owner_ref, row_ref, pos, tab, rows)
    pl.semaphore_wait(bar, GROUP - 1 + 16 - jnp.where(self_holder, 2, 0).astype(i32) + 15)

    def part_copy(j):
        return pltpu.make_async_remote_copy(
            src_ref=part_ref,
            dst_ref=held.at[rep],
            send_sem=held_send.at[j],
            recv_sem=held_recv.at[rep],
            device_id=dev(y, *holder(j)),
            device_id_type=MESH,
        )

    def send_part(j, carry):
        @pl.when(is_other(holder(j)))
        def _():
            part_copy(j).start()

        return carry

    lax.fori_loop(0, 8, send_part, 0)
    own = pltpu.make_async_copy(part_ref, held.at[rep], own_sem.at[0])

    @pl.when(self_holder)
    def _():
        own.start()

    def u_at(r):
        return u_full.at[pl.ds(pl.multiple_of(r * U_ROWS, 16), U_ROWS), :]

    def v_at(r):
        return v_full.at[pl.ds(pl.multiple_of(r * V_ROWS, 16), V_ROWS), :]

    def weight_copies(src_u, src_v, r, sends, recvs, slot, y_, z_, rep_):
        return [
            pltpu.make_async_remote_copy(
                src_ref=src,
                dst_ref=dst,
                send_sem=sends.at[2 * slot + i],
                recv_sem=recvs.at[2 * slot + i],
                device_id=dev(y_, z_, rep_),
                device_id_type=MESH,
            )
            for i, (src, dst) in enumerate([(src_u, u_at(r)), (src_v, v_at(r))])
        ]

    def quarter(q, act):
        @pl.when(q < 3)
        def _():
            act(U_PIECE, V_PIECE)

        @pl.when(q == 3)
        def _():
            act(U_ROWS - 3 * U_PIECE, CROSS - 3 * V_PIECE)

    def u_piece(ref, base, q, n):
        return ref.at[pl.ds(pl.multiple_of(base + q * U_PIECE, 16), n), :]

    def v_piece(ref, base, q, n):
        at = pl.ds(pl.multiple_of(q * V_PIECE, V_PIECE), n)
        return ref.at[pl.ds(pl.multiple_of(base, 16), V_ROWS), at]

    def x_weights(k, r, to, act):
        def run(u_n, v_n):
            pairs = [
                (u_piece(u_ref, 0, y, u_n), u_piece(u_full, r * U_ROWS, y, u_n)),
                (v_piece(v_ref, 0, y, v_n), v_piece(v_full, r * V_ROWS, y, v_n)),
            ]
            for i, (src, dst) in enumerate(pairs):
                act(
                    pltpu.make_async_remote_copy(
                        src_ref=src,
                        dst_ref=dst,
                        send_sem=w_send.at[2 * k + i],
                        recv_sem=w_recv.at[2 * k + i],
                        device_id=dev(y, z, to),
                        device_id_type=MESH,
                    )
                )

        quarter(y, run)

    def y_weights(k, n, q, to, act):
        r = ((x + 4 - k) & 3) * 2 + c

        def run(u_n, v_n):
            for i, ref in enumerate(
                [u_piece(u_full, r * U_ROWS, q, u_n), v_piece(v_full, r * V_ROWS, q, v_n)]
            ):
                sem = (k * 4 + n) * 2 + i
                act(
                    pltpu.make_async_remote_copy(
                        src_ref=ref,
                        dst_ref=ref,
                        send_sem=wy_send.at[sem],
                        recv_sem=wy_recv.at[sem],
                        device_id=dev(to, z, rep),
                        device_id_type=MESH,
                    )
                )

        quarter(q, run)

    for k in (2, 1, 3):
        x_weights(k, rep, ((x + k) & 3) * 2 + c, lambda copy: copy.start())
    w_copies = weight_copies(u_ref, v_ref, rep, w_send, w_recv, 0, y, z, sibling)
    for copy in w_copies:
        copy.start()
    own_u = pltpu.make_async_copy(u_ref, u_at(rep), own_sem.at[1])
    own_v = pltpu.make_async_copy(v_ref, v_at(rep), own_sem.at[2])
    own_u.start()
    own_v.start()

    lines16 = lax.broadcasted_iota(i32, (16, B), 0)

    def ask_copy(place):
        m = member_of(*place)
        return pltpu.make_async_remote_copy(
            src_ref=ask.at[m],
            dst_ref=asked.at[me],
            send_sem=ask_send.at[m],
            recv_sem=ask_recv.at[me],
            device_id=dev(*place),
            device_id_type=MESH,
        )

    def ask_pair(p, carry):
        at_a, at_b = peer(2 * p, y, z, rep), peer(2 * p + 1, y, z, rep)
        a, b = member_of(*at_a), member_of(*at_b)
        pick_a, pick_b = slots_of(pos, a), slots_of(pos, b)
        picks[a] = pick_a
        picks[b] = pick_b
        lhs = jnp.where(lines16 == 0, rows[pl.ds(a, 1), :], 0.0)
        lhs = jnp.where(lines16 == 1, tab[pl.ds(a, 1), :], lhs)
        lhs = jnp.where(lines16 == 2, rows[pl.ds(b, 1), :], lhs)
        lhs = jnp.where(lines16 == 3, tab[pl.ds(b, 1), :], lhs).astype(bf16)
        got = lax.dot_general(
            lhs, jnp.concatenate([pick_a, pick_b], axis=0), NT, preferred_element_type=f32
        )
        code_a = (got[0:1, :SLOTS] + got[1:2, :SLOTS] * float(ROWS)).astype(i32)
        code_b = (got[2:3, SLOTS:] + got[3:4, SLOTS:] * float(ROWS)).astype(i32)
        ask[a] = jnp.broadcast_to(code_a, (8, SLOTS))
        ask[b] = jnp.broadcast_to(code_b, (8, SLOTS))

        @pl.when(p != PAIR_SELF)
        def _():
            ask_copy(at_a).start()

        @pl.when(p == PAIR_SELF)
        def _():
            asked[me] = ask[me]

        ask_copy(at_b).start()
        return carry

    lax.fori_loop(0, GROUP // 2, ask_pair, 0)

    first[:, 0:E] = bottom_ref[...]
    hot_copy.wait()
    ids = ids_ref[...].astype(f32).T
    lanes = lax.broadcasted_iota(i32, (B, E), 1).astype(f32)
    for j in range(NHOT):
        one = jnp.where(lanes == ids[:, j : j + 1], 1.0, 0.0).astype(bf16)
        at = E + WIDE + j * E
        first[:, at : at + E] = jnp.dot(one, hot_ref[j], preferred_element_type=f32).astype(bf16)

    def await_part(j, carry):
        sz, srep = source(j)

        @pl.when(is_other((sz, srep)))
        def _():
            pltpu.make_async_remote_copy(
                src_ref=part_ref,
                dst_ref=held.at[srep],
                send_sem=held_send.at[0],
                recv_sem=held_recv.at[srep],
                device_id=dev(y, sz, srep),
                device_id_type=MESH,
            ).wait_recv()

        return carry

    lax.fori_loop(0, 8, await_part, 0)

    @pl.when(self_holder)
    def _():
        own.wait()

    for k in (1, 3, 2):
        came = ((x + 4 - k) & 3) * 2 + c
        x_weights(k, came, came, lambda copy: copy.wait_recv())
        for n in (2, 1, 3):
            y_weights(k, n, y, (y + n) & 3, lambda copy: copy.start())

    def reply_copy(place):
        m = member_of(*place)
        return pltpu.make_async_remote_copy(
            src_ref=back.at[m],
            dst_ref=replies.at[me],
            send_sem=rep_send.at[m],
            recv_sem=rep_recv.at[me],
            device_id=dev(*place),
            device_id_type=MESH,
        )

    def await_ask(m):
        pltpu.make_async_remote_copy(
            src_ref=ask.at[m],
            dst_ref=asked.at[m],
            send_sem=ask_send.at[m],
            recv_sem=ask_recv.at[m],
            device_id=member_dev(m, z),
            device_id_type=MESH,
        ).wait_recv()

    def reply_pair(p, carry):
        at_a, at_b = peer_back(2 * p, y, z, rep), peer_back(2 * p + 1, y, z, rep)
        a, b = member_of(*at_a), member_of(*at_b)

        @pl.when(p != PAIR_SELF)
        def _():
            await_ask(a)

        await_ask(b)
        code = jnp.concatenate([asked[a][0:1, :], asked[b][0:1, :]], axis=1)
        table = code >> 8
        found = jnp.dot(
            held[...].reshape(WIDE, ROWS), rows_of(code), preferred_element_type=f32
        )
        got = found[0:E]
        for t in range(1, NCOLD):
            got = jnp.where(table == t, found[t * E : (t + 1) * E], got)
        got = got.astype(bf16)
        back[a] = got[:, :SLOTS]
        back[b] = got[:, SLOTS:]

        @pl.when(p != PAIR_SELF)
        def _():
            reply_copy(at_a).start()

        @pl.when(p == PAIR_SELF)
        def _():
            replies[me] = back[me]

        reply_copy(at_b).start()
        return carry

    lax.fori_loop(0, GROUP // 2, reply_pair, 0)

    pooled[...] = jnp.zeros((WIDE, B), f32)

    def await_reply(m):
        pltpu.make_async_remote_copy(
            src_ref=back.at[m],
            dst_ref=replies.at[m],
            send_sem=rep_send.at[m],
            recv_sem=rep_recv.at[m],
            device_id=member_dev(m, z),
            device_id_type=MESH,
        ).wait_recv()

    def pool_pair(p, carry):
        at_a, at_b = peer(2 * p, y, z, rep), peer(2 * p + 1, y, z, rep)
        a, b = member_of(*at_a), member_of(*at_b)

        @pl.when(p != PAIR_SELF)
        def _():
            await_reply(a)

        await_reply(b)
        got_a = jnp.dot(replies[a], picks[a], preferred_element_type=f32)
        got_b = jnp.dot(replies[b], picks[b], preferred_element_type=f32)
        tab_a, tab_b = tab[pl.ds(a, 1), :], tab[pl.ds(b, 1), :]
        for t in range(NCOLD):
            more = jnp.where(tab_a == float(t), got_a, 0.0) + jnp.where(
                tab_b == float(t), got_b, 0.0
            )
            pooled[t * E : (t + 1) * E, :] += more
        return carry

    lax.fori_loop(0, 14, pool_pair, 0)

    wc_copies = []
    for k in (1, 3, 2):
        for n in (1, 3, 2):
            came = (y + 4 - n) & 3
            y_weights(k, n, came, came, lambda copy: copy.wait_recv())
        came = ((x + 4 - k) & 3) * 2 + c
        forward = weight_copies(u_at(came), v_at(came), came, wc_send, wc_recv, k, y, z, sibling)
        for copy in forward:
            copy.start()
        wc_copies += forward

    lax.fori_loop(14, 24, pool_pair, 0)

    for k in range(4):
        came = ((x + 4 - k) & 3) * 2 + other_c
        sends, recvs = (w_send, w_recv) if k == 0 else (wc_send, wc_recv)
        for copy in weight_copies(u_at(came), v_at(came), came, sends, recvs, k, y, z, sibling):
            copy.wait_recv()
    own_u.wait()
    own_v.wait()
    hot_at = E + WIDE
    low = jnp.dot(first[:, 0:E], u_full[0:E, :], preferred_element_type=f32)
    low = low + jnp.dot(first[:, hot_at:], u_full[hot_at:, :], preferred_element_type=f32)

    lax.fori_loop(24, 32, pool_pair, 0)
    for t in range(NCOLD):
        first[:, E + t * E : E + (t + 1) * E] = pooled[t * E : (t + 1) * E, :].T.astype(bf16)

    low = low + jnp.dot(first[:, E:hot_at], u_full[E:hot_at, :], preferred_element_type=f32)
    low_half = low.astype(bf16)
    low_kept[...] = low_half

    def cols(i, width):
        return pl.ds(pl.multiple_of(i * width, width), width)

    def line(ref, i):
        n = COLS // E
        return jnp.concatenate([ref[pl.ds(i * n + q, 1), :] for q in range(n)], axis=1)

    def forward_cols(i, sums):
        at = cols(i, COLS)
        mixing = jnp.dot(low_half, v_full[:, at], preferred_element_type=f32) + line(bias_ref, i)
        wide = first[:, at].astype(f32)
        crossed = (wide * mixing + wide) * line(head_ref, i)
        mixed[:, at] = mixing
        for q in range(COLS // E):
            sums = sums + crossed[:, q * E : (q + 1) * E]
        return sums

    sums = lax.fori_loop(0, CROSS // COLS, forward_cols, jnp.zeros((B, E), f32))
    logit = jnp.sum(sums, axis=1, keepdims=True)
    label = jnp.concatenate([label_ref[0:1, :], label_ref[1:2, :]], axis=1).astype(f32)
    label = jnp.broadcast_to(label, (8, B)).T
    dlogit = jax.nn.sigmoid(logit) - label[:, 0:1]

    dlow[...] = jnp.zeros((B, RANK), f32)

    def backward_cols(i, carry):
        at = cols(i, COLS)
        dmix = (dlogit * line(head_ref, i) * first[:, at].astype(f32)).astype(bf16)
        dlow[...] += lax.dot_general(dmix, v_full[:, at], NT, preferred_element_type=f32)
        return carry

    lax.fori_loop(0, CROSS // COLS, backward_cols, 0)
    dlow_half = dlow[...].astype(bf16)
    for t in range(NCOLD):
        lo, hi = E + t * E, E + (t + 1) * E
        direct = dlogit * head_ref[t + 1 : t + 2, :] * (mixed[:, lo:hi] + 1.0)
        through = lax.dot_general(u_full[lo:hi, :], dlow_half, NT, preferred_element_type=f32)
        dpool[t * E : (t + 1) * E, :] = (direct.T + through).astype(bf16).astype(f32)

    def out_copy(place):
        m = member_of(*place)
        return pltpu.make_async_remote_copy(
            src_ref=out.at[m],
            dst_ref=arrived.at[me],
            send_sem=out_send.at[m],
            recv_sem=out_recv.at[me],
            device_id=dev(*place),
            device_id_type=MESH,
        )

    def pack(m):
        which = tab[pl.ds(m, 1), :]
        chosen = dpool[0:E, :]
        for t in range(1, NCOLD):
            chosen = jnp.where(which == float(t), dpool[t * E : (t + 1) * E, :], chosen)
        out[m] = lax.dot_general(
            chosen.astype(bf16), picks[m], NT, preferred_element_type=f32
        ).astype(bf16)

    def pack_pair(p, carry):
        at_a, at_b = peer(2 * p, y, z, rep), peer(2 * p + 1, y, z, rep)
        a, b = member_of(*at_a), member_of(*at_b)
        pack(a)
        pack(b)

        @pl.when(p != PAIR_SELF)
        def _():
            out_copy(at_a).start()

        @pl.when(p == PAIR_SELF)
        def _():
            arrived[me] = out[me]

        out_copy(at_b).start()
        return carry

    lax.fori_loop(0, 32, pack_pair, 0)

    grads[:, CROSS:] = jnp.zeros((RANK, PADDED - CROSS), bf16)
    low_t = low_kept[...].astype(f32).T.astype(bf16)

    def grad_cols(i, carry):
        at = cols(i, COLS)
        dmix = (dlogit * line(head_ref, i) * first[:, at].astype(f32)).astype(bf16)
        grads[:, at] = jnp.dot(low_t, dmix, preferred_element_type=f32).astype(bf16)
        return carry

    lax.fori_loop(0, CROSS // COLS, grad_cols, 0)

    def v_rows(r):
        return pl.ds(pl.multiple_of(r * V_ROWS, V_ROWS), V_ROWS)

    core_copies = []
    for k in range(4):
        copy = pltpu.make_async_remote_copy(
            src_ref=grads.at[v_rows(2 * k + other_c), :],
            dst_ref=core_in.at[k],
            send_sem=core_send.at[k],
            recv_sem=core_recv.at[k],
            device_id=dev(y, z, sibling),
            device_id_type=MESH,
        )
        copy.start()
        core_copies.append(copy)

    acc[...] = jnp.zeros((WIDE, ROWS), f32)

    def await_out(m):
        pltpu.make_async_remote_copy(
            src_ref=out.at[m],
            dst_ref=arrived.at[m],
            send_sem=out_send.at[m],
            recv_sem=out_recv.at[m],
            device_id=member_dev(m, z),
            device_id_type=MESH,
        ).wait_recv()

    def add_pair(p, carry):
        at_a, at_b = peer_back(2 * p, y, z, rep), peer_back(2 * p + 1, y, z, rep)
        a, b = member_of(*at_a), member_of(*at_b)

        @pl.when(p != PAIR_SELF)
        def _():
            await_out(a)

        await_out(b)
        code = jnp.concatenate([asked[a][0:1, :], asked[b][0:1, :]], axis=1)
        table = code >> 8
        came = jnp.concatenate([arrived[a], arrived[b]], axis=1).astype(f32)
        lhs = jnp.concatenate(
            [jnp.where(table == t, came, 0.0).astype(bf16) for t in range(NCOLD)], axis=0
        )
        acc[...] += lax.dot_general(lhs, rows_of(code), NT, preferred_element_type=f32)
        return carry

    lax.fori_loop(0, V_START, add_pair, 0)

    for k in range(4):
        core_copies[k].wait_recv()
        pair[k] = (grads[v_rows(2 * k + c), :].astype(f32) + core_in[k].astype(f32)).astype(bf16)


    def piece(j):
        return pl.ds(pl.multiple_of(j * V_PIECE, V_PIECE), V_PIECE)

    y_copies = []
    for k in (2, 1, 3):
        to = (y + k) & 3
        copy = pltpu.make_async_remote_copy(
            src_ref=pair.at[:, :, piece(to)],
            dst_ref=y_in.at[k],
            send_sem=y_send.at[k],
            recv_sem=y_recv.at[k],
            device_id=dev(to, z, rep),
            device_id_type=MESH,
        )
        copy.start()
        y_copies.append(copy)
    lax.fori_loop(V_START, 32, add_pair, 0)


    def sum_copy(j):
        return pltpu.make_async_remote_copy(
            src_ref=part_out.at[j],
            dst_ref=part_in.at[group],
            send_sem=part_send.at[j],
            recv_sem=part_recv.at[group],
            device_id=dev(y, owner_z, j),
            device_id_type=MESH,
        )

    def send_sum(j, carry):
        part_out[j] = acc[pl.ds(pl.multiple_of(j * PART, PART), PART), :].astype(bf16)
        other = jnp.logical_or(owner_z != z, j != rep)

        @pl.when(other)
        def _():
            sum_copy(j).start()

        @pl.when(jnp.logical_not(other))
        def _():
            part_in[group] = part_out[j]

        return carry

    lax.fori_loop(0, 8, send_sum, 0)

    for copy in y_copies:
        copy.wait_recv()
    for k in range(4):
        band[k] = (
            pair[k, :, piece(y)].astype(f32)
            + y_in[1, k].astype(f32)
            + y_in[2, k].astype(f32)
            + y_in[3, k].astype(f32)
        )
    x_copies = []
    for k in (2, 1, 3):
        to = (x + k) & 3
        copy = pltpu.make_async_remote_copy(
            src_ref=band.at[to],
            dst_ref=x_in.at[k],
            send_sem=x_send.at[k],
            recv_sem=x_recv.at[k],
            device_id=dev(y, z, to * 2 + c),
            device_id_type=MESH,
        )
        copy.start()
        x_copies.append(copy)
    for copy in x_copies:
        copy.wait_recv()
    mine[...] = band[x] + x_in[1] + x_in[2] + x_in[3]

    def block(ref, j):
        return ref.at[
            pl.ds(pl.multiple_of((j & 1) * 16, 16), 16), pl.ds(pl.multiple_of((j >> 1) * E, E), E)
        ]

    def z_copy(k):
        to = (z + k) & 15
        return pltpu.make_async_remote_copy(
            src_ref=block(mine, to),
            dst_ref=z_in.at[k],
            send_sem=z_send.at[k],
            recv_sem=z_recv.at[k],
            device_id=dev(y, to, rep),
            device_id_type=MESH,
        )

    def z_start(k, carry):
        @pl.when((z + k) & 15 < VCHUNKS)
        def _():
            z_copy(k).start()

        return carry

    lax.fori_loop(1, 16, z_start, 0)

    def await_sum(j, carry):
        sz, srep = holder(j)

        @pl.when(is_other((sz, srep)))
        def _():
            pltpu.make_async_remote_copy(
                src_ref=part_out.at[0],
                dst_ref=part_in.at[sz >> 1],
                send_sem=part_send.at[0],
                recv_sem=part_recv.at[sz >> 1],
                device_id=dev(y, sz, srep),
                device_id_type=MESH,
            ).wait_recv()

        return carry

    lax.fori_loop(0, 8, await_sum, 0)
    total = part_in[0].astype(f32)
    for g in range(1, 8):
        total = total + part_in[g].astype(f32)
    whole[rep] = total.astype(bf16)

    def all_copy(j):
        return pltpu.make_async_remote_copy(
            src_ref=whole.at[rep],
            dst_ref=whole.at[rep],
            send_sem=all_send.at[j],
            recv_sem=all_recv.at[rep],
            device_id=dev(y, z, (rep + j) & 7),
            device_id_type=MESH,
        )

    def send_all(j, carry):
        all_copy(j).start()
        return carry

    lax.fori_loop(1, 8, send_all, 0)

    def zb_copy(k):
        return pltpu.make_async_remote_copy(
            src_ref=block(strip, z),
            dst_ref=block(strip, z),
            send_sem=zb_send.at[k],
            recv_sem=zb_recv.at[z],
            device_id=dev(y, (z + k) & 15, rep),
            device_id_type=MESH,
        )

    @pl.when(z < VCHUNKS)
    def _():
        def z_wait(k, carry):
            pltpu.make_async_remote_copy(
                src_ref=z_in.at[k],
                dst_ref=z_in.at[k],
                send_sem=z_send.at[k],
                recv_sem=z_recv.at[k],
                device_id=dev(y, (z + 16 - k) & 15, rep),
                device_id_type=MESH,
            ).wait_recv()
            return carry

        lax.fori_loop(1, 16, z_wait, 0)
        got = block(mine, z)[...]
        for k in range(1, 16):
            got = got + z_in[k]
        block(strip, z)[...] = got

        def zb_start(k, carry):
            zb_copy(k).start()
            return carry

        lax.fori_loop(1, 16, zb_start, 0)

    def drain(i):
        m = peer(i, y, z, rep)
        ask_copy(m).wait_send()
        reply_copy(m).wait_send()
        out_copy(m).wait_send()

    others(GROUP, drain)

    def zb_wait(k, carry):
        other = (z + 16 - k) & 15

        @pl.when(other < VCHUNKS)
        def _():
            pltpu.make_async_remote_copy(
                src_ref=block(strip, other),
                dst_ref=block(strip, other),
                send_sem=zb_send.at[k],
                recv_sem=zb_recv.at[other],
                device_id=dev(y, other, rep),
                device_id_type=MESH,
            ).wait_recv()

        return carry

    lax.fori_loop(1, 16, zb_wait, 0)
    summed[:, piece(y)] = strip[...]
    yb_copies = []
    for k in (2, 1, 3):
        copy = pltpu.make_async_remote_copy(
            src_ref=summed.at[:, piece(y)],
            dst_ref=summed.at[:, piece(y)],
            send_sem=yb_send.at[k],
            recv_sem=yb_recv.at[k],
            device_id=dev((y + k) & 3, z, rep),
            device_id_type=MESH,
        )
        copy.start()
        yb_copies.append(copy)

    def await_all(j, carry):
        other = (rep + 8 - j) & 7
        pltpu.make_async_remote_copy(
            src_ref=whole.at[other],
            dst_ref=whole.at[other],
            send_sem=all_send.at[j],
            recv_sem=all_recv.at[other],
            device_id=dev(y, z, other),
            device_id_type=MESH,
        ).wait_recv()
        return carry

    lax.fori_loop(1, 8, await_all, 0)
    grad_ref[...] = whole[...].astype(f32)
    for k in (1, 3, 2):
        came = piece((y + 4 - k) & 3)
        pltpu.make_async_remote_copy(
            src_ref=summed.at[:, came],
            dst_ref=summed.at[:, came],
            send_sem=yb_send.at[k],
            recv_sem=yb_recv.at[k],
            device_id=dev((y + 4 - k) & 3, z, rep),
            device_id_type=MESH,
        ).wait_recv()
    total_ref[...] = summed[:, :CROSS]

    for k in (1, 2, 3):
        x_weights(k, rep, ((x + k) & 3) * 2 + c, lambda copy: copy.wait_send())
        for n in (1, 2, 3):
            y_weights(k, n, y, (y + n) & 3, lambda copy: copy.wait_send())
    for copy in w_copies + wc_copies + core_copies + x_copies + y_copies + yb_copies:
        copy.wait_send()

    def drain_parts(j, carry):
        @pl.when(is_other(holder(j)))
        def _():
            part_copy(j).wait_send()

        @pl.when(jnp.logical_or(owner_z != z, j != rep))
        def _():
            sum_copy(j).wait_send()

        return carry

    lax.fori_loop(0, 8, drain_parts, 0)

    def drain_all(j, carry):
        all_copy(j).wait_send()
        return carry

    lax.fori_loop(1, 8, drain_all, 0)

    def drain_z(k, carry):
        @pl.when((z + k) & 15 < VCHUNKS)
        def _():
            z_copy(k).wait_send()

        @pl.when(z < VCHUNKS)
        def _():
            zb_copy(k).wait_send()

        return carry

    lax.fori_loop(1, 16, drain_z, 0)


def vmem():
    return pl.BlockSpec(memory_space=pltpu.VMEM)


def hbm():
    return pl.BlockSpec(memory_space=pl.ANY)


def dma(n):
    return pltpu.SemaphoreType.DMA((n,))


def step_call(*args):
    return pl.pallas_call(
        step_kernel,
        out_shape=(
            jax.ShapeDtypeStruct((8, PART, ROWS), f32),
            jax.ShapeDtypeStruct((V_ROWS, CROSS), f32),
        ),
        in_specs=[
            vmem(), vmem(), hbm(), vmem(), vmem(), hbm(), hbm(), vmem(), vmem(), vmem(), vmem(),
        ],
        out_specs=(vmem(), vmem()),
        scratch_shapes=[
            pltpu.VMEM((NHOT, E, E), bf16),
            pltpu.VMEM((V_ROWS, CROSS), bf16),
            pltpu.VMEM((8, PART, ROWS), bf16),
            pltpu.VMEM((GROUP, E, SLOTS), bf16),
            pltpu.VMEM((GROUP, E, SLOTS), bf16),
            pltpu.VMEM((GROUP, 8, SLOTS), i32),
            pltpu.VMEM((GROUP, 8, SLOTS), i32),
            pltpu.VMEM((GROUP, B), f32),
            pltpu.VMEM((GROUP, B), f32),
            pltpu.VMEM((GROUP, B), f32),
            pltpu.VMEM((GROUP, SLOTS, B), bf16),
            pltpu.VMEM((WIDE, B), f32),
            pltpu.VMEM((CROSS, RANK), bf16),
            pltpu.VMEM((RANK, CROSS), bf16),
            pltpu.VMEM((B, CROSS), bf16),
            pltpu.VMEM((B, CROSS), f32),
            pltpu.VMEM((B, RANK), bf16),
            pltpu.VMEM((B, RANK), f32),
            pltpu.VMEM((WIDE, B), f32),
            pltpu.VMEM((RANK, PADDED), bf16),
            pltpu.VMEM((GROUP, E, SLOTS), bf16),
            pltpu.VMEM((GROUP, E, SLOTS), bf16),
            pltpu.VMEM((WIDE, ROWS), f32),
            pltpu.VMEM((8, PART, ROWS), bf16),
            pltpu.VMEM((8, PART, ROWS), bf16),
            pltpu.VMEM((8, PART, ROWS), bf16),
            pltpu.VMEM((4, V_ROWS, PADDED), bf16),
            pltpu.VMEM((4, V_ROWS, PADDED), bf16),
            pltpu.VMEM((4, 4, V_ROWS, V_PIECE), bf16),
            pltpu.VMEM((4, V_ROWS, V_PIECE), f32),
            pltpu.VMEM((4, V_ROWS, V_PIECE), f32),
            pltpu.VMEM((V_ROWS, V_PIECE), f32),
            pltpu.VMEM((16, 16, E), f32),
            pltpu.VMEM((V_ROWS, V_PIECE), f32),
            pltpu.VMEM((V_ROWS, PADDED), f32),
            dma(8), dma(8), dma(GROUP), dma(GROUP), dma(GROUP), dma(GROUP), dma(4),
            dma(8), dma(8), dma(32), dma(32), dma(8), dma(8),
            dma(GROUP), dma(GROUP), dma(8), dma(8), dma(8), dma(8),
            dma(4), dma(4), dma(4), dma(4), dma(4), dma(4),
            dma(16), dma(16), dma(16), dma(16), dma(4), dma(4),
        ],
        compiler_params=pltpu.CompilerParams(
            collective_id=0, has_side_effects=True, vmem_limit_bytes=56 << 20
        ),
    )(*args)


def body(
    bottom,
    hot_ids,
    hot_tables,
    cold_owner,
    cold_row,
    cold_rows,
    cold_acc,
    u_weight,
    v_weight,
    v_acc,
    cross_bias,
    head,
    labels,
):
    rep = lax.axis_index("replica")
    turned = cold_rows.reshape(NCOLD, ROWS, E).transpose(0, 2, 1).reshape(8, PART, ROWS)
    part = lax.dynamic_index_in_dim(turned, rep, 0, keepdims=False).astype(bf16)
    grad_rows, grad_mine = step_call(
        cold_owner.T, cold_row.T, part, bottom, hot_ids.T, hot_tables, u_weight, v_weight,
        cross_bias.reshape(CROSS // E, E), head.reshape(CROSS // E, E), labels.reshape(2, E),
    )
    grad_rows = grad_rows.reshape(NCOLD, E, ROWS).transpose(0, 2, 1).reshape(NCOLD * ROWS, E)
    new_cold_acc = cold_acc + jnp.mean(grad_rows * grad_rows, axis=1)
    new_cold_rows = cold_rows - row_rate * grad_rows / (jnp.sqrt(new_cold_acc)[:, None] + eps_value)
    acc_dense = v_acc + jnp.mean(grad_mine * grad_mine, axis=1)
    new_v = v_weight - dense_rate * grad_mine / (jnp.sqrt(acc_dense)[:, None] + eps_value)
    return (new_cold_rows, new_cold_acc, new_v)


def solution(mesh):
    return jax.shard_map(
        body,
        mesh=mesh,
        in_specs=(
            P(("table", "replica"), None),
            P(("table", "replica"), None),
            P(),
            P(("table", "replica"), None),
            P(("table", "replica"), None),
            P("table", None),
            P("table"),
            P("replica", None),
            P("replica", None),
            P("replica"),
            P(),
            P(),
            P(("table", "replica")),
        ),
        out_specs=(P("table", None), P("table"), P("replica", None)),
        check_vma=False,
    )
```
